32 devices in a mesh: groups: 2 (over x), node: 8 (over z, y), local: 2 (over core).
Axes of the slice: x: 2, y: 2, z: 4, core: 2. Of those that a mesh axis runs over, the one named last changes fastest.
Arguments:
- tokens: bfloat16 [4096, 3584], P(('groups', 'node', 'local')), parts along dimension 0, may hold values from -6 to 6
- routes: int32 [4096, 2], P(('groups', 'node', 'local')), parts along dimension 0, may hold values from 0 to 7, all different within a row; in each aligned block of 128 rows (0 to 127, 128 to 255, ...) at most 80 rows name the same one
- route_scale: float32 [4096, 2], P(('groups', 'node', 'local')), parts along dimension 0, may hold values from 0.3 to 1.5
- w_gate: bfloat16 [8, 3584, 1024], P('node', None, 'local'), may hold values from -0.09375 to 0.09375
- w_up: bfloat16 [8, 3584, 1024], P('node', None, 'local'), may hold values from -0.09375 to 0.09375
- w_down: bfloat16 [8, 1024, 3584], P('node', 'local'), may hold values from -0.1875 to 0.1875
Outputs:
- mixed: bfloat16 [4096, 3584], P(('groups', 'node', 'local')), parts along dimension 0
The draws below stay inside these ranges and needn't reach their ends.
There are 2 independent parts, one for each index of `groups`. The reference program is written for one: setup_inputs(seed, part) draws one part's arguments, and reference() takes and returns one part's arrays. A program takes and returns all parts, laid end to end along the dimension named above; an argument that names none is the same for every part. Nothing has to cross between parts.
Inputs may be any that keep to these rules, and one draw needn't show every extreme that they name: `routes`: the 2 experts of a token differ. Within the rows of one device (aligned blocks of 128 tokens) no expert is named by more than 80 tokens, a bound that some block reaches.
All inputs are finite; a program needn't handle non-finite values.
Results may differ from the reference program's by a relative error of at most 0.006.
Values may be sent and summed in bfloat16 or wider, within the bound.
No kernel may reach another device: no remote copies, remote signals or barrier semaphores. Data moves between devices by JAX's collectives and lax.ppermute only.
A program may use at most 128 MiB of HBM per device.

```python
import math
import jax
import jax.numpy as jnp
import numpy as np
from jax import lax

D = 3584
HIDDEN_SIZE = 1024
TOP = 2
TOK_DEV = 128
EXPERTS = 8
CAP = 80
TOKENS = 2048
N_NODE = 8
N_LOCAL = 2


def block_levels(rng, shape, shards, least, largest):
    def one(position, shards_of):
        draws = jax.random.uniform(jax.random.fold_in(jax.random.fold_in(rng, 6), position), (shards_of,), jnp.float32, least / len(shards), largest / len(shards))
        return jnp.repeat(jnp.exp(draws), shape[position] // shards_of).reshape((-1,) + (1,) * (len(shape) - position - 1))

    factor_of = one(*shards[0])
    for cut in shards[1:]:
        factor_of = factor_of * one(*cut)
    return factor_of


def deal_out(own_key, own, number, rows, number_of, top, reach, lean):
    ranking = jax.random.permutation(own_key, number_of)
    packed, ordinary = shares(number_of, rows * top, reach, lean, True), shares(number_of, rows * top, reach, lean, False)
    places = jnp.arange(number_of)

    def named(tallies, turn):
        used = int((tallies > 0).sum())
        fixed = max(1, used // 4)
        shifted = fixed + (places - fixed + turn * (used - fixed)) % max(1, number_of - fixed)
        return jnp.zeros((number_of,), jnp.int32).at[ranking[jnp.where(places < fixed, places, shifted)]].set(jnp.asarray(tallies, jnp.int32))

    tallies = jnp.where(number % 4 == 0, named(packed, number // 4), named(ordinary, number - number // 4 - 1))
    mixed = jax.random.permutation(jax.random.fold_in(own, 3), number_of)
    source_of, receiver = mixed[0:number_of // 2 * 2:2], mixed[1:number_of // 2 * 2:2]
    margin = jnp.minimum(tallies[source_of] - 1, reach - tallies[receiver]) // 2
    margin = jnp.where((source_of == ranking[0]) | (receiver == ranking[0]) | (tallies[receiver] == 0), 0, jnp.maximum(margin, 0))
    shifted = jax.random.randint(jax.random.fold_in(own, 4), (number_of // 2,), 0, 1 << 20) % (margin + 1)
    tallies = tallies.at[source_of].add(-shifted).at[receiver].add(shifted)
    members = jnp.searchsorted(jnp.cumsum(tallies), jnp.arange(rows * top), side="right").astype(jnp.int32)
    listing = members.reshape(top, rows).T
    listing = listing[jax.random.permutation(jax.random.fold_in(own, 1), rows)]
    turn = jax.random.randint(jax.random.fold_in(own, 2), (rows, 1), 0, top)
    return jnp.take_along_axis(listing, (jnp.arange(top)[None, :] + turn) % top, axis=1)


def shares(number_of, total, limit, slope, full):
    portions = [(1 << 20) // math.isqrt(rank ** slope) + 1 for rank in range(1, number_of + 1)]
    largest = limit if full else min(limit, max(-(-total // number_of), total * portions[0] // sum(portions)))
    least = 1 if total - largest >= number_of - 1 else 0
    holding, surplus = [largest] + [least] * (number_of - 1), total - largest - least * (number_of - 1)
    while surplus > 0:
        free = [i for i in range(1, number_of) if holding[i] < largest] or [i for i in range(1, number_of) if holding[i] < limit]
        mass, budget = sum([portions[i] for i in free]), surplus
        for i in free:
            more = min(limit - holding[i], max(1, budget * portions[i] // mass), surplus)
            holding[i] = holding[i] + more
            surplus = surplus - more
    return np.array(holding)


def noise(rng, extent, deviation, reach, split=(), kind=jnp.bfloat16):
    result = deviation * jax.random.normal(rng, extent, jnp.float32)
    if split:
        result = result * block_levels(rng, extent, split, -0.22, 0.18)
    return jnp.clip(result, -reach, reach).astype(kind)


def setup_inputs(seed: int = 0, part: int = 0) -> dict:
    arg_keys = jax.random.split(jax.random.key(seed), 7)
    own_keys = jax.random.split(jax.random.fold_in(arg_keys[6], part), 7)
    tokens = noise(own_keys[0], (TOKENS, D), 1.0, 6.0, ((0, 16),))
    routes_keys = jax.random.split(jax.random.fold_in(own_keys[1], 1), TOKENS // TOK_DEV)
    routes_turns = jax.random.permutation(jax.random.fold_in(own_keys[1], 3), TOKENS // TOK_DEV)
    routes = jax.vmap(lambda own, number: deal_out(jax.random.fold_in(own_keys[1], 2), own, number, TOK_DEV, EXPERTS, TOP, CAP, 1))(routes_keys, routes_turns).reshape((TOKENS, TOP))
    route_scale = jnp.clip(jnp.exp(math.log(1.5) - 1.60943787 * jax.random.uniform(own_keys[2], (TOKENS, TOP), jnp.float32) ** block_levels(own_keys[2], (TOKENS, TOP), ((0, 16),), -0.2, 0.2)), 0.3, 1.5)
    w_gate = noise(arg_keys[3], (EXPERTS, D, HIDDEN_SIZE), D ** -0.5, 0.09375, ((0, 8), (2, 2)))
    w_up = noise(arg_keys[4], (EXPERTS, D, HIDDEN_SIZE), D ** -0.5, 0.09375, ((0, 8), (2, 2)))
    w_down = noise(arg_keys[5], (EXPERTS, HIDDEN_SIZE, D), HIDDEN_SIZE ** -0.5, 0.1875, ((0, 8), (1, 2)))
    return dict(tokens=tokens, routes=routes, route_scale=route_scale, w_gate=w_gate, w_up=w_up, w_down=w_down)


def reference(tokens, routes, route_scale, w_gate, w_up, w_down):
    pairs = routes.reshape(-1).astype(jnp.int32)
    total = pairs.shape[0]
    width = tokens.shape[1]
    experts = w_gate.shape[0]
    slots = N_NODE * N_LOCAL * CAP
    onehot = (pairs[:, None] == jnp.arange(experts, dtype=jnp.int32)[None, :]).astype(jnp.int32)
    rank = jnp.sum((jnp.cumsum(onehot, axis=0) - onehot) * onehot, axis=1).astype(jnp.int32)
    dest = (pairs * slots + rank).astype(jnp.int32)
    source = jnp.full((experts * slots,), total, jnp.int32).at[dest].set(jnp.arange(total, dtype=jnp.int32))
    padded = jnp.concatenate([tokens, jnp.zeros((1, width), tokens.dtype)], axis=0)
    rows = padded[source // 2].reshape(experts, slots, width)

    def expert(operands):
        block, gate_w, up_w, down_w = operands
        gate = jnp.dot(block, gate_w, preferred_element_type=jnp.float32)
        up = jnp.dot(block, up_w, preferred_element_type=jnp.float32)
        hidden = (jax.nn.silu(gate) * up).astype(jnp.bfloat16)
        return jnp.dot(hidden, down_w, preferred_element_type=jnp.float32).astype(jnp.bfloat16)

    outputs = lax.map(expert, (rows, w_gate, w_up, w_down)).reshape(experts * slots, width)
    picked = outputs[dest].astype(jnp.float32).reshape(-1, 2, width)
    mixed = jnp.sum(picked * route_scale[:, :, None].astype(jnp.float32), axis=1)
    return mixed.astype(jnp.bfloat16)
```

```python
import jax
import jax.numpy as jnp
from jax import lax
from jax.sharding import PartitionSpec as P


def on_device(tokens, routes, route_scale, w_gate, w_up, w_down):
    count, width = tokens.shape
    experts = lax.axis_size("node")
    me = lax.axis_index("node")
    swap = [(0, 1), (1, 0)]
    own = (w_gate[0], w_up[0], w_down[0])
    other = tuple(lax.ppermute(w, "local", swap) for w in own)
    every = lax.all_gather(tokens, "node", axis=0, tiled=True)
    mine = jnp.arange(experts, dtype=jnp.int32)
    weight = jnp.sum(
        jnp.where(routes[None, :, :] == mine[:, None, None], route_scale[None, :, :], 0.0), axis=2
    )
    weight = lax.all_gather(weight, "node", axis=0, tiled=False)
    weight = lax.dynamic_index_in_dim(weight, me, axis=1, keepdims=False).reshape(-1)
    scaled = []
    for rows, factor in zip(jnp.split(every, experts // 8), jnp.split(weight, experts // 8)):
        total = 0.0
        for gate_w, up_w, down_w in (own, other):
            gate = jnp.dot(rows, gate_w, preferred_element_type=jnp.float32)
            up = jnp.dot(rows, up_w, preferred_element_type=jnp.float32)
            hidden = (jax.nn.silu(gate) * up).astype(jnp.bfloat16)
            total = total + jnp.dot(hidden, down_w, preferred_element_type=jnp.float32)
        scaled.append((total * factor[:, None]).astype(jnp.bfloat16))
    scaled = jnp.concatenate(scaled, axis=0)
    return lax.psum_scatter(scaled, "node", scatter_dimension=0, tiled=True)


def solution(mesh):
    placed = (
        P(("groups", "node", "local"), None),
        P(("groups", "node", "local"), None),
        P(("groups", "node", "local"), None),
        P("node", None, "local"),
        P("node", None, "local"),
        P("node", "local", None),
    )
    return jax.shard_map(
        on_device,
        mesh=mesh,
        in_specs=placed,
        out_specs=P(("groups", "node", "local"), None),
        check_vma=False,
    )
```

```python
import jax
import jax.numpy as jnp
import numpy as np
from jax import lax
from jax.sharding import PartitionSpec as P


def arrivals(places):
    plan = []
    for place in range(places):
        spare, row = [], []
        for step in range(1, places):
            here = [way for way in (1, -1) if 0 <= place - way * step < places]
            if len(here) == 2 and place % 2 == 0:
                here.reverse()
            spare += [(way, step) for way in here[1:]]
            row.append((here[0], step) if here else spare.pop(0))
        plan.append(row)
    return plan


def parts_of(value):
    high = lax.reduce_precision(value, 8, 7)
    rest = value - high
    middle = lax.reduce_precision(rest, 8, 7)
    return [part.astype(jnp.bfloat16) for part in (high, middle, rest - middle)]


def on_device(tokens, routes, route_scale, w_gate, w_up, w_down):
    count, width = tokens.shape
    experts = lax.axis_size("node")
    places = experts // 2
    node = lax.axis_index("node")
    place, side = node // 2, node % 2
    cap = -(-(5 * count // experts) // 16) * 16

    swap = [(0, 1), (1, 0)]
    own = (w_gate[0], w_up[0], w_down[0])
    halves = (own, tuple(lax.ppermute(w, "local", swap) for w in own))

    def along(block, pairs):
        moves = [(2 * a + y, 2 * b + y) for a, b in pairs for y in range(2)]
        return lax.ppermute(block, "node", moves)

    def across(block):
        return lax.ppermute(block, "node", [(n, n ^ 1) for n in range(experts)])

    weight = jnp.sum(
        jnp.where(routes[:, :, None] == jnp.arange(experts, dtype=jnp.int32), route_scale[:, :, None], 0.0),
        axis=1,
    )
    marks = parts_of(weight)
    room = -(3 * experts) % 128
    block = jnp.concatenate([tokens, *marks, jnp.zeros((count, room), jnp.bfloat16)], axis=1)

    earlier = jnp.asarray(np.tri(count, k=-1), jnp.bfloat16)

    def picker(high):
        named = high != 0
        rank = jnp.dot(earlier, named.astype(jnp.bfloat16), preferred_element_type=jnp.float32)
        slot = jnp.arange(cap, dtype=jnp.float32)[:, None]
        return ((rank[None, :] == slot) & named[None, :]).astype(jnp.bfloat16)

    def column(rows, expert):
        return lax.dynamic_index_in_dim(rows, width + expert, axis=1, keepdims=False)

    def choose(candidates):
        picks, rows = [], []
        for expert in (node, node ^ 1):
            pick, row = 0, 0.0
            for cand, counts in candidates:
                one = picker(jnp.where(counts, column(cand, expert), 0))
                pick = pick + one
                row = row + jnp.dot(one, cand, preferred_element_type=jnp.float32)
            picks.append(pick)
            rows.append(row.astype(jnp.bfloat16))
        return jnp.concatenate(picks, axis=0), rows

    def expert_of(rows):
        data = rows[:, :width]
        scale = sum(
            lax.dynamic_index_in_dim(rows, width + k * experts + node, axis=1).astype(jnp.float32)
            for k in range(3)
        )
        total = 0.0
        for gate_w, up_w, down_w in halves:
            gate = jnp.dot(data, gate_w, preferred_element_type=jnp.float32)
            up = jnp.dot(data, up_w, preferred_element_type=jnp.float32)
            hidden = (jax.nn.silu(gate) * up).astype(jnp.bfloat16)
            total = total + jnp.dot(hidden, down_w, preferred_element_type=jnp.float32)
        return (total * scale).astype(jnp.bfloat16)

    def work(candidates):
        picks, (mine, theirs) = choose(candidates)
        rows = jnp.concatenate([mine, across(theirs)], axis=0)
        out = expert_of(rows)
        back = jnp.concatenate([out[:cap], across(out[cap:])], axis=0)
        return lax.dot_general(
            picks, back, (((0,), (0,)), ((), ())), preferred_element_type=jnp.float32
        ).astype(jnp.bfloat16)

    plan = arrivals(places)
    held = {}
    for step in range(1, places):
        for way in (1, -1):
            pairs = [
                (a, a + way)
                for a in range(places)
                if 0 <= a + way < places and 0 <= a - way * (step - 1) < places
            ]
            held[way, step] = along(held.get((way, step - 1), block), pairs)

    total = work([(block, True)]).astype(jnp.float32)
    for slot in range(places - 1):
        candidates = []
        for key in sorted({row[slot] for row in plan}):
            mine = np.array([row[slot] == key for row in plan])
            candidates.append((held[key], jnp.asarray(mine)[place]))
        done = work(candidates)
        home = [(a, a - row[slot][0] * row[slot][1]) for a, row in enumerate(plan)]
        while home:
            now = list({b: (a, b) for a, b in home}.values())
            home = [pair for pair in home if pair not in now]
            total = total + along(done, now).astype(jnp.float32)
    return total.astype(jnp.bfloat16)


def solution(mesh):
    placed = (
        P(("groups", "node", "local"), None),
        P(("groups", "node", "local"), None),
        P(("groups", "node", "local"), None),
        P("node", None, "local"),
        P("node", None, "local"),
        P("node", "local", None),
    )
    return jax.shard_map(
        on_device,
        mesh=mesh,
        in_specs=placed,
        out_specs=P(("groups", "node", "local"), None),
        check_vma=False,
    )
```

```python
import functools

import jax
import jax.numpy as jnp
from jax import lax
from jax.experimental import pallas as pl
from jax.experimental.pallas import tpu as pltpu
from jax.sharding import PartitionSpec as P

ANYWHERE = pl.BlockSpec(memory_space=pl.ANY)
IN_VMEM = pl.BlockSpec(memory_space=pltpu.VMEM)
MIB = 1024 * 1024


def arrivals(places):
    plan = []
    for place in range(places):
        left = [(-1, step) for step in range(1, places - place)]
        right = [(1, step) for step in range(1, place + 1)]
        plan.append(left + right if place < places // 2 else right + left)
    return plan


def call(kernel, outs, ins, after=(), scratch=(), specs=None, vmem=24):
    body = kernel
    if after:
        first, last = len(ins), len(ins) + len(after)

        def body(*refs):
            kernel(*refs[:first], *refs[last:])

    specs = list(specs or [IN_VMEM] * len(ins)) + [ANYWHERE] * len(after)
    return pl.pallas_call(
        body,
        out_shape=outs,
        in_specs=specs,
        out_specs=[IN_VMEM] * len(outs),
        scratch_shapes=scratch,
        compiler_params=pltpu.CompilerParams(vmem_limit_bytes=vmem * MIB),
        cost_estimate=pl.CostEstimate(flops=0, bytes_accessed=0, transcendentals=0),
    )(*ins, *after)


def mark_kernel(experts, tokens, routes, scale, block):
    count, width = tokens.shape
    lane = lax.broadcasted_iota(jnp.int32, (count, block.shape[1] - width), 1)
    expert, part = lax.rem(lane, experts), lax.div(lane, experts)
    weight = jnp.zeros(lane.shape, jnp.float32)
    for r in range(routes.shape[1]):
        weight += jnp.where(routes[:, r : r + 1] == expert, scale[:, r : r + 1], 0.0)
    high = weight.astype(jnp.bfloat16).astype(jnp.float32)
    middle = (weight - high).astype(jnp.bfloat16).astype(jnp.float32)
    low = weight - high - middle
    marks = jnp.where(part == 0, high, jnp.where(part == 1, middle, jnp.where(part == 2, low, 0.0)))
    block[:, :width] = tokens[...]
    block[:, width:] = marks.astype(jnp.bfloat16)


def pick_kernel(users, *refs):
    blocks, (own_map, other_map, own_rows, other_rows, held, sem) = refs[: len(users)], refs[len(users) :]
    node = lax.axis_index("node")
    for block, places in zip(blocks, users):
        here = functools.reduce(jnp.logical_or, [lax.div(node, 2) == place for place in places])

        @pl.when(here)
        def _():
            copy = pltpu.make_async_copy(block, held, sem)
            copy.start()
            copy.wait()

    count, cap = own_map.shape
    marks = held[:, held.shape[1] - 128 :].astype(jnp.float32)
    lane = lax.broadcasted_iota(jnp.int32, marks.shape, 1)
    earlier = lax.broadcasted_iota(jnp.int32, (count, count), 0) > lax.broadcasted_iota(jnp.int32, (count, count), 1)
    named = jnp.where(marks != 0, 1.0, 0.0)
    rank = jnp.dot(
        jnp.where(earlier, 1.0, 0.0).astype(jnp.bfloat16), named.astype(jnp.bfloat16), preferred_element_type=jnp.float32
    )
    place = jnp.where(named > 0, rank, -1.0)
    slot = lax.broadcasted_iota(jnp.int32, (count, cap), 1)
    for expert, one_hot, rows in ((node, own_map, own_rows), (node ^ 1, other_map, other_rows)):
        mine = jnp.sum(jnp.where(lane == expert, place, 0.0), axis=1, keepdims=True).astype(jnp.int32)
        chosen = jnp.where(mine == slot, 1.0, 0.0).astype(jnp.bfloat16)
        one_hot[...] = chosen
        rows[...] = lax.dot_general(
            chosen, held[...], (((0,), (0,)), ((), ())), preferred_element_type=jnp.float32
        ).astype(jnp.bfloat16)


def expert_kernel(experts, own, other, *refs):
    weights, (own_out, other_out, rows, total, gates, ups, downs, sems) = refs[:6], refs[6:]
    cap, width = own_out.shape
    tiles, _, size = gates.shape
    copies = []
    for tile in range(tiles):
        gate, up, down = weights[:3] if tile < tiles // 2 else weights[3:]
        part = pl.ds(tile % (tiles // 2) * size, size)
        copies.append(
            [
                pltpu.make_async_copy(gate.at[:, part], gates.at[tile], sems.at[tile, 0]),
                pltpu.make_async_copy(up.at[:, part], ups.at[tile], sems.at[tile, 1]),
                pltpu.make_async_copy(down.at[part, :], downs.at[tile], sems.at[tile, 2]),
            ]
        )
        for copy in copies[-1]:
            copy.start()
    rows[:cap] = own[:, :width]
    rows[cap:] = other[:, :width]
    node = lax.axis_index("node")
    for tile in range(tiles):
        copies[tile][0].wait()
        gate = jnp.dot(rows[...], gates[tile], preferred_element_type=jnp.float32)
        copies[tile][1].wait()
        up = jnp.dot(rows[...], ups[tile], preferred_element_type=jnp.float32)
        hidden = (gate / (1.0 + jnp.exp(-gate)) * up).astype(jnp.bfloat16)
        copies[tile][2].wait()
        out = jnp.dot(hidden, downs[tile], preferred_element_type=jnp.float32)
        if tile == 0:
            total[...] = out
        elif tile < tiles - 1:
            total[...] += out
        else:
            out += total[...]
            for first, marks, result in ((0, own, own_out), (cap, other, other_out)):
                marks = marks[:, width:].astype(jnp.float32)
                lane = lax.broadcasted_iota(jnp.int32, marks.shape, 1)
                mine = (lax.rem(lane, experts) == node) & (lane < 3 * experts)
                scale = jnp.sum(jnp.where(mine, marks, 0.0), axis=1, keepdims=True)
                result[...] = (out[first : first + cap] * scale).astype(jnp.bfloat16)


def spread_kernel(own_map, other_map, own_out, other_out, *refs):
    result = refs[-1]
    total = jnp.dot(own_map[...], own_out[...], preferred_element_type=jnp.float32)
    total += jnp.dot(other_map[...], other_out[...], preferred_element_type=jnp.float32)
    for extra in refs[:-1]:
        total += extra[...].astype(jnp.float32)
    result[...] = total.astype(jnp.bfloat16)


def on_device(tokens, routes, route_scale, w_gate, w_up, w_down):
    count, width = tokens.shape
    experts = lax.axis_size("node")
    places = experts // 2
    hidden = w_gate.shape[2]
    size = min(hidden, 256)
    cap = -(-(5 * count // experts) // 16) * 16
    wide = width + -(-3 * experts // 128) * 128
    bf16 = functools.partial(jax.ShapeDtypeStruct, dtype=jnp.bfloat16)

    own = (w_gate[0], w_up[0], w_down[0])
    weights = own + tuple(lax.ppermute(w, "local", [(0, 1), (1, 0)]) for w in own)

    def along(block, pairs):
        moves = [(2 * a + y, 2 * b + y) for a, b in pairs for y in range(2)]
        return lax.ppermute(block, "node", moves)

    def across(block):
        return lax.ppermute(block, "node", [(n, n ^ 1) for n in range(experts)])

    def pick(blocks, users, after=()):
        return call(
            functools.partial(pick_kernel, users),
            [bf16((count, cap)), bf16((count, cap)), bf16((cap, wide)), bf16((cap, wide))],
            blocks,
            after,
            [pltpu.VMEM((count, wide), jnp.bfloat16), pltpu.SemaphoreType.DMA],
            [ANYWHERE] * len(blocks),
        )

    def expert(own_rows, other_rows, after=()):
        tiles = 2 * hidden // size
        return call(
            functools.partial(expert_kernel, experts),
            [bf16((cap, width)), bf16((cap, width))],
            [own_rows, other_rows, *weights],
            after,
            [
                pltpu.VMEM((2 * cap, width), jnp.bfloat16),
                pltpu.VMEM((2 * cap, width), jnp.float32),
                pltpu.VMEM((tiles, width, size), jnp.bfloat16),
                pltpu.VMEM((tiles, width, size), jnp.bfloat16),
                pltpu.VMEM((tiles, size, width), jnp.bfloat16),
                pltpu.SemaphoreType.DMA((tiles, 3)),
            ],
            [IN_VMEM] * 2 + [ANYWHERE] * 6,
            56,
        )

    def spread(maps, own_out, other_out, extras=(), after=()):
        return call(spread_kernel, [bf16((count, width))], [*maps, own_out, other_out, *extras], after)[0]

    (block,) = call(
        functools.partial(mark_kernel, experts), [bf16((count, wide))], [tokens, routes, route_scale]
    )
    plan = arrivals(places)
    held = {}
    for step in range(1, places):
        for way in (1, -1):
            pairs = [
                (a, a + way)
                for a in range(places)
                if 0 <= a + way < places and 0 <= a - way * (step - 1) < places
            ]
            held[way, step] = along(held.get((way, step - 1), block), pairs)

    last = []

    def ordered(function, *args):
        out = function(*args, after=tuple(last))
        last[:] = [out[0] if isinstance(out, (list, tuple)) else out]
        return out

    picks, outs, returned = {}, {}, []

    def do_pick(slot):
        if slot == 0:
            blocks, users = [block], [range(places)]
        else:
            keys = sorted({row[slot - 1] for row in plan})
            blocks = [held[key] for key in keys]
            users = [[place for place, row in enumerate(plan) if row[slot - 1] == key] for key in keys]
        *maps, own_rows, other_rows = ordered(pick, blocks, users)
        picks[slot] = maps, own_rows, across(other_rows)

    def do_expert(slot):
        own_out, other_out = ordered(expert, picks[slot][1], picks[slot][2])
        outs[slot] = own_out, across(other_out)

    def do_spread(slot):
        done = ordered(spread, picks[slot][0], *outs[slot])
        home = [(a, a - row[slot - 1][0] * row[slot - 1][1]) for a, row in enumerate(plan)]
        rounds = []
        while home:
            now = list({b: (a, b) for a, b in home}.values())
            home = [pair for pair in home if pair not in now]
            rounds.append(along(done, now))
        returned.append(rounds)

    do_pick(0)
    do_pick(1)
    do_expert(0)
    for slot in range(1, places):
        do_expert(slot)
        if slot + 1 < places:
            do_pick(slot + 1)
            do_spread(slot)
    first = ordered(spread, picks[0][0], *outs[0], returned[0])
    do_spread(places - 1)
    total = first.astype(jnp.float32)
    for block in sum(returned[1:], []):
        total = total + block.astype(jnp.float32)
    return total.astype(jnp.bfloat16)


def solution(mesh):
    placed = (
        P(("groups", "node", "local"), None),
        P(("groups", "node", "local"), None),
        P(("groups", "node", "local"), None),
        P("node", None, "local"),
        P("node", None, "local"),
        P("node", "local", None),
    )
    return jax.shard_map(
        on_device,
        mesh=mesh,
        in_specs=placed,
        out_specs=P(("groups", "node", "local"), None),
        check_vma=False,
    )
```

```python
import functools

import jax
import jax.numpy as jnp
from jax import lax
from jax.experimental import pallas as pl
from jax.experimental.pallas import tpu as pltpu
from jax.sharding import PartitionSpec as P

ANYWHERE = pl.BlockSpec(memory_space=pl.ANY)
IN_HBM = pl.BlockSpec(memory_space=pltpu.HBM)
IN_VMEM = pl.BlockSpec(memory_space=pltpu.VMEM)
MIB = 1024 * 1024


def arrivals(places):
    plan = []
    for place in range(places):
        left = [(-1, step) for step in range(1, places - place)]
        right = [(1, step) for step in range(1, place + 1)]
        plan.append(left + right if place < places // 2 else right + left)
    return plan


def call(kernel, outs, ins, after=(), scratch=(), specs=None, vmem=24):
    body = kernel
    if after:
        first, last = len(ins), len(ins) + len(after)

        def body(*refs):
            kernel(*refs[:first], *refs[last:])

    specs = list(specs or [IN_VMEM] * len(ins)) + [ANYWHERE] * len(after)
    return pl.pallas_call(
        body,
        out_shape=outs,
        in_specs=specs,
        out_specs=[IN_VMEM] * len(outs),
        scratch_shapes=scratch,
        compiler_params=pltpu.CompilerParams(vmem_limit_bytes=vmem * MIB),
        cost_estimate=pl.CostEstimate(flops=0, bytes_accessed=0, transcendentals=0),
    )(*ins, *after)


def tied(arrays, after):
    return pl.pallas_call(
        lambda *refs: None,
        out_shape=[jax.ShapeDtypeStruct(a.shape, a.dtype) for a in arrays],
        in_specs=[ANYWHERE] * (len(arrays) + len(after)),
        out_specs=[ANYWHERE] * len(arrays),
        input_output_aliases={k: k for k in range(len(arrays))},
        cost_estimate=pl.CostEstimate(flops=0, bytes_accessed=0, transcendentals=0),
    )(*arrays, *after)


def mark_kernel(experts, tokens, routes, scale, block):
    count, width = tokens.shape
    lane = lax.broadcasted_iota(jnp.int32, (count, block.shape[1] - width), 1)
    expert, part = lax.rem(lane, experts), lax.div(lane, experts)
    weight = jnp.zeros(lane.shape, jnp.float32)
    routes, scale = routes[...].T, scale[...].T
    for r in range(routes.shape[1]):
        weight += jnp.where(routes[:, r : r + 1] == expert, scale[:, r : r + 1], 0.0)
    high = weight.astype(jnp.bfloat16).astype(jnp.float32)
    middle = (weight - high).astype(jnp.bfloat16).astype(jnp.float32)
    low = weight - high - middle
    marks = jnp.where(part == 0, high, jnp.where(part == 1, middle, jnp.where(part == 2, low, 0.0)))
    block[:, :width] = tokens[...]
    block[:, width:] = marks.astype(jnp.bfloat16)


def pick_kernel(users, *refs):
    blocks, (own_map, other_map, own_rows, other_rows, held, sem) = refs[: len(users)], refs[len(users) :]
    node = lax.axis_index("node")
    for block, places in zip(blocks, users):
        here = functools.reduce(jnp.logical_or, [lax.div(node, 2) == place for place in places])

        @pl.when(here)
        def _():
            copy = pltpu.make_async_copy(block, held, sem)
            copy.start()
            copy.wait()

    count, cap = own_map.shape
    marks = held[:, held.shape[1] - 128 :].astype(jnp.float32)
    lane = lax.broadcasted_iota(jnp.int32, marks.shape, 1)
    earlier = lax.broadcasted_iota(jnp.int32, (count, count), 0) > lax.broadcasted_iota(jnp.int32, (count, count), 1)
    named = jnp.where(marks != 0, 1.0, 0.0)
    rank = jnp.dot(
        jnp.where(earlier, 1.0, 0.0).astype(jnp.bfloat16), named.astype(jnp.bfloat16), preferred_element_type=jnp.float32
    )
    place = jnp.where(named > 0, rank, -1.0)
    slot = lax.broadcasted_iota(jnp.int32, (count, cap), 1)
    for expert, one_hot, rows in ((node, own_map, own_rows), (node ^ 1, other_map, other_rows)):
        mine = jnp.sum(jnp.where(lane == expert, place, 0.0), axis=1, keepdims=True).astype(jnp.int32)
        chosen = jnp.where(mine == slot, 1.0, 0.0).astype(jnp.bfloat16)
        one_hot[...] = chosen
        rows[...] = lax.dot_general(
            chosen, held[...], (((0,), (0,)), ((), ())), preferred_element_type=jnp.float32
        ).astype(jnp.bfloat16)


def expert_kernel(experts, own, other, gate_w, up_w, down_w, own_out, other_out, *scratch):
    rows, total, gates, ups, downs, sems = scratch
    cap, width = own_out.shape
    tiles, _, size = gates.shape
    each = tiles // gate_w.shape[0]
    copies = []
    for tile in range(tiles):
        half, part = tile // each, pl.ds(tile % each * size, size)
        copies.append(
            [
                pltpu.make_async_copy(gate_w.at[half, :, part], gates.at[tile], sems.at[tile, 0]),
                pltpu.make_async_copy(up_w.at[half, :, part], ups.at[tile], sems.at[tile, 1]),
                pltpu.make_async_copy(down_w.at[half, part, :], downs.at[tile], sems.at[tile, 2]),
            ]
        )
    ahead = [copy for tile in copies for copy in tile]
    for copy in ahead[:4]:
        copy.start()
    waiting = list(ahead[4:])

    def arrived(copy):
        copy.wait()
        if waiting:
            waiting.pop(0).start()

    rows[:cap] = own[:, :width]
    rows[cap:] = other[:, :width]
    node = lax.axis_index("node")
    for tile in range(tiles):
        arrived(copies[tile][0])
        gate = jnp.dot(rows[...], gates[tile], preferred_element_type=jnp.float32)
        arrived(copies[tile][1])
        up = jnp.dot(rows[...], ups[tile], preferred_element_type=jnp.float32)
        hidden = (gate / (1.0 + jnp.exp(-gate)) * up).astype(jnp.bfloat16)
        arrived(copies[tile][2])
        out = jnp.dot(hidden, downs[tile], preferred_element_type=jnp.float32)
        if tile == 0:
            total[...] = out
        elif tile < tiles - 1:
            total[...] += out
        else:
            out += total[...]
            for first, marks, result in ((0, own, own_out), (cap, other, other_out)):
                marks = marks[:, width:].astype(jnp.float32)
                lane = lax.broadcasted_iota(jnp.int32, marks.shape, 1)
                mine = (lax.rem(lane, experts) == node) & (lane < 3 * experts)
                scale = jnp.sum(jnp.where(mine, marks, 0.0), axis=1, keepdims=True)
                result[...] = (out[first : first + cap] * scale).astype(jnp.bfloat16)


def spread_kernel(own_map, other_map, own_out, other_out, *refs):
    result = refs[-1]
    total = jnp.dot(own_map[...], own_out[...], preferred_element_type=jnp.float32)
    total += jnp.dot(other_map[...], other_out[...], preferred_element_type=jnp.float32)
    for extra in refs[:-1]:
        total += extra[...].astype(jnp.float32)
    result[...] = total.astype(jnp.bfloat16)


def on_device(tokens, routes, route_scale, w_gate, w_up, w_down):
    count, width = tokens.shape
    experts = lax.axis_size("node")
    places = experts // 2
    hidden = w_gate.shape[2]
    size = min(hidden, 256)
    cap = -(-(5 * count // experts) // 16) * 16
    wide = width + -(-3 * experts // 128) * 128
    bf16 = functools.partial(jax.ShapeDtypeStruct, dtype=jnp.bfloat16)

    own = (w_gate[0], w_up[0], w_down[0])
    weights = tuple(lax.all_gather(w, "local") for w in own)

    def along(block, pairs):
        moves = [(2 * a + y, 2 * b + y) for a, b in pairs for y in range(2)]
        return lax.ppermute(block, "node", moves)

    def across(block):
        return lax.ppermute(block, "node", [(n, n ^ 1) for n in range(experts)])

    def pick(blocks, users, after=()):
        return call(
            functools.partial(pick_kernel, users),
            [bf16((count, cap)), bf16((count, cap)), bf16((cap, wide)), bf16((cap, wide))],
            blocks,
            after,
            [pltpu.VMEM((count, wide), jnp.bfloat16), pltpu.SemaphoreType.DMA],
            [ANYWHERE] * len(blocks),
        )

    def expert(own_rows, other_rows, after=()):
        tiles = 2 * hidden // size
        return call(
            functools.partial(expert_kernel, experts),
            [bf16((cap, width)), bf16((cap, width))],
            [own_rows, other_rows, *weights],
            after,
            [
                pltpu.VMEM((2 * cap, width), jnp.bfloat16),
                pltpu.VMEM((2 * cap, width), jnp.float32),
                pltpu.VMEM((tiles, width, size), jnp.bfloat16),
                pltpu.VMEM((tiles, width, size), jnp.bfloat16),
                pltpu.VMEM((tiles, size, width), jnp.bfloat16),
                pltpu.SemaphoreType.DMA((tiles, 3)),
            ],
            [IN_VMEM] * 2 + [IN_HBM] * 3,
            36,
        )

    def spread(maps, own_out, other_out, extras=(), after=()):
        return call(spread_kernel, [bf16((count, width))], [*maps, own_out, other_out, *extras], after)[0]

    (block,) = call(
        functools.partial(mark_kernel, experts), [bf16((count, wide))], [tokens, routes.T, route_scale.T]
    )
    plan = arrivals(places)
    held = {}

    last = []

    def ordered(function, *args, after=()):
        out = function(*args, after=(*last, *after))
        last[:] = [out[0] if isinstance(out, (list, tuple)) else out]
        return out

    picks, outs, returned = {}, {}, []

    def relay(step):
        for way in (1, -1):
            pairs = [
                (a, a + way)
                for a in range(places)
                if 0 <= a + way < places and 0 <= a - way * (step - 1) < places
            ]
            held[way, step] = along(held.get((way, step - 1), block), pairs)

    def do_pick(slot, after=()):
        if slot == 0:
            blocks, users = [block], [range(places)]
        else:
            keys = sorted({row[slot - 1] for row in plan})
            blocks = [held[key] for key in keys]
            users = [[place for place, row in enumerate(plan) if row[slot - 1] == key] for key in keys]
        *maps, own_rows, other_rows = ordered(pick, blocks, users, after=after)
        picks[slot] = maps, own_rows, across(other_rows)

    def do_expert(slot, after=()):
        own_out, other_out = ordered(expert, picks[slot][1], picks[slot][2], after=after)
        outs[slot] = own_out, across(other_out)

    def do_spread(slot, after=()):
        done = ordered(spread, picks[slot][0], *outs[slot], after=after)
        home = [(a, a - row[slot - 1][0] * row[slot - 1][1]) for a, row in enumerate(plan)]
        rounds = []
        while home:
            now = list({b: (a, b) for a, b in home}.values())
            home = [pair for pair in home if pair not in now]
            rounds.append(along(done, now))
        returned.append(rounds)

    relay(1)
    do_pick(0)
    held[1, 1], held[-1, 1] = tied([held[1, 1], held[-1, 1]], [picks[0][2]])
    for step in range(2, places):
        relay(step)
    do_pick(1)
    do_expert(0)
    do_expert(1)
    do_pick(2, after=[outs[0][1]])
    total = ordered(spread, picks[0][0], *outs[0])
    do_spread(1)
    for slot in range(2, places):
        do_expert(slot, after=returned[slot - 3] if slot > 2 else ())
        if slot + 1 < places:
            do_pick(slot + 1)
        if slot > 2:
            do_spread(slot - 1)
    do_spread(places - 1)
    total = total.astype(jnp.float32)
    for block in sum(returned, []):
        total = total + block.astype(jnp.float32)
    return total.astype(jnp.bfloat16)


def solution(mesh):
    placed = (
        P(("groups", "node", "local"), None),
        P(("groups", "node", "local"), None),
        P(("groups", "node", "local"), None),
        P("node", None, "local"),
        P("node", None, "local"),
        P("node", "local", None),
    )
    return jax.shard_map(
        on_device,
        mesh=mesh,
        in_specs=placed,
        out_specs=P(("groups", "node", "local"), None),
        check_vma=False,
    )
```

```python
import functools

import jax
import jax.numpy as jnp
from jax import lax
from jax.experimental import pallas as pl
from jax.experimental.pallas import tpu as pltpu
from jax.sharding import PartitionSpec as P

ANYWHERE = pl.BlockSpec(memory_space=pl.ANY)
IN_HBM = pl.BlockSpec(memory_space=pltpu.HBM)
IN_VMEM = pl.BlockSpec(memory_space=pltpu.VMEM)
MIB = 1024 * 1024


def arrivals(places):
    plan = []
    for place in range(places):
        left = [(-1, step) for step in range(1, places - place)]
        right = [(1, step) for step in range(1, place + 1)]
        plan.append(left + right if place < places // 2 else right + left)
    return plan


def call(kernel, outs, ins, after=(), scratch=(), specs=None, vmem=24, out_specs=None):
    body = kernel
    if after:
        first, last = len(ins), len(ins) + len(after)

        def body(*refs):
            kernel(*refs[:first], *refs[last:])

    specs = list(specs or [IN_VMEM] * len(ins)) + [ANYWHERE] * len(after)
    return pl.pallas_call(
        body,
        out_shape=outs,
        in_specs=specs,
        out_specs=out_specs or [IN_VMEM] * len(outs),
        scratch_shapes=scratch,
        compiler_params=pltpu.CompilerParams(vmem_limit_bytes=vmem * MIB),
        cost_estimate=pl.CostEstimate(flops=0, bytes_accessed=0, transcendentals=0),
    )(*ins, *after)


def tied(arrays, after):
    return pl.pallas_call(
        lambda *refs: None,
        out_shape=[jax.ShapeDtypeStruct(a.shape, a.dtype) for a in arrays],
        in_specs=[ANYWHERE] * (len(arrays) + len(after)),
        out_specs=[ANYWHERE] * len(arrays),
        input_output_aliases={k: k for k in range(len(arrays))},
        cost_estimate=pl.CostEstimate(flops=0, bytes_accessed=0, transcendentals=0),
    )(*arrays, *after)


def first_kernel(experts, tokens, routes, scale, gate_w, up_w, block, *refs):
    picked, (stack, sems) = refs[:4], refs[4:]
    copies = [
        pltpu.make_async_copy(gate_w, stack.at[0], sems.at[0]),
        pltpu.make_async_copy(up_w, stack.at[1], sems.at[1]),
    ]
    for copy in copies:
        copy.start()
    count, width = tokens.shape
    lane = lax.broadcasted_iota(jnp.int32, (count, block.shape[1] - width), 1)
    expert, part = lax.rem(lane, experts), lax.div(lane, experts)
    weight = jnp.zeros(lane.shape, jnp.float32)
    routes, scale = routes[...].T, scale[...].T
    for r in range(routes.shape[1]):
        weight += jnp.where(routes[:, r : r + 1] == expert, scale[:, r : r + 1], 0.0)
    high = weight.astype(jnp.bfloat16).astype(jnp.float32)
    middle = (weight - high).astype(jnp.bfloat16).astype(jnp.float32)
    low = weight - high - middle
    marks = jnp.where(part == 0, high, jnp.where(part == 1, middle, jnp.where(part == 2, low, 0.0)))
    block[:, :width] = tokens[...]
    block[:, width:] = marks.astype(jnp.bfloat16)
    choose(block, *picked)
    for copy in copies:
        copy.wait()


def choose(held, own_map, other_map, own_rows, other_rows):
    node = lax.axis_index("node")
    count, cap = own_map.shape
    marks = held[:, held.shape[1] - 128 :].astype(jnp.float32)
    lane = lax.broadcasted_iota(jnp.int32, marks.shape, 1)
    earlier = lax.broadcasted_iota(jnp.int32, (count, count), 0) > lax.broadcasted_iota(jnp.int32, (count, count), 1)
    named = jnp.where(marks != 0, 1.0, 0.0)
    rank = jnp.dot(
        jnp.where(earlier, 1.0, 0.0).astype(jnp.bfloat16), named.astype(jnp.bfloat16), preferred_element_type=jnp.float32
    )
    place = jnp.where(named > 0, rank, -1.0)
    slot = lax.broadcasted_iota(jnp.int32, (count, cap), 1)
    for expert, one_hot, rows in ((node, own_map, own_rows), (node ^ 1, other_map, other_rows)):
        mine = jnp.sum(jnp.where(lane == expert, place, 0.0), axis=1, keepdims=True).astype(jnp.int32)
        chosen = jnp.where(mine == slot, 1.0, 0.0).astype(jnp.bfloat16)
        one_hot[...] = chosen
        rows[...] = lax.dot_general(
            chosen, held[...], (((0,), (0,)), ((), ())), preferred_element_type=jnp.float32
        ).astype(jnp.bfloat16)


def pick_kernel(users, *refs):
    blocks, (held, sem) = refs[: len(users)], refs[len(users) + 4 :]
    node = lax.axis_index("node")
    for block, places in zip(blocks, users):
        here = functools.reduce(jnp.logical_or, [lax.div(node, 2) == place for place in places])

        @pl.when(here)
        def _():
            copy = pltpu.make_async_copy(block, held, sem)
            copy.start()
            copy.wait()

    choose(held, *refs[len(users) : len(users) + 4])


def expert_kernel(experts, own, other, *refs):
    own_w, other_w, own_down, other_down, own_out, other_out, rows, hidden, gates, ups, downs, sems = refs
    cap, width = own_out.shape
    tiles, _, size = gates.shape
    each = tiles // 2
    queue = []
    for tile in range(tiles):
        stack, part = (own_w, other_w)[tile // each], pl.ds(tile % each * size, size)
        queue.append(pltpu.make_async_copy(stack.at[0, :, part], gates.at[tile], sems.at[tile, 0]))
        queue.append(pltpu.make_async_copy(stack.at[1, :, part], ups.at[tile], sems.at[tile, 1]))
    for half, down in enumerate((own_down, other_down)):
        queue.append(pltpu.make_async_copy(down, downs.at[half], sems.at[half, 2]))
    ahead = iter(queue[4:])
    for copy in queue[:4]:
        copy.start()

    def arrived(copy):
        copy.wait()
        for following in ahead:
            following.start()
            break

    rows[:cap] = own[:, :width]
    rows[cap:] = other[:, :width]
    for tile in range(tiles):
        arrived(queue[2 * tile])
        gate = jnp.dot(rows[...], gates[tile], preferred_element_type=jnp.float32)
        arrived(queue[2 * tile + 1])
        up = jnp.dot(rows[...], ups[tile], preferred_element_type=jnp.float32)
        hidden[:, tile * size : (tile + 1) * size] = (gate / (1.0 + jnp.exp(-gate)) * up).astype(jnp.bfloat16)
    arrived(queue[-2])
    arrived(queue[-1])
    node = lax.axis_index("node")
    scales = []
    for marked in (own, other):
        marks = marked[:, width:].astype(jnp.float32)
        lane = lax.broadcasted_iota(jnp.int32, marks.shape, 1)
        mine = (lax.rem(lane, experts) == node) & (lane < 3 * experts)
        scales.append(jnp.sum(jnp.where(mine, marks, 0.0), axis=1, keepdims=True))
    step = 512 if width % 512 == 0 else width
    for start in range(0, width, step):
        cut = slice(start, start + step)
        out = jnp.dot(hidden[:, : each * size], downs[0, :, cut], preferred_element_type=jnp.float32)
        out += jnp.dot(hidden[:, each * size :], downs[1, :, cut], preferred_element_type=jnp.float32)
        own_out[:, cut] = (out[:cap] * scales[0]).astype(jnp.bfloat16)
        other_out[:, cut] = (out[cap:] * scales[1]).astype(jnp.bfloat16)


def spread_kernel(own_map, other_map, own_out, other_out, *refs):
    result = refs[-1]
    total = jnp.dot(own_map[...], own_out[...], preferred_element_type=jnp.float32)
    total += jnp.dot(other_map[...], other_out[...], preferred_element_type=jnp.float32)
    for extra in refs[:-1]:
        total += extra[...].astype(jnp.float32)
    result[...] = total.astype(jnp.bfloat16)


def on_device(tokens, routes, route_scale, w_gate, w_up, w_down):
    count, width = tokens.shape
    experts = lax.axis_size("node")
    places = experts // 2
    hidden = w_gate.shape[2]
    size = min(hidden, 256)
    cap = -(-(5 * count // experts) // 16) * 16
    wide = width + -(-3 * experts // 128) * 128
    in_hbm = functools.partial(pltpu.with_memory_space_constraint, memory_space=pltpu.HBM)
    bf16 = functools.partial(jax.ShapeDtypeStruct, dtype=jnp.bfloat16)

    block, *picked, stack = call(
        functools.partial(first_kernel, experts),
        [
            bf16((count, wide)),
            bf16((count, cap)),
            bf16((count, cap)),
            bf16((cap, wide)),
            bf16((cap, wide)),
            pltpu.HBM((2, width, hidden), jnp.bfloat16),
        ],
        [tokens, routes.T, route_scale.T, in_hbm(w_gate[0]), in_hbm(w_up[0])],
        (),
        [pltpu.SemaphoreType.DMA((2,))],
        [IN_VMEM] * 3 + [ANYWHERE] * 2,
        out_specs=[IN_VMEM] * 5 + [IN_HBM],
    )
    swap = functools.partial(lax.ppermute, axis_name="local", perm=[(0, 1), (1, 0)])
    weights = [in_hbm(stack), swap(stack), in_hbm(w_down[0]), swap(w_down[0])]

    def along(block, pairs):
        moves = [(2 * a + y, 2 * b + y) for a, b in pairs for y in range(2)]
        return lax.ppermute(block, "node", moves)

    def across(block):
        return lax.ppermute(block, "node", [(n, n ^ 1) for n in range(experts)])

    def pick(blocks, users, after=()):
        return call(
            functools.partial(pick_kernel, users),
            [bf16((count, cap)), bf16((count, cap)), bf16((cap, wide)), bf16((cap, wide))],
            blocks,
            after,
            [pltpu.VMEM((count, wide), jnp.bfloat16), pltpu.SemaphoreType.DMA],
            [ANYWHERE] * len(blocks),
        )

    def expert(own_rows, other_rows, after=()):
        tiles = 2 * hidden // size
        return call(
            functools.partial(expert_kernel, experts),
            [bf16((cap, width)), bf16((cap, width))],
            [own_rows, other_rows, *weights],
            after,
            [
                pltpu.VMEM((2 * cap, width), jnp.bfloat16),
                pltpu.VMEM((2 * cap, 2 * hidden), jnp.bfloat16),
                pltpu.VMEM((tiles, width, size), jnp.bfloat16),
                pltpu.VMEM((tiles, width, size), jnp.bfloat16),
                pltpu.VMEM((2, hidden, width), jnp.bfloat16),
                pltpu.SemaphoreType.DMA((tiles, 3)),
            ],
            [IN_VMEM] * 2 + [ANYWHERE] * 4,
            36,
        )

    def spread(maps, own_out, other_out, extras=(), after=()):
        return call(spread_kernel, [bf16((count, width))], [*maps, own_out, other_out, *extras], after)[0]

    plan = arrivals(places)
    held = {}

    last = []

    def ordered(function, *args, after=()):
        out = function(*args, after=(*last, *after))
        last[:] = [out[0] if isinstance(out, (list, tuple)) else out]
        return out

    picks, outs, returned = {}, {}, []

    def relay(step):
        for way in (1, -1):
            pairs = [
                (a, a + way)
                for a in range(places)
                if 0 <= a + way < places and 0 <= a - way * (step - 1) < places
            ]
            held[way, step] = along(held.get((way, step - 1), block), pairs)

    def do_pick(slot, after=()):
        keys = sorted({row[slot - 1] for row in plan})
        blocks = [held[key] for key in keys]
        users = [[place for place, row in enumerate(plan) if row[slot - 1] == key] for key in keys]
        *maps, own_rows, other_rows = ordered(pick, blocks, users, after=after)
        picks[slot] = maps, own_rows, across(other_rows)

    def do_expert(slot, after=()):
        own_out, other_out = ordered(expert, picks[slot][1], picks[slot][2], after=after)
        outs[slot] = own_out, across(other_out)

    def do_spread(slot, after=()):
        done = ordered(spread, picks[slot][0], *outs[slot], after=after)
        home = [(a, a - row[slot - 1][0] * row[slot - 1][1]) for a, row in enumerate(plan)]
        rounds = []
        while home:
            now = list({b: (a, b) for a, b in home}.values())
            home = [pair for pair in home if pair not in now]
            rounds.append(along(done, now))
        returned.append(rounds)

    relay(1)
    picks[0] = picked[:2], picked[2], across(picked[3])
    held[1, 1], held[-1, 1] = tied([held[1, 1], held[-1, 1]], [picks[0][2]])
    for step in range(2, places):
        relay(step)
    do_pick(1)
    do_expert(0)
    do_expert(1)
    do_pick(2, after=[outs[0][1]])
    total = ordered(spread, picks[0][0], *outs[0])
    do_spread(1)
    for slot in range(2, places):
        do_expert(slot, after=returned[slot - 3] if slot > 2 else ())
        if slot + 1 < places:
            do_pick(slot + 1)
        if slot > 2:
            do_spread(slot - 1)
    do_spread(places - 1)
    total = total.astype(jnp.float32)
    for block in sum(returned, []):
        total = total + block.astype(jnp.float32)
    return total.astype(jnp.bfloat16)


def solution(mesh):
    placed = (
        P(("groups", "node", "local"), None),
        P(("groups", "node", "local"), None),
        P(("groups", "node", "local"), None),
        P("node", None, "local"),
        P("node", None, "local"),
        P("node", "local", None),
    )
    return jax.shard_map(
        on_device,
        mesh=mesh,
        in_specs=placed,
        out_specs=P(("groups", "node", "local"), None),
        check_vma=False,
    )
```

```python
import functools

import jax
import jax.numpy as jnp
from jax import lax
from jax.experimental import pallas as pl
from jax.experimental.pallas import tpu as pltpu
from jax.sharding import PartitionSpec as P

ANYWHERE = pl.BlockSpec(memory_space=pl.ANY)
IN_VMEM = pl.BlockSpec(memory_space=pltpu.VMEM)
MIB = 1024 * 1024


def arrivals(places):
    plan = []
    for place in range(places):
        left = [(-1, step) for step in range(1, places - place)]
        right = [(1, step) for step in range(1, place + 1)]
        plan.append(left + right if place < places // 2 else right + left)
    return plan


def call(kernel, outs, ins, after=(), scratch=(), specs=None, vmem=16, out_specs=None):
    body = kernel
    if after:
        first, last = len(ins), len(ins) + len(after)

        def body(*refs):
            kernel(*refs[:first], *refs[last:])

    specs = list(specs or [IN_VMEM] * len(ins)) + [ANYWHERE] * len(after)
    return pl.pallas_call(
        body,
        out_shape=outs,
        in_specs=specs,
        out_specs=out_specs or [IN_VMEM] * len(outs),
        scratch_shapes=scratch,
        compiler_params=pltpu.CompilerParams(vmem_limit_bytes=vmem * MIB),
        cost_estimate=pl.CostEstimate(flops=0, bytes_accessed=0, transcendentals=0),
    )(*ins, *after)


def in_vmem(array):
    return pltpu.with_memory_space_constraint(array, pltpu.VMEM)


def tied(arrays, after):
    return pl.pallas_call(
        lambda *refs: None,
        out_shape=[jax.ShapeDtypeStruct(a.shape, a.dtype) for a in arrays],
        in_specs=[ANYWHERE] * (len(arrays) + len(after)),
        out_specs=[ANYWHERE] * len(arrays),
        input_output_aliases={k: k for k in range(len(arrays))},
        cost_estimate=pl.CostEstimate(flops=0, bytes_accessed=0, transcendentals=0),
    )(*[in_vmem(a) for a in arrays], *after)


def first_kernel(experts, tokens, routes, scale, gate_w, up_w, block, *refs):
    picked, (stack, sems) = refs[:4], refs[4:]
    copies = [
        pltpu.make_async_copy(gate_w, stack.at[0], sems.at[0]),
        pltpu.make_async_copy(up_w, stack.at[1], sems.at[1]),
    ]
    for copy in copies:
        copy.start()
    count, width = tokens.shape
    lane = lax.broadcasted_iota(jnp.int32, (count, block.shape[1] - width), 1)
    expert, part = lax.rem(lane, experts), lax.div(lane, experts)
    weight = jnp.zeros(lane.shape, jnp.float32)
    routes, scale = routes[...].T, scale[...].T
    for r in range(routes.shape[1]):
        weight += jnp.where(routes[:, r : r + 1] == expert, scale[:, r : r + 1], 0.0)
    high = weight.astype(jnp.bfloat16).astype(jnp.float32)
    middle = (weight - high).astype(jnp.bfloat16).astype(jnp.float32)
    low = weight - high - middle
    marks = jnp.where(part == 0, high, jnp.where(part == 1, middle, jnp.where(part == 2, low, 0.0)))
    block[:, :width] = tokens[...]
    block[:, width:] = marks.astype(jnp.bfloat16)
    choose(block, *picked)
    for copy in copies:
        copy.wait()


def choose(held, own_map, other_map, own_rows, other_rows):
    node = lax.axis_index("node")
    count, cap = own_map.shape
    marks = held[:, held.shape[1] - 128 :].astype(jnp.float32)
    lane = lax.broadcasted_iota(jnp.int32, marks.shape, 1)
    earlier = lax.broadcasted_iota(jnp.int32, (count, count), 0) > lax.broadcasted_iota(jnp.int32, (count, count), 1)
    named = jnp.where(marks != 0, 1.0, 0.0)
    rank = jnp.dot(
        jnp.where(earlier, 1.0, 0.0).astype(jnp.bfloat16), named.astype(jnp.bfloat16), preferred_element_type=jnp.float32
    )
    place = jnp.where(named > 0, rank, -1.0)
    slot = lax.broadcasted_iota(jnp.int32, (count, cap), 1)
    for expert, one_hot, rows in ((node, own_map, own_rows), (node ^ 1, other_map, other_rows)):
        mine = jnp.sum(jnp.where(lane == expert, place, 0.0), axis=1, keepdims=True).astype(jnp.int32)
        chosen = jnp.where(mine == slot, 1.0, 0.0).astype(jnp.bfloat16)
        one_hot[...] = chosen
        rows[...] = lax.dot_general(
            chosen, held[...], (((0,), (0,)), ((), ())), preferred_element_type=jnp.float32
        ).astype(jnp.bfloat16)


def pick_kernel(users, *refs):
    blocks, (held, sem) = refs[: len(users)], refs[len(users) + 4 :]
    node = lax.axis_index("node")
    for block, places in zip(blocks, users):
        here = functools.reduce(jnp.logical_or, [lax.div(node, 2) == place for place in places])

        @pl.when(here)
        def _():
            copy = pltpu.make_async_copy(block, held, sem)
            copy.start()
            copy.wait()

    choose(held, *refs[len(users) : len(users) + 4])


def expert_kernel(experts, own, other, *refs):
    own_w, other_w, own_down, other_down, own_out, other_out, rows, hidden, gates, ups, downs, sems = refs
    cap, width = own_out.shape
    tiles, _, size = gates.shape
    each = tiles // 2
    queue = []
    for tile in range(tiles):
        stack, part = (own_w, other_w)[tile // each], pl.ds(tile % each * size, size)
        queue.append(pltpu.make_async_copy(stack.at[0, :, part], gates.at[tile], sems.at[tile, 0]))
        queue.append(pltpu.make_async_copy(stack.at[1, :, part], ups.at[tile], sems.at[tile, 1]))
    for half, down in enumerate((own_down, other_down)):
        queue.append(pltpu.make_async_copy(down, downs.at[half], sems.at[half, 2]))
    ahead = iter(queue[4:])
    for copy in queue[:4]:
        copy.start()

    def arrived(copy):
        copy.wait()
        for following in ahead:
            following.start()
            break

    rows[:cap] = own[:, :width]
    rows[cap:] = other[:, :width]
    for tile in range(tiles):
        arrived(queue[2 * tile])
        gate = jnp.dot(rows[...], gates[tile], preferred_element_type=jnp.float32)
        arrived(queue[2 * tile + 1])
        up = jnp.dot(rows[...], ups[tile], preferred_element_type=jnp.float32)
        hidden[:, tile * size : (tile + 1) * size] = (gate / (1.0 + jnp.exp(-gate)) * up).astype(jnp.bfloat16)
    arrived(queue[-2])
    arrived(queue[-1])
    node = lax.axis_index("node")
    scales = []
    for marked in (own, other):
        marks = marked[:, width:].astype(jnp.float32)
        lane = lax.broadcasted_iota(jnp.int32, marks.shape, 1)
        mine = (lax.rem(lane, experts) == node) & (lane < 3 * experts)
        scales.append(jnp.sum(jnp.where(mine, marks, 0.0), axis=1, keepdims=True))
    step = 512 if width % 512 == 0 else width
    for start in range(0, width, step):
        cut = slice(start, start + step)
        out = jnp.dot(hidden[:, : each * size], downs[0, :, cut], preferred_element_type=jnp.float32)
        out += jnp.dot(hidden[:, each * size :], downs[1, :, cut], preferred_element_type=jnp.float32)
        own_out[:, cut] = (out[:cap] * scales[0]).astype(jnp.bfloat16)
        other_out[:, cut] = (out[cap:] * scales[1]).astype(jnp.bfloat16)


def spread_kernel(own_map, other_map, own_out, other_out, *refs):
    result = refs[-1]
    total = jnp.dot(own_map[...], own_out[...], preferred_element_type=jnp.float32)
    total += jnp.dot(other_map[...], other_out[...], preferred_element_type=jnp.float32)
    for extra in refs[:-1]:
        total += extra[...].astype(jnp.float32)
    result[...] = total.astype(jnp.bfloat16)


def on_device(tokens, routes, route_scale, w_gate, w_up, w_down):
    count, width = tokens.shape
    experts = lax.axis_size("node")
    places = experts // 2
    hidden = w_gate.shape[2]
    size = min(hidden, 256)
    cap = -(-(5 * count // experts) // 16) * 16
    wide = width + -(-3 * experts // 128) * 128
    in_hbm = functools.partial(pltpu.with_memory_space_constraint, memory_space=pltpu.HBM)
    bf16 = functools.partial(jax.ShapeDtypeStruct, dtype=jnp.bfloat16)

    block, *picked, stack = call(
        functools.partial(first_kernel, experts),
        [
            bf16((count, wide)),
            bf16((count, cap)),
            bf16((count, cap)),
            bf16((cap, wide)),
            bf16((cap, wide)),
            bf16((2, width, hidden)),
        ],
        [tokens, routes.T, route_scale.T, in_hbm(w_gate[0]), in_hbm(w_up[0])],
        (),
        [pltpu.SemaphoreType.DMA((2,))],
        [IN_VMEM] * 3 + [ANYWHERE] * 2,
        out_specs=[IN_VMEM] * 6,
    )
    swap = functools.partial(lax.ppermute, axis_name="local", perm=[(0, 1), (1, 0)])
    weights = [in_hbm(stack), swap(stack), in_hbm(w_down[0]), swap(w_down[0])]

    def along(block, pairs):
        moves = [(2 * a + y, 2 * b + y) for a, b in pairs for y in range(2)]
        return lax.ppermute(block, "node", moves)

    def across(block):
        return lax.ppermute(block, "node", [(n, n ^ 1) for n in range(experts)])

    def pick(blocks, users, after=()):
        return call(
            functools.partial(pick_kernel, users),
            [bf16((count, cap)), bf16((count, cap)), bf16((cap, wide)), bf16((cap, wide))],
            blocks,
            after,
            [pltpu.VMEM((count, wide), jnp.bfloat16), pltpu.SemaphoreType.DMA],
            [ANYWHERE] * len(blocks),
        )

    def expert(own_rows, other_rows, after=()):
        tiles = 2 * hidden // size
        return call(
            functools.partial(expert_kernel, experts),
            [bf16((cap, width)), bf16((cap, width))],
            [own_rows, other_rows, *weights],
            after,
            [
                pltpu.VMEM((2 * cap, width), jnp.bfloat16),
                pltpu.VMEM((2 * cap, 2 * hidden), jnp.bfloat16),
                pltpu.VMEM((tiles, width, size), jnp.bfloat16),
                pltpu.VMEM((tiles, width, size), jnp.bfloat16),
                pltpu.VMEM((2, hidden, width), jnp.bfloat16),
                pltpu.SemaphoreType.DMA((tiles, 3)),
            ],
            [IN_VMEM] * 2 + [ANYWHERE] * 4,
            32,
        )

    def spread(maps, own_out, other_out, extras=(), after=()):
        return call(spread_kernel, [bf16((count, width))], [*maps, own_out, other_out, *extras], after)[0]

    plan = arrivals(places)
    held = {}

    last = []

    def ordered(function, *args, after=()):
        out = function(*args, after=(*last, *after))
        last[:] = [out[0] if isinstance(out, (list, tuple)) else out]
        return out

    picks, outs, returned = {}, {}, []

    def relay(step):
        for way in (1, -1):
            pairs = [
                (a, a + way)
                for a in range(places)
                if 0 <= a + way < places and 0 <= a - way * (step - 1) < places
            ]
            held[way, step] = along(held.get((way, step - 1), block), pairs)

    def hold(step, until):
        held[1, step], held[-1, step] = tied([held[1, step], held[-1, step]], until)

    def do_pick(slot, after=()):
        keys = sorted({row[slot - 1] for row in plan})
        blocks = [held[key] for key in keys]
        users = [[place for place, row in enumerate(plan) if row[slot - 1] == key] for key in keys]
        *maps, own_rows, other_rows = ordered(pick, blocks, users, after=after)
        picks[slot] = maps, own_rows, across(other_rows)

    def do_expert(slot, after=()):
        own_out, other_out = ordered(expert, picks[slot][1], picks[slot][2], after=after)
        outs[slot] = own_out, across(other_out)

    def do_spread(slot, after=()):
        done = ordered(spread, picks[slot][0], *outs[slot], after=after)
        home = [(a, a - row[slot - 1][0] * row[slot - 1][1]) for a, row in enumerate(plan)]
        rounds = []
        while home:
            now = list({b: (a, b) for a, b in home}.values())
            home = [pair for pair in home if pair not in now]
            rounds.append(along(done, now))
        returned.append(rounds)

    relay(1)
    picks[0] = picked[:2], picked[2], across(picked[3])
    hold(1, [picks[0][2]])
    relay(2)
    do_pick(1)
    do_expert(0)
    hold(2, [picks[1][2], outs[0][0]])
    for step in range(3, places):
        relay(step)
    do_pick(2)
    do_expert(1, after=[outs[0][1]])
    total = ordered(spread, picks[0][0], *outs[0], after=[picks[2][2]])
    do_expert(2)
    for slot in range(3, places):
        do_pick(slot)
        do_spread(slot - 2)
        do_expert(slot)
        do_spread(slot - 1)
    do_spread(places - 1, after=returned[0])
    total = total.astype(jnp.float32)
    for block in sum(returned, []):
        total = total + block.astype(jnp.float32)
    return total.astype(jnp.bfloat16)


def solution(mesh):
    placed = (
        P(("groups", "node", "local"), None),
        P(("groups", "node", "local"), None),
        P(("groups", "node", "local"), None),
        P("node", None, "local"),
        P("node", None, "local"),
        P("node", "local", None),
    )
    return jax.shard_map(
        on_device,
        mesh=mesh,
        in_specs=placed,
        out_specs=P(("groups", "node", "local"), None),
        check_vma=False,
    )
```

```python
import functools

import jax
import jax.numpy as jnp
from jax import lax
from jax.experimental import pallas as pl
from jax.experimental.pallas import tpu as pltpu
from jax.sharding import PartitionSpec as P

ANYWHERE = pl.BlockSpec(memory_space=pl.ANY)
IN_VMEM = pl.BlockSpec(memory_space=pltpu.VMEM)
MIB = 1024 * 1024


def arrivals(places):
    plan = []
    for place in range(places):
        left = [(-1, step) for step in range(1, places - place)]
        right = [(1, step) for step in range(1, place + 1)]
        plan.append(left + right if place < places // 2 else right + left)
    return plan


def call(kernel, outs, ins, after=(), scratch=(), specs=None, vmem=16, out_specs=None):
    body = kernel
    if after:
        first, last = len(ins), len(ins) + len(after)

        def body(*refs):
            kernel(*refs[:first], *refs[last:])

    specs = list(specs or [IN_VMEM] * len(ins)) + [ANYWHERE] * len(after)
    return pl.pallas_call(
        body,
        out_shape=outs,
        in_specs=specs,
        out_specs=out_specs or [IN_VMEM] * len(outs),
        scratch_shapes=scratch,
        compiler_params=pltpu.CompilerParams(vmem_limit_bytes=vmem * MIB),
        cost_estimate=pl.CostEstimate(flops=0, bytes_accessed=0, transcendentals=0),
    )(*ins, *after)


def in_vmem(array):
    return pltpu.with_memory_space_constraint(array, pltpu.VMEM)


def tied(arrays, after):
    return pl.pallas_call(
        lambda *refs: None,
        out_shape=[jax.ShapeDtypeStruct(a.shape, a.dtype) for a in arrays],
        in_specs=[ANYWHERE] * (len(arrays) + len(after)),
        out_specs=[ANYWHERE] * len(arrays),
        input_output_aliases={k: k for k in range(len(arrays))},
        cost_estimate=pl.CostEstimate(flops=0, bytes_accessed=0, transcendentals=0),
    )(*[in_vmem(a) for a in arrays], *after)


def first_kernel(experts, tokens, routes, scale, block, *picked):
    count, width = tokens.shape
    lane = lax.broadcasted_iota(jnp.int32, (count, block.shape[1] - width), 1)
    expert, part = lax.rem(lane, experts), lax.div(lane, experts)
    weight = jnp.zeros(lane.shape, jnp.float32)
    routes, scale = routes[...].T, scale[...].T
    for r in range(routes.shape[1]):
        weight += jnp.where(routes[:, r : r + 1] == expert, scale[:, r : r + 1], 0.0)
    high = weight.astype(jnp.bfloat16).astype(jnp.float32)
    middle = (weight - high).astype(jnp.bfloat16).astype(jnp.float32)
    low = weight - high - middle
    marks = jnp.where(part == 0, high, jnp.where(part == 1, middle, jnp.where(part == 2, low, 0.0)))
    block[:, :width] = tokens[...]
    block[:, width:] = marks.astype(jnp.bfloat16)
    choose(block, *picked)


def copy_kernel(source, result, held, sems):
    pieces = sems.shape[1]
    rows = source.shape[0] // pieces
    cuts = [pl.ds(k * rows, rows) for k in range(pieces)]
    fetch = [pltpu.make_async_copy(source.at[cut], held.at[cut], sems.at[0, k]) for k, cut in enumerate(cuts)]
    store = [pltpu.make_async_copy(held.at[cut], result.at[cut], sems.at[1, k]) for k, cut in enumerate(cuts)]
    for copy in fetch:
        copy.start()
    for arrived, leaving in zip(fetch, store):
        arrived.wait()
        leaving.start()
    for copy in store:
        copy.wait()


def passing_kernel(*refs):
    for source, result in zip(refs, refs[len(refs) // 2 :]):
        result[...] = source[...]


def choose(held, own_map, other_map, own_rows, other_rows):
    node = lax.axis_index("node")
    count, cap = own_map.shape
    marks = held[:, held.shape[1] - 128 :].astype(jnp.float32)
    lane = lax.broadcasted_iota(jnp.int32, marks.shape, 1)
    earlier = lax.broadcasted_iota(jnp.int32, (count, count), 0) > lax.broadcasted_iota(jnp.int32, (count, count), 1)
    named = jnp.where(marks != 0, 1.0, 0.0)
    rank = jnp.dot(
        jnp.where(earlier, 1.0, 0.0).astype(jnp.bfloat16), named.astype(jnp.bfloat16), preferred_element_type=jnp.float32
    )
    place = jnp.where(named > 0, rank, -1.0)
    slot = lax.broadcasted_iota(jnp.int32, (count, cap), 1)
    for expert, one_hot, rows in ((node, own_map, own_rows), (node ^ 1, other_map, other_rows)):
        mine = jnp.sum(jnp.where(lane == expert, place, 0.0), axis=1, keepdims=True).astype(jnp.int32)
        chosen = jnp.where(mine == slot, 1.0, 0.0).astype(jnp.bfloat16)
        one_hot[...] = chosen
        rows[...] = lax.dot_general(
            chosen, held[...], (((0,), (0,)), ((), ())), preferred_element_type=jnp.float32
        ).astype(jnp.bfloat16)


def pick_kernel(users, *refs):
    blocks, (held, sem) = refs[: len(users)], refs[len(users) + 4 :]
    node = lax.axis_index("node")
    for block, places in zip(blocks, users):
        here = functools.reduce(jnp.logical_or, [lax.div(node, 2) == place for place in places])

        @pl.when(here)
        def _():
            copy = pltpu.make_async_copy(block, held, sem)
            copy.start()
            copy.wait()

    choose(held, *refs[len(users) : len(users) + 4])


def expert_kernel(experts, own, other, *refs):
    weights, (own_out, other_out, rows, hidden, gates, ups, downs, sems) = refs[:6], refs[6:]
    cap, width = own_out.shape
    tiles, _, size = gates.shape
    each = tiles // 2
    queue = []
    for tile in range(tiles):
        part = pl.ds(tile % each * size, size)
        gate_w, up_w = weights[tile // each * 3 : tile // each * 3 + 2]
        queue.append(pltpu.make_async_copy(gate_w.at[:, part], gates.at[tile], sems.at[tile, 0]))
        queue.append(pltpu.make_async_copy(up_w.at[:, part], ups.at[tile], sems.at[tile, 1]))
    for half, down in enumerate(weights[2::3]):
        queue.append(pltpu.make_async_copy(down, downs.at[half], sems.at[half, 2]))
    ahead = iter(queue[4:])
    for copy in queue[:4]:
        copy.start()

    def arrived(copy):
        copy.wait()
        for following in ahead:
            following.start()
            break

    rows[:cap] = own[:, :width]
    rows[cap:] = other[:, :width]
    for tile in range(tiles):
        arrived(queue[2 * tile])
        gate = jnp.dot(rows[...], gates[tile], preferred_element_type=jnp.float32)
        arrived(queue[2 * tile + 1])
        up = jnp.dot(rows[...], ups[tile], preferred_element_type=jnp.float32)
        hidden[:, tile * size : (tile + 1) * size] = (gate / (1.0 + jnp.exp(-gate)) * up).astype(jnp.bfloat16)
    arrived(queue[-2])
    arrived(queue[-1])
    node = lax.axis_index("node")
    scales = []
    for marked in (own, other):
        marks = marked[:, width:].astype(jnp.float32)
        lane = lax.broadcasted_iota(jnp.int32, marks.shape, 1)
        mine = (lax.rem(lane, experts) == node) & (lane < 3 * experts)
        scales.append(jnp.sum(jnp.where(mine, marks, 0.0), axis=1, keepdims=True))
    step = 512 if width % 512 == 0 else width
    for start in range(0, width, step):
        cut = slice(start, start + step)
        out = jnp.dot(hidden[:, : each * size], downs[0, :, cut], preferred_element_type=jnp.float32)
        out += jnp.dot(hidden[:, each * size :], downs[1, :, cut], preferred_element_type=jnp.float32)
        own_out[:, cut] = (out[:cap] * scales[0]).astype(jnp.bfloat16)
        other_out[:, cut] = (out[cap:] * scales[1]).astype(jnp.bfloat16)


def spread_kernel(own_map, other_map, own_out, other_out, *refs):
    result = refs[-1]
    total = jnp.dot(own_map[...], own_out[...], preferred_element_type=jnp.float32)
    total += jnp.dot(other_map[...], other_out[...], preferred_element_type=jnp.float32)
    for extra in refs[:-1]:
        total += extra[...].astype(jnp.float32)
    result[...] = total.astype(jnp.bfloat16)


def on_device(tokens, routes, route_scale, w_gate, w_up, w_down):
    count, width = tokens.shape
    experts = lax.axis_size("node")
    places = experts // 2
    hidden = w_gate.shape[2]
    size = min(hidden, 256)
    cap = -(-(5 * count // experts) // 16) * 16
    wide = width + -(-3 * experts // 128) * 128
    hbm = functools.partial(pltpu.HBM, dtype=jnp.bfloat16)
    in_hbm = functools.partial(pltpu.with_memory_space_constraint, memory_space=pltpu.HBM)
    bf16 = functools.partial(jax.ShapeDtypeStruct, dtype=jnp.bfloat16)

    block, *picked = call(
        functools.partial(first_kernel, experts),
        [
            bf16((count, wide)),
            bf16((count, cap)),
            bf16((count, cap)),
            bf16((cap, wide)),
            bf16((cap, wide)),
        ],
        [in_hbm(tokens), in_hbm(routes.T), in_hbm(route_scale.T)],
    )
    own = (w_gate[0], w_up[0], w_down[0])
    swap = functools.partial(lax.ppermute, axis_name="local", perm=[(0, 1), (1, 0)])
    others = [swap(own[0]), swap(own[1])]

    def along(block, pairs):
        moves = [(2 * a + y, 2 * b + y) for a, b in pairs for y in range(2)]
        return lax.ppermute(block, "node", moves)

    def across(block):
        return lax.ppermute(block, "node", [(n, n ^ 1) for n in range(experts)])

    def pick(blocks, users, after=()):
        return call(
            functools.partial(pick_kernel, users),
            [bf16((count, cap)), bf16((count, cap)), bf16((cap, wide)), bf16((cap, wide))],
            blocks,
            after,
            [pltpu.VMEM((count, wide), jnp.bfloat16), pltpu.SemaphoreType.DMA],
            [ANYWHERE] * len(blocks),
        )

    def expert(own_rows, other_rows, after=()):
        tiles = 2 * hidden // size
        return call(
            functools.partial(expert_kernel, experts),
            [bf16((cap, width)), bf16((cap, width))],
            [own_rows, other_rows, *weights],
            after,
            [
                pltpu.VMEM((2 * cap, width), jnp.bfloat16),
                pltpu.VMEM((2 * cap, 2 * hidden), jnp.bfloat16),
                pltpu.VMEM((tiles, width, size), jnp.bfloat16),
                pltpu.VMEM((tiles, width, size), jnp.bfloat16),
                pltpu.VMEM((2, hidden, width), jnp.bfloat16),
                pltpu.SemaphoreType.DMA((tiles, 3)),
            ],
            [IN_VMEM] * 2 + [ANYWHERE] * 6,
            32,
        )

    def carry(weight, after=()):
        return call(
            copy_kernel,
            [hbm(weight.shape)],
            [in_hbm(weight)],
            after,
            [pltpu.VMEM(weight.shape, jnp.bfloat16), pltpu.SemaphoreType.DMA((2, 4))],
            [ANYWHERE],
            out_specs=[ANYWHERE],
        )

    def spread(maps, own_out, other_out, extras=(), after=()):
        return call(spread_kernel, [bf16((count, width))], [*maps, own_out, other_out, *extras], after)[0]

    plan = arrivals(places)
    held = {}

    last = []

    def ordered(function, *args, after=()):
        out = function(*args, after=(*last, *after))
        last[:] = [out[0] if isinstance(out, (list, tuple)) else out]
        return out

    picks, outs, returned = {}, {}, []

    def relay(step):
        for way in (1, -1):
            pairs = [
                (a, a + way)
                for a in range(places)
                if 0 <= a + way < places and 0 <= a - way * (step - 1) < places
            ]
            held[way, step] = along(held.get((way, step - 1), block), pairs)

    def do_pick(slot, after=()):
        keys = sorted({row[slot - 1] for row in plan})
        blocks = [held[key] for key in keys]
        users = [[place for place, row in enumerate(plan) if row[slot - 1] == key] for key in keys]
        *maps, own_rows, other_rows = ordered(pick, blocks, users, after=after)
        picks[slot] = maps, own_rows, across(other_rows)

    def do_expert(slot, after=()):
        own_out, other_out = ordered(expert, picks[slot][1], picks[slot][2], after=after)
        outs[slot] = own_out, across(other_out)

    def do_spread(slot, after=()):
        done = ordered(spread, picks[slot][0], *outs[slot], after=after)
        home = [(a, a - row[slot - 1][0] * row[slot - 1][1]) for a, row in enumerate(plan)]
        rounds = []
        while home:
            now = list({b: (a, b) for a, b in home}.values())
            home = [pair for pair in home if pair not in now]
            rounds.append(along(done, now))
        returned.append(rounds)

    relay(1)
    picks[0] = picked[:2], picked[2], across(picked[3])
    (down,) = carry(own[2], [picks[0][2]])
    held[1, 1], held[-1, 1] = tied([held[1, 1], held[-1, 1]], [down, *others])
    others.append(swap(down))
    weights = [*map(in_hbm, own), *others]
    relay(2)
    do_pick(1)
    held[1, 2], held[-1, 2] = call(
        passing_kernel, [bf16((count, wide))] * 2, [held[1, 2], held[-1, 2]], [*last, picks[1][2]]
    )
    for step in range(3, places):
        relay(step)
    do_expert(1)
    do_pick(2)
    do_expert(0)
    do_spread(1)
    do_pick(3)
    do_expert(2)
    for slot in range(3, places):
        do_spread(slot - 1, after=returned[slot - 3])
        do_expert(slot)
        if slot + 1 < places:
            do_pick(slot + 1)
    total = ordered(spread, picks[0][0], *outs[0])
    do_spread(places - 1)
    total = total.astype(jnp.float32)
    for block in sum(returned, []):
        total = total + block.astype(jnp.float32)
    return total.astype(jnp.bfloat16)


def solution(mesh):
    placed = (
        P(("groups", "node", "local"), None),
        P(("groups", "node", "local"), None),
        P(("groups", "node", "local"), None),
        P("node", None, "local"),
        P("node", None, "local"),
        P("node", "local", None),
    )
    return jax.shard_map(
        on_device,
        mesh=mesh,
        in_specs=placed,
        out_specs=P(("groups", "node", "local"), None),
        check_vma=False,
    )
```

```python
import functools

import jax
import jax.numpy as jnp
from jax import lax
from jax.experimental import pallas as pl
from jax.experimental.pallas import tpu as pltpu
from jax.sharding import PartitionSpec as P

ANYWHERE = pl.BlockSpec(memory_space=pl.ANY)
IN_VMEM = pl.BlockSpec(memory_space=pltpu.VMEM)
MIB = 1024 * 1024


def arrivals(places):
    plan = []
    for place in range(places):
        left = [(-1, step) for step in range(1, places - place)]
        right = [(1, step) for step in range(1, place + 1)]
        plan.append(left + right if place < places // 2 else right + left)
    return plan


def call(kernel, outs, ins, after=(), scratch=(), specs=None, vmem=16, out_specs=None):
    body = kernel
    if after:
        first, last = len(ins), len(ins) + len(after)

        def body(*refs):
            kernel(*refs[:first], *refs[last:])

    specs = list(specs or [IN_VMEM] * len(ins)) + [ANYWHERE] * len(after)
    return pl.pallas_call(
        body,
        out_shape=outs,
        in_specs=specs,
        out_specs=out_specs or [IN_VMEM] * len(outs),
        scratch_shapes=scratch,
        compiler_params=pltpu.CompilerParams(vmem_limit_bytes=vmem * MIB),
        cost_estimate=pl.CostEstimate(flops=0, bytes_accessed=0, transcendentals=0),
    )(*ins, *after)


def in_vmem(array):
    return pltpu.with_memory_space_constraint(array, pltpu.VMEM)


def tied(arrays, after):
    return pl.pallas_call(
        lambda *refs: None,
        out_shape=[jax.ShapeDtypeStruct(a.shape, a.dtype) for a in arrays],
        in_specs=[ANYWHERE] * (len(arrays) + len(after)),
        out_specs=[ANYWHERE] * len(arrays),
        input_output_aliases={k: k for k in range(len(arrays))},
        cost_estimate=pl.CostEstimate(flops=0, bytes_accessed=0, transcendentals=0),
    )(*[in_vmem(a) for a in arrays], *after)


def first_kernel(experts, tokens, routes, scale, gate_w, up_w, block, *refs):
    picked, (stack, held, sems) = refs[:4], refs[4:]
    pieces = sems.shape[2]
    rows = gate_w.shape[0] // pieces
    fetch, store = [], []
    for k in range(pieces):
        cut = pl.ds(k * rows, rows)
        for n, source in enumerate((gate_w, up_w)):
            fetch.append(pltpu.make_async_copy(source.at[cut], held.at[n, cut], sems.at[0, n, k]))
            store.append(pltpu.make_async_copy(held.at[n, cut], stack.at[n, cut], sems.at[1, n, k]))
    for copy in fetch:
        copy.start()
    count, width = tokens.shape
    lane = lax.broadcasted_iota(jnp.int32, (count, block.shape[1] - width), 1)
    expert, part = lax.rem(lane, experts), lax.div(lane, experts)
    weight = jnp.zeros(lane.shape, jnp.float32)
    routes, scale = routes[...].T, scale[...].T
    for r in range(routes.shape[1]):
        weight += jnp.where(routes[:, r : r + 1] == expert, scale[:, r : r + 1], 0.0)
    high = weight.astype(jnp.bfloat16).astype(jnp.float32)
    middle = (weight - high).astype(jnp.bfloat16).astype(jnp.float32)
    low = weight - high - middle
    marks = jnp.where(part == 0, high, jnp.where(part == 1, middle, jnp.where(part == 2, low, 0.0)))
    block[:, :width] = tokens[...]
    block[:, width:] = marks.astype(jnp.bfloat16)
    for arrived, leaving in zip(fetch, store):
        arrived.wait()
        leaving.start()
    choose(block, *picked)
    for copy in store:
        copy.wait()


def passing_kernel(*refs):
    for source, result in zip(refs, refs[len(refs) // 2 :]):
        result[...] = source[...]


def choose(held, own_map, other_map, own_rows, other_rows):
    node = lax.axis_index("node")
    count, cap = own_map.shape
    marks = held[:, held.shape[1] - 128 :].astype(jnp.float32)
    lane = lax.broadcasted_iota(jnp.int32, marks.shape, 1)
    earlier = lax.broadcasted_iota(jnp.int32, (count, count), 0) > lax.broadcasted_iota(jnp.int32, (count, count), 1)
    named = jnp.where(marks != 0, 1.0, 0.0)
    rank = jnp.dot(
        jnp.where(earlier, 1.0, 0.0).astype(jnp.bfloat16), named.astype(jnp.bfloat16), preferred_element_type=jnp.float32
    )
    place = jnp.where(named > 0, rank, -1.0)
    slot = lax.broadcasted_iota(jnp.int32, (count, cap), 1)
    for expert, one_hot, rows in ((node, own_map, own_rows), (node ^ 1, other_map, other_rows)):
        mine = jnp.sum(jnp.where(lane == expert, place, 0.0), axis=1, keepdims=True).astype(jnp.int32)
        chosen = jnp.where(mine == slot, 1.0, 0.0).astype(jnp.bfloat16)
        one_hot[...] = chosen
        rows[...] = lax.dot_general(
            chosen, held[...], (((0,), (0,)), ((), ())), preferred_element_type=jnp.float32
        ).astype(jnp.bfloat16)


def pick_kernel(users, *refs):
    blocks, (held, sem) = refs[: len(users)], refs[len(users) + 4 :]
    node = lax.axis_index("node")
    for block, places in zip(blocks, users):
        here = functools.reduce(jnp.logical_or, [lax.div(node, 2) == place for place in places])

        @pl.when(here)
        def _():
            copy = pltpu.make_async_copy(block, held, sem)
            copy.start()
            copy.wait()

    choose(held, *refs[len(users) : len(users) + 4])


def expert_kernel(experts, own, other, *refs):
    own_w, other_w, own_down, other_down, own_out, other_out, rows, hidden, gates, ups, downs, sems = refs
    cap, width = own_out.shape
    tiles, _, size = gates.shape
    each = tiles // 2
    queue = []
    for tile in range(tiles):
        stack, part = (own_w, other_w)[tile // each], pl.ds(tile % each * size, size)
        queue.append(pltpu.make_async_copy(stack.at[0, :, part], gates.at[tile], sems.at[tile, 0]))
        queue.append(pltpu.make_async_copy(stack.at[1, :, part], ups.at[tile], sems.at[tile, 1]))
    for half, down in enumerate((own_down, other_down)):
        queue.append(pltpu.make_async_copy(down, downs.at[half], sems.at[half, 2]))
    ahead = iter(queue[4:])
    for copy in queue[:4]:
        copy.start()

    def arrived(copy):
        copy.wait()
        for following in ahead:
            following.start()
            break

    rows[:cap] = own[:, :width]
    rows[cap:] = other[:, :width]
    for tile in range(tiles):
        arrived(queue[2 * tile])
        gate = jnp.dot(rows[...], gates[tile], preferred_element_type=jnp.float32)
        arrived(queue[2 * tile + 1])
        up = jnp.dot(rows[...], ups[tile], preferred_element_type=jnp.float32)
        hidden[:, tile * size : (tile + 1) * size] = (gate / (1.0 + jnp.exp(-gate)) * up).astype(jnp.bfloat16)
    arrived(queue[-2])
    arrived(queue[-1])
    node = lax.axis_index("node")
    scales = []
    for marked in (own, other):
        marks = marked[:, width:].astype(jnp.float32)
        lane = lax.broadcasted_iota(jnp.int32, marks.shape, 1)
        mine = (lax.rem(lane, experts) == node) & (lane < 3 * experts)
        scales.append(jnp.sum(jnp.where(mine, marks, 0.0), axis=1, keepdims=True))
    step = 512 if width % 512 == 0 else width
    for start in range(0, width, step):
        cut = slice(start, start + step)
        out = jnp.dot(hidden[:, : each * size], downs[0, :, cut], preferred_element_type=jnp.float32)
        out += jnp.dot(hidden[:, each * size :], downs[1, :, cut], preferred_element_type=jnp.float32)
        own_out[:, cut] = (out[:cap] * scales[0]).astype(jnp.bfloat16)
        other_out[:, cut] = (out[cap:] * scales[1]).astype(jnp.bfloat16)


def spread_kernel(own_map, other_map, own_out, other_out, *refs):
    result = refs[-1]
    total = jnp.dot(own_map[...], own_out[...], preferred_element_type=jnp.float32)
    total += jnp.dot(other_map[...], other_out[...], preferred_element_type=jnp.float32)
    for extra in refs[:-1]:
        total += extra[...].astype(jnp.float32)
    result[...] = total.astype(jnp.bfloat16)


def on_device(tokens, routes, route_scale, w_gate, w_up, w_down):
    count, width = tokens.shape
    experts = lax.axis_size("node")
    places = experts // 2
    hidden = w_gate.shape[2]
    size = min(hidden, 256)
    cap = -(-(5 * count // experts) // 16) * 16
    wide = width + -(-3 * experts // 128) * 128
    hbm = functools.partial(pltpu.HBM, dtype=jnp.bfloat16)
    in_hbm = functools.partial(pltpu.with_memory_space_constraint, memory_space=pltpu.HBM)
    bf16 = functools.partial(jax.ShapeDtypeStruct, dtype=jnp.bfloat16)

    own = (w_gate[0], w_up[0], w_down[0])
    block, *picked, stack = call(
        functools.partial(first_kernel, experts),
        [
            bf16((count, wide)),
            bf16((count, cap)),
            bf16((count, cap)),
            bf16((cap, wide)),
            bf16((cap, wide)),
            hbm((2, width, hidden)),
        ],
        [*map(in_hbm, (tokens, routes.T, route_scale.T, own[0], own[1]))],
        (),
        [pltpu.VMEM((2, width, hidden), jnp.bfloat16), pltpu.SemaphoreType.DMA((2, 2, 4))],
        [IN_VMEM] * 3 + [ANYWHERE] * 2,
        out_specs=[IN_VMEM] * 5 + [ANYWHERE],
    )
    swap = functools.partial(lax.ppermute, axis_name="local", perm=[(0, 1), (1, 0)])
    weights = [in_hbm(stack), swap(stack), in_hbm(own[2]), swap(own[2])]

    def along(block, pairs):
        moves = [(2 * a + y, 2 * b + y) for a, b in pairs for y in range(2)]
        return lax.ppermute(block, "node", moves)

    def across(block):
        return lax.ppermute(block, "node", [(n, n ^ 1) for n in range(experts)])

    def pick(blocks, users, after=()):
        return call(
            functools.partial(pick_kernel, users),
            [bf16((count, cap)), bf16((count, cap)), bf16((cap, wide)), bf16((cap, wide))],
            blocks,
            after,
            [pltpu.VMEM((count, wide), jnp.bfloat16), pltpu.SemaphoreType.DMA],
            [ANYWHERE] * len(blocks),
        )

    def expert(own_rows, other_rows, after=()):
        tiles = 2 * hidden // size
        return call(
            functools.partial(expert_kernel, experts),
            [bf16((cap, width)), bf16((cap, width))],
            [own_rows, other_rows, *weights],
            after,
            [
                pltpu.VMEM((2 * cap, width), jnp.bfloat16),
                pltpu.VMEM((2 * cap, 2 * hidden), jnp.bfloat16),
                pltpu.VMEM((tiles, width, size), jnp.bfloat16),
                pltpu.VMEM((tiles, width, size), jnp.bfloat16),
                pltpu.VMEM((2, hidden, width), jnp.bfloat16),
                pltpu.SemaphoreType.DMA((tiles, 3)),
            ],
            [IN_VMEM] * 2 + [ANYWHERE] * 4,
            32,
        )

    def spread(maps, own_out, other_out, extras=(), after=()):
        return call(spread_kernel, [bf16((count, width))], [*maps, own_out, other_out, *extras], after)[0]

    plan = arrivals(places)
    held = {}

    last = []

    def ordered(function, *args, after=()):
        out = function(*args, after=(*last, *after))
        last[:] = [out[0] if isinstance(out, (list, tuple)) else out]
        return out

    picks, outs, returned = {}, {}, []

    def relay(step):
        for way in (1, -1):
            pairs = [
                (a, a + way)
                for a in range(places)
                if 0 <= a + way < places and 0 <= a - way * (step - 1) < places
            ]
            held[way, step] = along(held.get((way, step - 1), block), pairs)

    def do_pick(slot, after=()):
        keys = sorted({row[slot - 1] for row in plan})
        blocks = [held[key] for key in keys]
        users = [[place for place, row in enumerate(plan) if row[slot - 1] == key] for key in keys]
        *maps, own_rows, other_rows = ordered(pick, blocks, users, after=after)
        picks[slot] = maps, own_rows, across(other_rows)

    def do_expert(slot, after=()):
        own_out, other_out = ordered(expert, picks[slot][1], picks[slot][2], after=after)
        outs[slot] = own_out, across(other_out)

    def do_spread(slot, after=()):
        done = ordered(spread, picks[slot][0], *outs[slot], after=after)
        home = [(a, a - row[slot - 1][0] * row[slot - 1][1]) for a, row in enumerate(plan)]
        rounds = []
        while home:
            now = list({b: (a, b) for a, b in home}.values())
            home = [pair for pair in home if pair not in now]
            rounds.append(along(done, now))
        returned.append(rounds)

    relay(1)
    picks[0] = picked[:2], picked[2], across(picked[3])
    held[1, 1], held[-1, 1] = tied([held[1, 1], held[-1, 1]], [picks[0][2]])
    relay(2)
    do_pick(1)
    do_expert(0)
    held[1, 2], held[-1, 2] = call(
        passing_kernel, [bf16((count, wide))] * 2, [held[1, 2], held[-1, 2]], [*last, picks[1][2], outs[0][1]]
    )
    for step in range(3, places):
        relay(step)
    do_pick(2)
    do_expert(1)
    do_expert(2)
    do_spread(1)
    do_pick(3)
    for slot in range(3, places):
        do_expert(slot)
        do_spread(slot - 1, after=returned[slot - 3])
        if slot + 1 < places:
            do_pick(slot + 1)
    total = ordered(spread, picks[0][0], *outs[0])
    do_spread(places - 1)
    total = total.astype(jnp.float32)
    for block in sum(returned, []):
        total = total + block.astype(jnp.float32)
    return total.astype(jnp.bfloat16)


def solution(mesh):
    placed = (
        P(("groups", "node", "local"), None),
        P(("groups", "node", "local"), None),
        P(("groups", "node", "local"), None),
        P("node", None, "local"),
        P("node", None, "local"),
        P("node", "local", None),
    )
    return jax.shard_map(
        on_device,
        mesh=mesh,
        in_specs=placed,
        out_specs=P(("groups", "node", "local"), None),
        check_vma=False,
    )
```

```python
import functools

import jax
import jax.numpy as jnp
from jax import lax
from jax.experimental import pallas as pl
from jax.experimental.pallas import tpu as pltpu
from jax.sharding import PartitionSpec as P

ANYWHERE = pl.BlockSpec(memory_space=pl.ANY)
IN_VMEM = pl.BlockSpec(memory_space=pltpu.VMEM)
MIB = 1024 * 1024


def arrivals(places):
    plan = []
    for place in range(places):
        left = [(-1, step) for step in range(1, places - place)]
        right = [(1, step) for step in range(1, place + 1)]
        plan.append(left + right if place < places // 2 else right + left)
    return plan


def call(kernel, outs, ins, after=(), scratch=(), specs=None, vmem=16, out_specs=None, cost=0):
    body = kernel
    if after:
        first, last = len(ins), len(ins) + len(after)

        def body(*refs):
            kernel(*refs[:first], *refs[last:])

    specs = list(specs or [IN_VMEM] * len(ins)) + [ANYWHERE] * len(after)
    return pl.pallas_call(
        body,
        out_shape=outs,
        in_specs=specs,
        out_specs=out_specs or [IN_VMEM] * len(outs),
        scratch_shapes=scratch,
        compiler_params=pltpu.CompilerParams(vmem_limit_bytes=vmem * MIB),
        cost_estimate=pl.CostEstimate(flops=0, bytes_accessed=cost, transcendentals=0),
    )(*ins, *after)


def in_vmem(array):
    return pltpu.with_memory_space_constraint(array, pltpu.VMEM)


def tied(arrays, after):
    return pl.pallas_call(
        lambda *refs: None,
        out_shape=[jax.ShapeDtypeStruct(a.shape, a.dtype) for a in arrays],
        in_specs=[ANYWHERE] * (len(arrays) + len(after)),
        out_specs=[ANYWHERE] * len(arrays),
        input_output_aliases={k: k for k in range(len(arrays))},
        cost_estimate=pl.CostEstimate(flops=0, bytes_accessed=0, transcendentals=0),
    )(*[in_vmem(a) for a in arrays], *after)


def first_kernel(experts, tokens, routes, scale, gate_w, up_w, block, *refs):
    picked, (stack, held, sems) = refs[:4], refs[4:]
    pieces = sems.shape[2]
    rows = gate_w.shape[0] // pieces
    fetch, store = [], []
    for k in range(pieces):
        cut = pl.ds(k * rows, rows)
        for n, source in enumerate((gate_w, up_w)):
            fetch.append(pltpu.make_async_copy(source.at[cut], held.at[n, cut], sems.at[0, n, k]))
            store.append(pltpu.make_async_copy(held.at[n, cut], stack.at[n, cut], sems.at[1, n, k]))
    for copy in fetch:
        copy.start()
    count, width = tokens.shape
    lane = lax.broadcasted_iota(jnp.int32, (count, block.shape[1] - width), 1)
    expert, part = lax.rem(lane, experts), lax.div(lane, experts)
    weight = jnp.zeros(lane.shape, jnp.float32)
    routes, scale = routes[...].T, scale[...].T
    for r in range(routes.shape[1]):
        weight += jnp.where(routes[:, r : r + 1] == expert, scale[:, r : r + 1], 0.0)
    high = weight.astype(jnp.bfloat16).astype(jnp.float32)
    middle = (weight - high).astype(jnp.bfloat16).astype(jnp.float32)
    low = weight - high - middle
    marks = jnp.where(part == 0, high, jnp.where(part == 1, middle, jnp.where(part == 2, low, 0.0)))
    block[:, :width] = tokens[...]
    block[:, width:] = marks.astype(jnp.bfloat16)
    for arrived, leaving in zip(fetch, store):
        arrived.wait()
        leaving.start()
    choose(block, *picked)
    for copy in store:
        copy.wait()


def passing_kernel(*refs):
    for source, result in zip(refs, refs[len(refs) // 2 :]):
        result[...] = source[...]


def choose(held, own_map, other_map, own_rows, other_rows):
    node = lax.axis_index("node")
    count, cap = own_map.shape
    marks = held[:, held.shape[1] - 128 :].astype(jnp.float32)
    lane = lax.broadcasted_iota(jnp.int32, marks.shape, 1)
    earlier = lax.broadcasted_iota(jnp.int32, (count, count), 0) > lax.broadcasted_iota(jnp.int32, (count, count), 1)
    named = jnp.where(marks != 0, 1.0, 0.0)
    rank = jnp.dot(
        jnp.where(earlier, 1.0, 0.0).astype(jnp.bfloat16), named.astype(jnp.bfloat16), preferred_element_type=jnp.float32
    )
    place = jnp.where(named > 0, rank, -1.0)
    slot = lax.broadcasted_iota(jnp.int32, (count, cap), 1)
    for expert, one_hot, rows in ((node, own_map, own_rows), (node ^ 1, other_map, other_rows)):
        mine = jnp.sum(jnp.where(lane == expert, place, 0.0), axis=1, keepdims=True).astype(jnp.int32)
        chosen = jnp.where(mine == slot, 1.0, 0.0).astype(jnp.bfloat16)
        one_hot[...] = chosen
        rows[...] = lax.dot_general(
            chosen, held[...], (((0,), (0,)), ((), ())), preferred_element_type=jnp.float32
        ).astype(jnp.bfloat16)


def pick_kernel(users, *refs):
    blocks, (held, sem) = refs[: len(users)], refs[len(users) + 4 :]
    node = lax.axis_index("node")
    for block, places in zip(blocks, users):
        here = functools.reduce(jnp.logical_or, [lax.div(node, 2) == place for place in places])

        @pl.when(here)
        def _():
            copy = pltpu.make_async_copy(block, held, sem)
            copy.start()
            copy.wait()

    choose(held, *refs[len(users) : len(users) + 4])


def expert_kernel(experts, own, other, *refs):
    own_w, other_w, own_down, other_down, own_out, other_out, rows, hidden, gates, ups, downs, sems = refs
    cap, width = own_out.shape
    tiles, _, size = gates.shape
    each = tiles // 2
    queue = []
    for tile in range(tiles):
        stack, part = (own_w, other_w)[tile // each], pl.ds(tile % each * size, size)
        queue.append(pltpu.make_async_copy(stack.at[0, :, part], gates.at[tile], sems.at[tile, 0]))
        queue.append(pltpu.make_async_copy(stack.at[1, :, part], ups.at[tile], sems.at[tile, 1]))
    for half, down in enumerate((own_down, other_down)):
        queue.append(pltpu.make_async_copy(down, downs.at[half], sems.at[half, 2]))
    ahead = iter(queue[4:])
    for copy in queue[:4]:
        copy.start()

    def arrived(copy):
        copy.wait()
        for following in ahead:
            following.start()
            break

    rows[:cap] = own[:, :width]
    rows[cap:] = other[:, :width]
    for tile in range(tiles):
        arrived(queue[2 * tile])
        gate = jnp.dot(rows[...], gates[tile], preferred_element_type=jnp.float32)
        arrived(queue[2 * tile + 1])
        up = jnp.dot(rows[...], ups[tile], preferred_element_type=jnp.float32)
        hidden[:, tile * size : (tile + 1) * size] = (gate / (1.0 + jnp.exp(-gate)) * up).astype(jnp.bfloat16)
    arrived(queue[-2])
    arrived(queue[-1])
    node = lax.axis_index("node")
    scales = []
    for marked in (own, other):
        marks = marked[:, width:].astype(jnp.float32)
        lane = lax.broadcasted_iota(jnp.int32, marks.shape, 1)
        mine = (lax.rem(lane, experts) == node) & (lane < 3 * experts)
        scales.append(jnp.sum(jnp.where(mine, marks, 0.0), axis=1, keepdims=True))
    step = 512 if width % 512 == 0 else width
    for start in range(0, width, step):
        cut = slice(start, start + step)
        out = jnp.dot(hidden[:, : each * size], downs[0, :, cut], preferred_element_type=jnp.float32)
        out += jnp.dot(hidden[:, each * size :], downs[1, :, cut], preferred_element_type=jnp.float32)
        own_out[:, cut] = (out[:cap] * scales[0]).astype(jnp.bfloat16)
        other_out[:, cut] = (out[cap:] * scales[1]).astype(jnp.bfloat16)


def spread_kernel(own_map, other_map, own_out, other_out, *refs):
    result = refs[-1]
    total = jnp.dot(own_map[...], own_out[...], preferred_element_type=jnp.float32)
    total += jnp.dot(other_map[...], other_out[...], preferred_element_type=jnp.float32)
    for extra in refs[:-1]:
        total += extra[...].astype(jnp.float32)
    result[...] = total.astype(jnp.bfloat16)


def sum_kernel(*refs):
    total = refs[0][...].astype(jnp.float32)
    for extra in refs[1:-1]:
        total += extra[...].astype(jnp.float32)
    refs[-1][...] = total.astype(jnp.bfloat16)


def on_device(tokens, routes, route_scale, w_gate, w_up, w_down):
    count, width = tokens.shape
    experts = lax.axis_size("node")
    places = experts // 2
    hidden = w_gate.shape[2]
    size = min(hidden, 256)
    cap = -(-(5 * count // experts) // 16) * 16
    wide = width + -(-3 * experts // 128) * 128
    hbm = functools.partial(pltpu.HBM, dtype=jnp.bfloat16)
    in_hbm = functools.partial(pltpu.with_memory_space_constraint, memory_space=pltpu.HBM)
    bf16 = functools.partial(jax.ShapeDtypeStruct, dtype=jnp.bfloat16)

    own = (w_gate[0], w_up[0], w_down[0])
    block, *picked, stack = call(
        functools.partial(first_kernel, experts),
        [
            bf16((count, wide)),
            bf16((count, cap)),
            bf16((count, cap)),
            bf16((cap, wide)),
            bf16((cap, wide)),
            hbm((2, width, hidden)),
        ],
        [*map(in_hbm, (tokens, routes.T, route_scale.T, own[0], own[1]))],
        (),
        [pltpu.VMEM((2, width, hidden), jnp.bfloat16), pltpu.SemaphoreType.DMA((2, 2, 4))],
        [IN_VMEM] * 3 + [ANYWHERE] * 2,
        out_specs=[IN_VMEM] * 5 + [ANYWHERE],
    )
    swap = functools.partial(lax.ppermute, axis_name="local", perm=[(0, 1), (1, 0)])
    weights = [in_hbm(stack), swap(stack), in_hbm(own[2]), swap(own[2])]

    def along(block, pairs):
        moves = [(2 * a + y, 2 * b + y) for a, b in pairs for y in range(2)]
        return lax.ppermute(block, "node", moves)

    def across(block):
        return lax.ppermute(block, "node", [(n, n ^ 1) for n in range(experts)])

    def pick(blocks, users, after=()):
        return call(
            functools.partial(pick_kernel, users),
            [bf16((count, cap)), bf16((count, cap)), bf16((cap, wide)), bf16((cap, wide))],
            blocks,
            after,
            [pltpu.VMEM((count, wide), jnp.bfloat16), pltpu.SemaphoreType.DMA],
            [ANYWHERE] * len(blocks),
        )

    def expert(own_rows, other_rows, after=()):
        tiles = 2 * hidden // size
        return call(
            functools.partial(expert_kernel, experts),
            [bf16((cap, width)), bf16((cap, width))],
            [own_rows, other_rows, *weights],
            after,
            [
                pltpu.VMEM((2 * cap, width), jnp.bfloat16),
                pltpu.VMEM((2 * cap, 2 * hidden), jnp.bfloat16),
                pltpu.VMEM((tiles, width, size), jnp.bfloat16),
                pltpu.VMEM((tiles, width, size), jnp.bfloat16),
                pltpu.VMEM((2, hidden, width), jnp.bfloat16),
                pltpu.SemaphoreType.DMA((tiles, 3)),
            ],
            [IN_VMEM] * 2 + [ANYWHERE] * 4,
            32,
        )

    def spread(maps, own_out, other_out, extras=(), after=()):
        return call(spread_kernel, [bf16((count, width))], [*maps, own_out, other_out, *extras], after)[0]

    plan = arrivals(places)
    held = {}

    last = []

    def ordered(function, *args, after=(), **options):
        out = function(*args, after=(*last, *after), **options)
        last[:] = [out[0] if isinstance(out, (list, tuple)) else out]
        return out

    picks, outs, returned = {}, {}, []

    def relay(step):
        for way in (1, -1):
            pairs = [
                (a, a + way)
                for a in range(places)
                if 0 <= a + way < places and 0 <= a - way * (step - 1) < places
            ]
            held[way, step] = along(held.get((way, step - 1), block), pairs)

    def do_pick(slot, after=()):
        keys = sorted({row[slot - 1] for row in plan})
        blocks = [held[key] for key in keys]
        users = [[place for place, row in enumerate(plan) if row[slot - 1] == key] for key in keys]
        *maps, own_rows, other_rows = ordered(pick, blocks, users, after=after)
        picks[slot] = maps, own_rows, across(other_rows)

    def do_expert(slot, after=()):
        own_out, other_out = ordered(expert, picks[slot][1], picks[slot][2], after=after)
        outs[slot] = own_out, across(other_out)

    def origin(place, slot):
        way, step = plan[place][slot - 1]
        return place - way * step

    hops = []
    for place in range(places):
        target = origin(place, places - 1)
        near = place + (1 if target > place else -1)
        if near != target and origin(near, places - 2) == target:
            hops.append((place, near))
    staying = {places - 1: [a for a, _ in hops], places - 2: [b for _, b in hops]}
    kept = {}

    def do_spread(slot, after=()):
        kept[slot] = done = ordered(spread, picks[slot][0], *outs[slot], after=after)
        home = [(a, origin(a, slot)) for a in range(places) if a not in staying.get(slot, ())]
        rounds = []
        while home:
            now = list({b: (a, b) for a, b in home}.values())
            home = [pair for pair in home if pair not in now]
            rounds.append(along(done, now))
        returned.append(rounds)

    def call_sum(blocks, after=(), cost=0):
        return call(sum_kernel, [bf16((count, width))], blocks, after, cost=cost)

    relay(1)
    picks[0] = picked[:2], picked[2], across(picked[3])
    held[1, 1], held[-1, 1] = tied([held[1, 1], held[-1, 1]], [picks[0][2]])
    relay(2)
    do_pick(1)
    do_expert(1)
    held[1, 2], held[-1, 2] = call(
        passing_kernel, [bf16((count, wide))] * 2, [held[1, 2], held[-1, 2]], [*last, picks[1][2]]
    )
    for step in range(3, places):
        relay(step)
    do_pick(2)
    do_spread(1)
    do_pick(3)
    do_expert(2)
    for slot in range(3, places):
        do_expert(slot)
        do_spread(slot - 1, after=returned[slot - 3])
        if slot + 1 < places:
            do_pick(slot + 1)
    do_expert(0)
    do_spread(places - 1)
    near = returned.pop(places - 3)
    (summed,) = ordered(call_sum, [*returned.pop(0), *near] if places > 3 else near, cost=128 * MIB)
    (joined,) = ordered(call_sum, [kept[places - 2], along(kept[places - 1], hops)])
    returned.append([summed, along(joined, [(q, origin(q, places - 2)) for _, q in hops])])
    total = ordered(spread, picks[0][0], *outs[0])
    total = total.astype(jnp.float32)
    for block in sum(returned, []):
        total = total + block.astype(jnp.float32)
    return total.astype(jnp.bfloat16)


def solution(mesh):
    placed = (
        P(("groups", "node", "local"), None),
        P(("groups", "node", "local"), None),
        P(("groups", "node", "local"), None),
        P("node", None, "local"),
        P("node", None, "local"),
        P("node", "local", None),
    )
    return jax.shard_map(
        on_device,
        mesh=mesh,
        in_specs=placed,
        out_specs=P(("groups", "node", "local"), None),
        check_vma=False,
    )
```

```python
import functools

import jax
import jax.numpy as jnp
from jax import lax
from jax.experimental import pallas as pl
from jax.experimental.pallas import tpu as pltpu
from jax.sharding import PartitionSpec as P

ANYWHERE = pl.BlockSpec(memory_space=pl.ANY)
IN_VMEM = pl.BlockSpec(memory_space=pltpu.VMEM)
MIB = 1024 * 1024


def arrivals(places):
    plan = []
    for place in range(places):
        left = [(-1, step) for step in range(1, places - place)]
        right = [(1, step) for step in range(1, place + 1)]
        plan.append(left + right if place < places // 2 else right + left)
    return plan


def call(kernel, outs, ins, after=(), scratch=(), specs=None, vmem=16, out_specs=None, cost=0):
    body = kernel
    if after:
        first, last = len(ins), len(ins) + len(after)

        def body(*refs):
            kernel(*refs[:first], *refs[last:])

    specs = list(specs or [IN_VMEM] * len(ins)) + [ANYWHERE] * len(after)
    return pl.pallas_call(
        body,
        out_shape=outs,
        in_specs=specs,
        out_specs=out_specs or [IN_VMEM] * len(outs),
        scratch_shapes=scratch,
        compiler_params=pltpu.CompilerParams(vmem_limit_bytes=vmem * MIB),
        cost_estimate=pl.CostEstimate(flops=0, bytes_accessed=cost, transcendentals=0),
    )(*ins, *after)


def in_vmem(array):
    return pltpu.with_memory_space_constraint(array, pltpu.VMEM)


def tied(arrays, after):
    return pl.pallas_call(
        lambda *refs: None,
        out_shape=[jax.ShapeDtypeStruct(a.shape, a.dtype) for a in arrays],
        in_specs=[ANYWHERE] * (len(arrays) + len(after)),
        out_specs=[ANYWHERE] * len(arrays),
        input_output_aliases={k: k for k in range(len(arrays))},
        cost_estimate=pl.CostEstimate(flops=0, bytes_accessed=0, transcendentals=0),
    )(*[in_vmem(a) for a in arrays], *after)


def first_kernel(experts, tokens, routes, scale, gate_w, up_w, block, *refs):
    picked, (stack, held, sems) = refs[:4], refs[4:]
    pieces = sems.shape[2]
    rows = gate_w.shape[0] // pieces
    fetch, store = [], []
    for k in range(pieces):
        cut = pl.ds(k * rows, rows)
        for n, source in enumerate((gate_w, up_w)):
            fetch.append(pltpu.make_async_copy(source.at[cut], held.at[n, cut], sems.at[0, n, k]))
            store.append(pltpu.make_async_copy(held.at[n, cut], stack.at[n, cut], sems.at[1, n, k]))
    for copy in fetch:
        copy.start()
    count, width = tokens.shape
    lane = lax.broadcasted_iota(jnp.int32, (count, block.shape[1] - width), 1)
    expert, part = lax.rem(lane, experts), lax.div(lane, experts)
    weight = jnp.zeros(lane.shape, jnp.float32)
    routes, scale = routes[...].T, scale[...].T
    for r in range(routes.shape[1]):
        weight += jnp.where(routes[:, r : r + 1] == expert, scale[:, r : r + 1], 0.0)
    high = weight.astype(jnp.bfloat16).astype(jnp.float32)
    middle = (weight - high).astype(jnp.bfloat16).astype(jnp.float32)
    low = weight - high - middle
    marks = jnp.where(part == 0, high, jnp.where(part == 1, middle, jnp.where(part == 2, low, 0.0)))
    block[:, :width] = tokens[...]
    block[:, width:] = marks.astype(jnp.bfloat16)
    for arrived, leaving in zip(fetch, store):
        arrived.wait()
        leaving.start()
    choose(block, *picked)
    for copy in store:
        copy.wait()


def passing_kernel(*refs):
    for source, result in zip(refs, refs[len(refs) // 2 :]):
        result[...] = source[...]


def choose(held, own_map, other_map, own_rows, other_rows):
    node = lax.axis_index("node")
    count, cap = own_map.shape
    marks = held[:, held.shape[1] - 128 :].astype(jnp.float32)
    lane = lax.broadcasted_iota(jnp.int32, marks.shape, 1)
    earlier = lax.broadcasted_iota(jnp.int32, (count, count), 0) > lax.broadcasted_iota(jnp.int32, (count, count), 1)
    named = jnp.where(marks != 0, 1.0, 0.0)
    rank = jnp.dot(
        jnp.where(earlier, 1.0, 0.0).astype(jnp.bfloat16), named.astype(jnp.bfloat16), preferred_element_type=jnp.float32
    )
    place = jnp.where(named > 0, rank, -1.0)
    slot = lax.broadcasted_iota(jnp.int32, (count, cap), 1)
    for expert, one_hot, rows in ((node, own_map, own_rows), (node ^ 1, other_map, other_rows)):
        mine = jnp.sum(jnp.where(lane == expert, place, 0.0), axis=1, keepdims=True).astype(jnp.int32)
        chosen = jnp.where(mine == slot, 1.0, 0.0).astype(jnp.bfloat16)
        one_hot[...] = chosen
        rows[...] = lax.dot_general(
            chosen, held[...], (((0,), (0,)), ((), ())), preferred_element_type=jnp.float32
        ).astype(jnp.bfloat16)


def pick_kernel(users, *refs):
    blocks, (held, sem) = refs[: len(users)], refs[len(users) + 4 :]
    node = lax.axis_index("node")
    for block, places in zip(blocks, users):
        here = functools.reduce(jnp.logical_or, [lax.div(node, 2) == place for place in places])

        @pl.when(here)
        def _():
            copy = pltpu.make_async_copy(block, held, sem)
            copy.start()
            copy.wait()

    choose(held, *refs[len(users) : len(users) + 4])


def expert_kernel(experts, own, other, *refs):
    own_w, other_w, own_down, other_down, own_out, other_out, rows, hidden, total, gates, ups, downs, sems = refs
    cap, width = own_out.shape
    tiles, _, size = gates.shape
    each = tiles // 2
    halves = []
    for half, (stack, down) in enumerate(((own_w, own_down), (other_w, other_down))):
        queue = []
        for tile in range(half * each, half * each + each):
            part = pl.ds(tile % each * size, size)
            queue.append(pltpu.make_async_copy(stack.at[0, :, part], gates.at[tile], sems.at[tile, 0]))
            queue.append(pltpu.make_async_copy(stack.at[1, :, part], ups.at[tile], sems.at[tile, 1]))
        for tile in range(half * each, half * each + each):
            part = pl.ds(tile % each * size, size)
            queue.append(pltpu.make_async_copy(down.at[part], downs.at[tile], sems.at[tile, 2]))
        halves.append(queue)
    ahead = iter(halves[0] + halves[1])
    for _ in range(4):
        next(ahead).start()

    def arrived(copy):
        copy.wait()
        for following in ahead:
            following.start()
            break

    rows[:cap] = own[:, :width]
    rows[cap:] = other[:, :width]
    node = lax.axis_index("node")
    scales = []
    for marked in (own, other):
        marks = marked[:, width:].astype(jnp.float32)
        lane = lax.broadcasted_iota(jnp.int32, marks.shape, 1)
        mine = (lax.rem(lane, experts) == node) & (lane < 3 * experts)
        scales.append(jnp.sum(jnp.where(mine, marks, 0.0), axis=1, keepdims=True))
    step = 512 if width % 512 == 0 else width
    for half, queue in enumerate(halves):
        for k in range(each):
            tile = half * each + k
            arrived(queue[2 * k])
            gate = jnp.dot(rows[...], gates[tile], preferred_element_type=jnp.float32)
            arrived(queue[2 * k + 1])
            up = jnp.dot(rows[...], ups[tile], preferred_element_type=jnp.float32)
            hidden[tile] = (gate / (1.0 + jnp.exp(-gate)) * up).astype(jnp.bfloat16)
        for copy in queue[2 * each :]:
            arrived(copy)
        for first in range(0, width, step):
            cut = slice(first, first + step)
            out = jnp.zeros((2 * cap, step), jnp.float32) if half == 0 else total[:, cut]
            for tile in range(half * each, half * each + each):
                out += jnp.dot(hidden[tile], downs[tile, :, cut], preferred_element_type=jnp.float32)
            if half == 0:
                total[:, cut] = out
            else:
                own_out[:, cut] = (out[:cap] * scales[0]).astype(jnp.bfloat16)
                other_out[:, cut] = (out[cap:] * scales[1]).astype(jnp.bfloat16)


def spread_kernel(own_map, other_map, own_out, other_out, *refs):
    result = refs[-1]
    total = jnp.dot(own_map[...], own_out[...], preferred_element_type=jnp.float32)
    total += jnp.dot(other_map[...], other_out[...], preferred_element_type=jnp.float32)
    for extra in refs[:-1]:
        total += extra[...].astype(jnp.float32)
    result[...] = total.astype(jnp.bfloat16)


def sum_kernel(*refs):
    total = refs[0][...].astype(jnp.float32)
    for extra in refs[1:-1]:
        total += extra[...].astype(jnp.float32)
    refs[-1][...] = total.astype(jnp.bfloat16)


def on_device(tokens, routes, route_scale, w_gate, w_up, w_down):
    count, width = tokens.shape
    experts = lax.axis_size("node")
    places = experts // 2
    hidden = w_gate.shape[2]
    size = min(hidden, 256)
    cap = -(-(5 * count // experts) // 16) * 16
    wide = width + -(-3 * experts // 128) * 128
    hbm = functools.partial(pltpu.HBM, dtype=jnp.bfloat16)
    in_hbm = functools.partial(pltpu.with_memory_space_constraint, memory_space=pltpu.HBM)
    bf16 = functools.partial(jax.ShapeDtypeStruct, dtype=jnp.bfloat16)

    own = (w_gate[0], w_up[0], w_down[0])
    block, *picked, stack = call(
        functools.partial(first_kernel, experts),
        [
            bf16((count, wide)),
            bf16((count, cap)),
            bf16((count, cap)),
            bf16((cap, wide)),
            bf16((cap, wide)),
            hbm((2, width, hidden)),
        ],
        [*map(in_hbm, (tokens, routes.T, route_scale.T, own[0], own[1]))],
        (),
        [pltpu.VMEM((2, width, hidden), jnp.bfloat16), pltpu.SemaphoreType.DMA((2, 2, 4))],
        [IN_VMEM] * 3 + [ANYWHERE] * 2,
        out_specs=[IN_VMEM] * 5 + [ANYWHERE],
    )
    swap = functools.partial(lax.ppermute, axis_name="local", perm=[(0, 1), (1, 0)])
    weights = [in_hbm(stack), swap(stack), in_hbm(own[2]), swap(own[2])]

    def along(block, pairs):
        moves = [(2 * a + y, 2 * b + y) for a, b in pairs for y in range(2)]
        return lax.ppermute(block, "node", moves)

    def across(block):
        return lax.ppermute(block, "node", [(n, n ^ 1) for n in range(experts)])

    def pick(blocks, users, after=()):
        return call(
            functools.partial(pick_kernel, users),
            [bf16((count, cap)), bf16((count, cap)), bf16((cap, wide)), bf16((cap, wide))],
            blocks,
            after,
            [pltpu.VMEM((count, wide), jnp.bfloat16), pltpu.SemaphoreType.DMA],
            [ANYWHERE] * len(blocks),
        )

    def expert(own_rows, other_rows, after=()):
        tiles = 2 * hidden // size
        return call(
            functools.partial(expert_kernel, experts),
            [bf16((cap, width)), bf16((cap, width))],
            [own_rows, other_rows, *weights],
            after,
            [
                pltpu.VMEM((2 * cap, width), jnp.bfloat16),
                pltpu.VMEM((tiles, 2 * cap, size), jnp.bfloat16),
                pltpu.VMEM((2 * cap, width), jnp.float32),
                pltpu.VMEM((tiles, width, size), jnp.bfloat16),
                pltpu.VMEM((tiles, width, size), jnp.bfloat16),
                pltpu.VMEM((tiles, size, width), jnp.bfloat16),
                pltpu.SemaphoreType.DMA((tiles, 3)),
            ],
            [IN_VMEM] * 2 + [ANYWHERE] * 4,
            32,
        )

    def spread(maps, own_out, other_out, extras=(), after=()):
        return call(spread_kernel, [bf16((count, width))], [*maps, own_out, other_out, *extras], after)[0]

    plan = arrivals(places)
    held = {}

    last = []

    def ordered(function, *args, after=(), **options):
        out = function(*args, after=(*last, *after), **options)
        last[:] = [out[0] if isinstance(out, (list, tuple)) else out]
        return out

    picks, outs, returned = {}, {}, []

    def relay(step):
        for way in (1, -1):
            pairs = [
                (a, a + way)
                for a in range(places)
                if 0 <= a + way < places and 0 <= a - way * (step - 1) < places
            ]
            held[way, step] = along(held.get((way, step - 1), block), pairs)

    def do_pick(slot, after=()):
        keys = sorted({row[slot - 1] for row in plan})
        blocks = [held[key] for key in keys]
        users = [[place for place, row in enumerate(plan) if row[slot - 1] == key] for key in keys]
        *maps, own_rows, other_rows = ordered(pick, blocks, users, after=after)
        picks[slot] = maps, own_rows, across(other_rows)

    def do_expert(slot, after=()):
        own_out, other_out = ordered(expert, picks[slot][1], picks[slot][2], after=after)
        outs[slot] = own_out, across(other_out)

    def origin(place, slot):
        way, step = plan[place][slot - 1]
        return place - way * step

    hops = []
    for place in range(places):
        target = origin(place, places - 1)
        near = place + (1 if target > place else -1)
        if near != target and origin(near, places - 2) == target:
            hops.append((place, near))
    staying = {places - 1: [a for a, _ in hops], places - 2: [b for _, b in hops]}
    kept = {}

    def do_spread(slot, after=()):
        kept[slot] = done = ordered(spread, picks[slot][0], *outs[slot], after=after)
        home = [(a, origin(a, slot)) for a in range(places) if a not in staying.get(slot, ())]
        rounds = []
        while home:
            now = list({b: (a, b) for a, b in home}.values())
            home = [pair for pair in home if pair not in now]
            rounds.append(along(done, now))
        returned.append(rounds)

    def call_sum(blocks, after=(), cost=0):
        return call(sum_kernel, [bf16((count, width))], blocks, after, cost=cost)

    relay(1)
    picks[0] = picked[:2], picked[2], across(picked[3])
    held[1, 1], held[-1, 1] = tied([held[1, 1], held[-1, 1]], [picks[0][2]])
    relay(2)
    do_pick(1)
    do_expert(1)
    held[1, 2], held[-1, 2] = call(
        passing_kernel, [bf16((count, wide))] * 2, [held[1, 2], held[-1, 2]], [*last, picks[1][2]]
    )
    for step in range(3, places):
        relay(step)
    do_pick(2)
    do_spread(1)
    do_pick(3, after=[picks[2][2]])
    do_expert(2)
    for slot in range(3, places):
        do_expert(slot, after=returned[slot - 3])
        do_spread(slot - 1)
        if slot + 1 < places:
            do_pick(slot + 1)
    do_spread(places - 1)
    do_expert(0)
    near = returned.pop(places - 3)
    (summed,) = ordered(call_sum, [*returned.pop(0), *near] if places > 3 else near, cost=128 * MIB)
    (joined,) = ordered(call_sum, [kept[places - 2], along(kept[places - 1], hops)])
    returned.append([summed, along(joined, [(q, origin(q, places - 2)) for _, q in hops])])
    total = ordered(spread, picks[0][0], *outs[0])
    total = total.astype(jnp.float32)
    for block in sum(returned, []):
        total = total + block.astype(jnp.float32)
    return total.astype(jnp.bfloat16)


def solution(mesh):
    placed = (
        P(("groups", "node", "local"), None),
        P(("groups", "node", "local"), None),
        P(("groups", "node", "local"), None),
        P("node", None, "local"),
        P("node", None, "local"),
        P("node", "local", None),
    )
    return jax.shard_map(
        on_device,
        mesh=mesh,
        in_specs=placed,
        out_specs=P(("groups", "node", "local"), None),
        check_vma=False,
    )
```

```python
import functools

import jax
import jax.numpy as jnp
from jax import lax
from jax.experimental import pallas as pl
from jax.experimental.pallas import tpu as pltpu
from jax.sharding import PartitionSpec as P

ANYWHERE = pl.BlockSpec(memory_space=pl.ANY)
IN_VMEM = pl.BlockSpec(memory_space=pltpu.VMEM)
MIB = 1024 * 1024


def arrivals(places):
    plan = []
    for place in range(places):
        left = [(-1, step) for step in range(1, places - place)]
        right = [(1, step) for step in range(1, place + 1)]
        plan.append(left + right if place < places // 2 else right + left)
    return plan


def call(kernel, outs, ins, after=(), scratch=(), specs=None, vmem=16, out_specs=None, cost=0):
    body = kernel
    if after:
        first, last = len(ins), len(ins) + len(after)

        def body(*refs):
            kernel(*refs[:first], *refs[last:])

    specs = list(specs or [IN_VMEM] * len(ins)) + [ANYWHERE] * len(after)
    return pl.pallas_call(
        body,
        out_shape=outs,
        in_specs=specs,
        out_specs=out_specs or [IN_VMEM] * len(outs),
        scratch_shapes=scratch,
        compiler_params=pltpu.CompilerParams(vmem_limit_bytes=vmem * MIB),
        cost_estimate=pl.CostEstimate(flops=0, bytes_accessed=cost, transcendentals=0),
    )(*ins, *after)


def in_vmem(array):
    return pltpu.with_memory_space_constraint(array, pltpu.VMEM)


def tied(arrays, after):
    return pl.pallas_call(
        lambda *refs: None,
        out_shape=[jax.ShapeDtypeStruct(a.shape, a.dtype) for a in arrays],
        in_specs=[ANYWHERE] * (len(arrays) + len(after)),
        out_specs=[ANYWHERE] * len(arrays),
        input_output_aliases={k: k for k in range(len(arrays))},
        cost_estimate=pl.CostEstimate(flops=0, bytes_accessed=0, transcendentals=0),
    )(*[in_vmem(a) for a in arrays], *after)


def first_kernel(experts, tokens, routes, scale, gate_w, up_w, block, *refs):
    picked, (stack, held, route_held, scale_held, sems, own_sems) = refs[:4], refs[4:]
    pieces = sems.shape[2]
    count, width = tokens.shape
    ins = [
        pltpu.make_async_copy(routes, route_held, own_sems.at[0]),
        pltpu.make_async_copy(scale, scale_held, own_sems.at[1]),
        pltpu.make_async_copy(tokens, block.at[:, :width], own_sems.at[2]),
    ]
    for copy in ins:
        copy.start()
    rows = gate_w.shape[0] // pieces
    fetch, store = [], []
    for k in range(pieces):
        cut = pl.ds(k * rows, rows)
        for n, source in enumerate((gate_w, up_w)):
            fetch.append(pltpu.make_async_copy(source.at[cut], held.at[n, cut], sems.at[0, n, k]))
            store.append(pltpu.make_async_copy(held.at[n, cut], stack.at[n, cut], sems.at[1, n, k]))
    for copy in fetch:
        copy.start()
    for copy in ins[:2]:
        copy.wait()
    lane = lax.broadcasted_iota(jnp.int32, (count, block.shape[1] - width), 1)
    expert, part = lax.rem(lane, experts), lax.div(lane, experts)
    weight = jnp.zeros(lane.shape, jnp.float32)
    routes, scale = route_held[...].T, scale_held[...].T
    for r in range(routes.shape[1]):
        weight += jnp.where(routes[:, r : r + 1] == expert, scale[:, r : r + 1], 0.0)
    high = weight.astype(jnp.bfloat16).astype(jnp.float32)
    middle = (weight - high).astype(jnp.bfloat16).astype(jnp.float32)
    low = weight - high - middle
    marks = jnp.where(part == 0, high, jnp.where(part == 1, middle, jnp.where(part == 2, low, 0.0)))
    block[:, width:] = marks.astype(jnp.bfloat16)
    ins[2].wait()
    for arrived, leaving in zip(fetch, store):
        arrived.wait()
        leaving.start()
    choose(block, *picked)
    for copy in store:
        copy.wait()


def passing_kernel(*refs):
    for source, result in zip(refs, refs[len(refs) // 2 :]):
        result[...] = source[...]


def choose(held, own_map, other_map, own_rows, other_rows):
    node = lax.axis_index("node")
    count, cap = own_map.shape
    marks = held[:, held.shape[1] - 128 :].astype(jnp.float32)
    lane = lax.broadcasted_iota(jnp.int32, marks.shape, 1)
    earlier = lax.broadcasted_iota(jnp.int32, (count, count), 0) > lax.broadcasted_iota(jnp.int32, (count, count), 1)
    named = jnp.where(marks != 0, 1.0, 0.0)
    rank = jnp.dot(
        jnp.where(earlier, 1.0, 0.0).astype(jnp.bfloat16), named.astype(jnp.bfloat16), preferred_element_type=jnp.float32
    )
    place = jnp.where(named > 0, rank, -1.0)
    slot = lax.broadcasted_iota(jnp.int32, (count, cap), 1)
    for expert, one_hot, rows in ((node, own_map, own_rows), (node ^ 1, other_map, other_rows)):
        mine = jnp.sum(jnp.where(lane == expert, place, 0.0), axis=1, keepdims=True).astype(jnp.int32)
        chosen = jnp.where(mine == slot, 1.0, 0.0).astype(jnp.bfloat16)
        one_hot[...] = chosen
        rows[...] = lax.dot_general(
            chosen, held[...], (((0,), (0,)), ((), ())), preferred_element_type=jnp.float32
        ).astype(jnp.bfloat16)


def pick_kernel(users, *refs):
    blocks, (held, sem) = refs[: len(users)], refs[len(users) + 4 :]
    node = lax.axis_index("node")
    for block, places in zip(blocks, users):
        here = functools.reduce(jnp.logical_or, [lax.div(node, 2) == place for place in places])

        @pl.when(here)
        def _():
            copy = pltpu.make_async_copy(block, held, sem)
            copy.start()
            copy.wait()

    choose(held, *refs[len(users) : len(users) + 4])


def expert_kernel(experts, own, other, *refs):
    own_w, other_w, own_down, other_down, own_out, other_out, rows, hidden, gates, ups, downs, sems = refs
    cap, width = own_out.shape
    tiles, _, size = gates.shape
    each = tiles // 2
    queue = []
    for tile in range(tiles):
        stack, part = (own_w, other_w)[tile // each], pl.ds(tile % each * size, size)
        queue.append(pltpu.make_async_copy(stack.at[0, :, part], gates.at[tile], sems.at[tile, 0]))
        queue.append(pltpu.make_async_copy(stack.at[1, :, part], ups.at[tile], sems.at[tile, 1]))
    for half, down in enumerate((own_down, other_down)):
        queue.append(pltpu.make_async_copy(down, downs.at[half], sems.at[half, 2]))
    ahead = iter(queue[4:])
    for copy in queue[:4]:
        copy.start()

    def arrived(copy):
        copy.wait()
        for following in ahead:
            following.start()
            break

    rows[:cap] = own[:, :width]
    rows[cap:] = other[:, :width]
    for tile in range(tiles):
        arrived(queue[2 * tile])
        gate = jnp.dot(rows[...], gates[tile], preferred_element_type=jnp.float32)
        arrived(queue[2 * tile + 1])
        up = jnp.dot(rows[...], ups[tile], preferred_element_type=jnp.float32)
        hidden[:, tile * size : (tile + 1) * size] = (gate / (1.0 + jnp.exp(-gate)) * up).astype(jnp.bfloat16)
    arrived(queue[-2])
    arrived(queue[-1])
    node = lax.axis_index("node")
    scales = []
    for marked in (own, other):
        marks = marked[:, width:].astype(jnp.float32)
        lane = lax.broadcasted_iota(jnp.int32, marks.shape, 1)
        mine = (lax.rem(lane, experts) == node) & (lane < 3 * experts)
        scales.append(jnp.sum(jnp.where(mine, marks, 0.0), axis=1, keepdims=True))
    step = 512 if width % 512 == 0 else width
    for start in range(0, width, step):
        cut = slice(start, start + step)
        out = jnp.dot(hidden[:, : each * size], downs[0, :, cut], preferred_element_type=jnp.float32)
        out += jnp.dot(hidden[:, each * size :], downs[1, :, cut], preferred_element_type=jnp.float32)
        own_out[:, cut] = (out[:cap] * scales[0]).astype(jnp.bfloat16)
        other_out[:, cut] = (out[cap:] * scales[1]).astype(jnp.bfloat16)


def spread_kernel(own_map, other_map, own_out, other_out, *refs):
    result = refs[-1]
    total = jnp.dot(own_map[...], own_out[...], preferred_element_type=jnp.float32)
    total += jnp.dot(other_map[...], other_out[...], preferred_element_type=jnp.float32)
    for extra in refs[:-1]:
        total += extra[...].astype(jnp.float32)
    result[...] = total.astype(jnp.bfloat16)


def sum_kernel(*refs):
    total = refs[0][...].astype(jnp.float32)
    for extra in refs[1:-1]:
        total += extra[...].astype(jnp.float32)
    refs[-1][...] = total.astype(jnp.bfloat16)


def on_device(tokens, routes, route_scale, w_gate, w_up, w_down):
    count, width = tokens.shape
    experts = lax.axis_size("node")
    places = experts // 2
    hidden = w_gate.shape[2]
    size = min(hidden, 256)
    cap = -(-(5 * count // experts) // 16) * 16
    wide = width + -(-3 * experts // 128) * 128
    hbm = functools.partial(pltpu.HBM, dtype=jnp.bfloat16)
    in_hbm = functools.partial(pltpu.with_memory_space_constraint, memory_space=pltpu.HBM)
    bf16 = functools.partial(jax.ShapeDtypeStruct, dtype=jnp.bfloat16)

    own = (w_gate[0], w_up[0], w_down[0])
    block, *picked, stack = call(
        functools.partial(first_kernel, experts),
        [
            bf16((count, wide)),
            bf16((count, cap)),
            bf16((count, cap)),
            hbm((cap, wide)),
            bf16((cap, wide)),
            hbm((2, width, hidden)),
        ],
        [*map(in_hbm, (tokens, routes.T, route_scale.T, own[0], own[1]))],
        (),
        [
            pltpu.VMEM((2, width, hidden), jnp.bfloat16),
            pltpu.VMEM(routes.shape[::-1], routes.dtype),
            pltpu.VMEM(routes.shape[::-1], route_scale.dtype),
            pltpu.SemaphoreType.DMA((2, 2, 8)),
            pltpu.SemaphoreType.DMA((3,)),
        ],
        [ANYWHERE] * 5,
        out_specs=[IN_VMEM] * 5 + [ANYWHERE],
    )
    swap = functools.partial(lax.ppermute, axis_name="local", perm=[(0, 1), (1, 0)])
    weights = [in_hbm(stack), swap(stack), in_hbm(own[2]), swap(own[2])]

    def along(block, pairs):
        moves = [(2 * a + y, 2 * b + y) for a, b in pairs for y in range(2)]
        return lax.ppermute(block, "node", moves)

    def across(block):
        return lax.ppermute(block, "node", [(n, n ^ 1) for n in range(experts)])

    def pick(blocks, users, after=()):
        return call(
            functools.partial(pick_kernel, users),
            [bf16((count, cap)), bf16((count, cap)), bf16((cap, wide)), bf16((cap, wide))],
            blocks,
            after,
            [pltpu.VMEM((count, wide), jnp.bfloat16), pltpu.SemaphoreType.DMA],
            [ANYWHERE] * len(blocks),
        )

    def expert(own_rows, other_rows, after=()):
        tiles = 2 * hidden // size
        return call(
            functools.partial(expert_kernel, experts),
            [bf16((cap, width)), bf16((cap, width))],
            [own_rows, other_rows, *weights],
            after,
            [
                pltpu.VMEM((2 * cap, width), jnp.bfloat16),
                pltpu.VMEM((2 * cap, 2 * hidden), jnp.bfloat16),
                pltpu.VMEM((tiles, width, size), jnp.bfloat16),
                pltpu.VMEM((tiles, width, size), jnp.bfloat16),
                pltpu.VMEM((2, hidden, width), jnp.bfloat16),
                pltpu.SemaphoreType.DMA((tiles, 3)),
            ],
            [IN_VMEM] * 2 + [ANYWHERE] * 4,
            32,
            cost=64 * MIB,
        )

    def spread(maps, own_out, other_out, extras=(), after=(), cost=0):
        ins = [*maps, own_out, other_out, *extras]
        return call(spread_kernel, [bf16((count, width))], ins, after, cost=cost)[0]

    plan = arrivals(places)
    held = {}

    last = []

    def ordered(function, *args, after=(), **options):
        out = function(*args, after=(*last, *after), **options)
        last[:] = [out[0] if isinstance(out, (list, tuple)) else out]
        return out

    picks, outs, returned = {}, {}, []

    def relay(step):
        for way in (1, -1):
            pairs = [
                (a, a + way)
                for a in range(places)
                if 0 <= a + way < places and 0 <= a - way * (step - 1) < places
            ]
            held[way, step] = along(held.get((way, step - 1), block), pairs)

    def do_pick(slot, after=()):
        keys = sorted({row[slot - 1] for row in plan})
        blocks = [held[key] for key in keys]
        users = [[place for place, row in enumerate(plan) if row[slot - 1] == key] for key in keys]
        *maps, own_rows, other_rows = ordered(pick, blocks, users, after=after)
        picks[slot] = maps, own_rows, across(other_rows)

    def do_expert(slot, after=()):
        own_out, other_out = ordered(expert, picks[slot][1], picks[slot][2], after=after)
        outs[slot] = own_out, across(other_out)

    def origin(place, slot):
        way, step = plan[place][slot - 1]
        return place - way * step

    hops = []
    for place in range(places):
        target = origin(place, places - 1)
        near = place + (1 if target > place else -1)
        if near != target and origin(near, places - 2) == target:
            hops.append((place, near))
    staying = {places - 1: [a for a, _ in hops], places - 2: [b for _, b in hops]}
    kept = {}

    def do_spread(slot, after=()):
        kept[slot] = done = ordered(spread, picks[slot][0], *outs[slot], after=after)
        home = [(a, origin(a, slot)) for a in range(places) if a not in staying.get(slot, ())]
        rounds = []
        while home:
            now = list({b: (a, b) for a, b in home}.values())
            home = [pair for pair in home if pair not in now]
            rounds.append(along(done, now))
        returned.append(rounds)

    def call_sum(blocks, after=(), cost=0):
        return call(sum_kernel, [bf16((count, width))], blocks, after, cost=cost)

    relay(1)
    picks[0] = picked[:2], picked[2], across(picked[3])
    held[1, 1], held[-1, 1] = tied([held[1, 1], held[-1, 1]], [picks[0][2]])
    relay(2)
    do_pick(1)
    do_expert(1)
    held[1, 2], held[-1, 2] = call(
        passing_kernel, [bf16((count, wide))] * 2, [held[1, 2], held[-1, 2]], [*last, picks[1][2]]
    )
    for step in range(3, places):
        relay(step)
    do_pick(2)
    do_spread(1)
    do_pick(3)
    do_expert(2)
    for slot in range(3, places):
        do_expert(slot)
        do_spread(slot - 1, after=returned[slot - 3])
        if slot + 1 < places:
            do_pick(slot + 1)
    do_expert(0)
    do_spread(places - 1)
    near = returned.pop(places - 3)
    total = ordered(spread, picks[0][0], *outs[0], [*returned.pop(0), *near] if places > 3 else near, cost=128 * MIB)
    (joined,) = ordered(call_sum, [kept[places - 2], along(kept[places - 1], hops)])
    returned.append([along(joined, [(q, origin(q, places - 2)) for _, q in hops])])
    total = total.astype(jnp.float32)
    for block in sum(returned, []):
        total = total + block.astype(jnp.float32)
    return total.astype(jnp.bfloat16)


def solution(mesh):
    placed = (
        P(("groups", "node", "local"), None),
        P(("groups", "node", "local"), None),
        P(("groups", "node", "local"), None),
        P("node", None, "local"),
        P("node", None, "local"),
        P("node", "local", None),
    )
    return jax.shard_map(
        on_device,
        mesh=mesh,
        in_specs=placed,
        out_specs=P(("groups", "node", "local"), None),
        check_vma=False,
    )
```

```python
import functools

import jax
import jax.numpy as jnp
from jax import lax
from jax.experimental import pallas as pl
from jax.experimental.pallas import tpu as pltpu
from jax.sharding import PartitionSpec as P

ANYWHERE = pl.BlockSpec(memory_space=pl.ANY)
IN_VMEM = pl.BlockSpec(memory_space=pltpu.VMEM)
MIB = 1024 * 1024


def arrivals(places):
    plan = []
    for place in range(places):
        spare, row = [], []
        for step in range(1, places):
            here = [way for way in (1, -1) if 0 <= place - way * step < places]
            if len(here) == 2 and place % 2 == 0:
                here.reverse()
            spare += [(way, step) for way in here[1:]]
            row.append((here[0], step) if here else spare.pop(0))
        plan.append(row)
    return plan


def call(kernel, outs, ins, after=(), scratch=(), specs=None, vmem=16, out_specs=None, cost=0):
    body = kernel
    if after:
        first, last = len(ins), len(ins) + len(after)

        def body(*refs):
            kernel(*refs[:first], *refs[last:])

    specs = list(specs or [IN_VMEM] * len(ins)) + [ANYWHERE] * len(after)
    return pl.pallas_call(
        body,
        out_shape=outs,
        in_specs=specs,
        out_specs=out_specs or [IN_VMEM] * len(outs),
        scratch_shapes=scratch,
        compiler_params=pltpu.CompilerParams(vmem_limit_bytes=vmem * MIB),
        cost_estimate=pl.CostEstimate(flops=0, bytes_accessed=cost, transcendentals=0),
    )(*ins, *after)


def in_vmem(array):
    return pltpu.with_memory_space_constraint(array, pltpu.VMEM)


def tied(arrays, after):
    return pl.pallas_call(
        lambda *refs: None,
        out_shape=[jax.ShapeDtypeStruct(a.shape, a.dtype) for a in arrays],
        in_specs=[ANYWHERE] * (len(arrays) + len(after)),
        out_specs=[ANYWHERE] * len(arrays),
        input_output_aliases={k: k for k in range(len(arrays))},
        cost_estimate=pl.CostEstimate(flops=0, bytes_accessed=0, transcendentals=0),
    )(*[in_vmem(a) for a in arrays], *after)


def first_kernel(experts, tokens, routes, scale, gate_w, up_w, block, *refs):
    picked, (stack, held, route_held, scale_held, sems, own_sems) = refs[:4], refs[4:]
    pieces = sems.shape[2]
    count, width = tokens.shape
    ins = [
        pltpu.make_async_copy(routes, route_held, own_sems.at[0]),
        pltpu.make_async_copy(scale, scale_held, own_sems.at[1]),
        pltpu.make_async_copy(tokens, block.at[:, :width], own_sems.at[2]),
    ]
    for copy in ins:
        copy.start()
    rows = gate_w.shape[0] // pieces
    fetch, store = [], []
    for k in range(pieces):
        cut = pl.ds(k * rows, rows)
        for n, source in enumerate((gate_w, up_w)):
            fetch.append(pltpu.make_async_copy(source.at[cut], held.at[n, cut], sems.at[0, n, k]))
            store.append(pltpu.make_async_copy(held.at[n, cut], stack.at[n, cut], sems.at[1, n, k]))
    for copy in fetch:
        copy.start()
    for copy in ins[:2]:
        copy.wait()
    lane = lax.broadcasted_iota(jnp.int32, (count, block.shape[1] - width), 1)
    expert, part = lax.rem(lane, experts), lax.div(lane, experts)
    weight = jnp.zeros(lane.shape, jnp.float32)
    routes, scale = route_held[...].T, scale_held[...].T
    for r in range(routes.shape[1]):
        weight += jnp.where(routes[:, r : r + 1] == expert, scale[:, r : r + 1], 0.0)
    high = weight.astype(jnp.bfloat16).astype(jnp.float32)
    middle = (weight - high).astype(jnp.bfloat16).astype(jnp.float32)
    low = weight - high - middle
    marks = jnp.where(part == 0, high, jnp.where(part == 1, middle, jnp.where(part == 2, low, 0.0)))
    block[:, width:] = marks.astype(jnp.bfloat16)
    ins[2].wait()
    for arrived, leaving in zip(fetch, store):
        arrived.wait()
        leaving.start()
    choose(block, *picked)
    for copy in store:
        copy.wait()


def passing_kernel(*refs):
    for source, result in zip(refs, refs[len(refs) // 2 :]):
        result[...] = source[...]


def choose(held, own_map, other_map, own_rows, other_rows):
    node = lax.axis_index("node")
    count, cap = own_map.shape
    marks = held[:, held.shape[1] - 128 :].astype(jnp.float32)
    lane = lax.broadcasted_iota(jnp.int32, marks.shape, 1)
    earlier = lax.broadcasted_iota(jnp.int32, (count, count), 0) > lax.broadcasted_iota(jnp.int32, (count, count), 1)
    named = jnp.where(marks != 0, 1.0, 0.0)
    rank = jnp.dot(
        jnp.where(earlier, 1.0, 0.0).astype(jnp.bfloat16), named.astype(jnp.bfloat16), preferred_element_type=jnp.float32
    )
    place = jnp.where(named > 0, rank, -1.0)
    slot = lax.broadcasted_iota(jnp.int32, (count, cap), 1)
    for expert, one_hot, rows in ((node, own_map, own_rows), (node ^ 1, other_map, other_rows)):
        mine = jnp.sum(jnp.where(lane == expert, place, 0.0), axis=1, keepdims=True).astype(jnp.int32)
        chosen = jnp.where(mine == slot, 1.0, 0.0).astype(jnp.bfloat16)
        one_hot[...] = chosen
        rows[...] = lax.dot_general(
            chosen, held[...], (((0,), (0,)), ((), ())), preferred_element_type=jnp.float32
        ).astype(jnp.bfloat16)


def pick_kernel(users, *refs):
    blocks, (held, sem) = refs[: len(users)], refs[len(users) + 4 :]
    node = lax.axis_index("node")
    for block, places in zip(blocks, users):
        here = functools.reduce(jnp.logical_or, [lax.div(node, 2) == place for place in places])

        @pl.when(here)
        def _():
            copy = pltpu.make_async_copy(block, held, sem)
            copy.start()
            copy.wait()

    choose(held, *refs[len(users) : len(users) + 4])


def expert_kernel(experts, own, other, *refs):
    own_w, other_w, own_down, other_down, own_out, other_out, rows, hidden, gates, ups, downs, sems = refs
    cap, width = own_out.shape
    tiles, _, size = gates.shape
    each = tiles // 2
    queue = []
    for tile in range(tiles):
        stack, part = (own_w, other_w)[tile // each], pl.ds(tile % each * size, size)
        queue.append(pltpu.make_async_copy(stack.at[0, :, part], gates.at[tile], sems.at[tile, 0]))
        queue.append(pltpu.make_async_copy(stack.at[1, :, part], ups.at[tile], sems.at[tile, 1]))
    for half, down in enumerate((own_down, other_down)):
        queue.append(pltpu.make_async_copy(down, downs.at[half], sems.at[half, 2]))
    ahead = iter(queue[4:])
    for copy in queue[:4]:
        copy.start()

    def arrived(copy):
        copy.wait()
        for following in ahead:
            following.start()
            break

    rows[:cap] = own[:, :width]
    rows[cap:] = other[:, :width]
    for tile in range(tiles):
        arrived(queue[2 * tile])
        gate = jnp.dot(rows[...], gates[tile], preferred_element_type=jnp.float32)
        arrived(queue[2 * tile + 1])
        up = jnp.dot(rows[...], ups[tile], preferred_element_type=jnp.float32)
        hidden[:, tile * size : (tile + 1) * size] = (gate / (1.0 + jnp.exp(-gate)) * up).astype(jnp.bfloat16)
    arrived(queue[-2])
    arrived(queue[-1])
    node = lax.axis_index("node")
    scales = []
    for marked in (own, other):
        marks = marked[:, width:].astype(jnp.float32)
        lane = lax.broadcasted_iota(jnp.int32, marks.shape, 1)
        mine = (lax.rem(lane, experts) == node) & (lane < 3 * experts)
        scales.append(jnp.sum(jnp.where(mine, marks, 0.0), axis=1, keepdims=True))
    step = 512 if width % 512 == 0 else width
    for start in range(0, width, step):
        cut = slice(start, start + step)
        out = jnp.dot(hidden[:, : each * size], downs[0, :, cut], preferred_element_type=jnp.float32)
        out += jnp.dot(hidden[:, each * size :], downs[1, :, cut], preferred_element_type=jnp.float32)
        own_out[:, cut] = (out[:cap] * scales[0]).astype(jnp.bfloat16)
        other_out[:, cut] = (out[cap:] * scales[1]).astype(jnp.bfloat16)


def spread_kernel(own_map, other_map, own_out, other_out, *refs):
    result = refs[-1]
    total = jnp.dot(own_map[...], own_out[...], preferred_element_type=jnp.float32)
    total += jnp.dot(other_map[...], other_out[...], preferred_element_type=jnp.float32)
    for extra in refs[:-1]:
        total += extra[...].astype(jnp.float32)
    result[...] = total.astype(jnp.bfloat16)


def sum_kernel(*refs):
    total = refs[0][...].astype(jnp.float32)
    for extra in refs[1:-1]:
        total += extra[...].astype(jnp.float32)
    refs[-1][...] = total.astype(jnp.bfloat16)


def on_device(tokens, routes, route_scale, w_gate, w_up, w_down):
    count, width = tokens.shape
    experts = lax.axis_size("node")
    places = experts // 2
    hidden = w_gate.shape[2]
    size = min(hidden, 256)
    cap = -(-(5 * count // experts) // 16) * 16
    wide = width + -(-3 * experts // 128) * 128
    hbm = functools.partial(pltpu.HBM, dtype=jnp.bfloat16)
    in_hbm = functools.partial(pltpu.with_memory_space_constraint, memory_space=pltpu.HBM)
    bf16 = functools.partial(jax.ShapeDtypeStruct, dtype=jnp.bfloat16)

    own = (w_gate[0], w_up[0], w_down[0])
    block, *picked, stack = call(
        functools.partial(first_kernel, experts),
        [
            bf16((count, wide)),
            bf16((count, cap)),
            bf16((count, cap)),
            hbm((cap, wide)),
            bf16((cap, wide)),
            hbm((2, width, hidden)),
        ],
        [*map(in_hbm, (tokens, routes.T, route_scale.T, own[0], own[1]))],
        (),
        [
            pltpu.VMEM((2, width, hidden), jnp.bfloat16),
            pltpu.VMEM(routes.shape[::-1], routes.dtype),
            pltpu.VMEM(routes.shape[::-1], route_scale.dtype),
            pltpu.SemaphoreType.DMA((2, 2, 8)),
            pltpu.SemaphoreType.DMA((3,)),
        ],
        [ANYWHERE] * 5,
        out_specs=[IN_VMEM] * 5 + [ANYWHERE],
    )
    swap = functools.partial(lax.ppermute, axis_name="local", perm=[(0, 1), (1, 0)])
    weights = [in_hbm(stack), swap(stack), in_hbm(own[2]), swap(own[2])]

    def along(block, pairs):
        moves = [(2 * a + y, 2 * b + y) for a, b in pairs for y in range(2)]
        return lax.ppermute(block, "node", moves)

    def across(block):
        return lax.ppermute(block, "node", [(n, n ^ 1) for n in range(experts)])

    def pick(blocks, users, after=()):
        return call(
            functools.partial(pick_kernel, users),
            [bf16((count, cap)), bf16((count, cap)), bf16((cap, wide)), bf16((cap, wide))],
            blocks,
            after,
            [pltpu.VMEM((count, wide), jnp.bfloat16), pltpu.SemaphoreType.DMA],
            [ANYWHERE] * len(blocks),
        )

    def expert(own_rows, other_rows, after=()):
        tiles = 2 * hidden // size
        return call(
            functools.partial(expert_kernel, experts),
            [bf16((cap, width)), bf16((cap, width))],
            [own_rows, other_rows, *weights],
            after,
            [
                pltpu.VMEM((2 * cap, width), jnp.bfloat16),
                pltpu.VMEM((2 * cap, 2 * hidden), jnp.bfloat16),
                pltpu.VMEM((tiles, width, size), jnp.bfloat16),
                pltpu.VMEM((tiles, width, size), jnp.bfloat16),
                pltpu.VMEM((2, hidden, width), jnp.bfloat16),
                pltpu.SemaphoreType.DMA((tiles, 3)),
            ],
            [IN_VMEM] * 2 + [ANYWHERE] * 4,
            32,
            cost=64 * MIB,
        )

    def spread(maps, own_out, other_out, extras=(), after=(), cost=0):
        ins = [*maps, own_out, other_out, *extras]
        return call(spread_kernel, [bf16((count, width))], ins, after, cost=cost)[0]

    plan = arrivals(places)
    held = {}

    last = []

    def ordered(function, *args, after=(), **options):
        out = function(*args, after=(*last, *after), **options)
        last[:] = [out[0] if isinstance(out, (list, tuple)) else out]
        return out

    picks, outs, returned = {}, {}, []

    def relay(step):
        for way in (1, -1):
            pairs = [
                (a, a + way)
                for a in range(places)
                if 0 <= a + way < places and 0 <= a - way * (step - 1) < places
            ]
            held[way, step] = along(held.get((way, step - 1), block), pairs)

    def do_pick(slot, after=()):
        keys = sorted({row[slot - 1] for row in plan})
        blocks = [held[key] for key in keys]
        users = [[place for place, row in enumerate(plan) if row[slot - 1] == key] for key in keys]
        *maps, own_rows, other_rows = ordered(pick, blocks, users, after=after)
        picks[slot] = maps, own_rows, across(other_rows)

    def do_expert(slot, after=()):
        own_out, other_out = ordered(expert, picks[slot][1], picks[slot][2], after=after)
        outs[slot] = own_out, across(other_out)

    def origin(place, slot):
        way, step = plan[place][slot - 1]
        return place - way * step

    hops = []
    for place in range(places):
        target = origin(place, places - 1)
        near = place + (1 if target > place else -1)
        if near != target and origin(near, places - 2) == target:
            hops.append((place, near))
    staying = {places - 1: [a for a, _ in hops], places - 2: [b for _, b in hops]}
    kept = {}

    def do_spread(slot, after=()):
        kept[slot] = done = ordered(spread, picks[slot][0], *outs[slot], after=after)
        home = [(a, origin(a, slot)) for a in range(places) if a not in staying.get(slot, ())]
        rounds = []
        while home:
            now = list({b: (a, b) for a, b in home}.values())
            home = [pair for pair in home if pair not in now]
            rounds.append(along(done, now))
        returned.append(rounds)

    def call_sum(blocks, after=(), cost=0):
        return call(sum_kernel, [bf16((count, width))], blocks, after, cost=cost)

    relay(1)
    picks[0] = picked[:2], picked[2], across(picked[3])
    held[1, 1], held[-1, 1] = tied([held[1, 1], held[-1, 1]], [picks[0][2]])
    relay(2)
    do_pick(1)
    do_expert(1)
    held[1, 2], held[-1, 2] = call(
        passing_kernel, [bf16((count, wide))] * 2, [held[1, 2], held[-1, 2]], [*last, picks[1][2]]
    )
    for step in range(3, places):
        relay(step)
    do_pick(2)
    do_spread(1)
    do_pick(3)
    do_expert(2)
    for slot in range(3, places):
        do_expert(slot)
        do_spread(slot - 1, after=returned[slot - 3])
        if slot + 1 < places:
            do_pick(slot + 1)
    do_expert(0)
    do_spread(places - 1)
    near = returned.pop(places - 3)
    total = ordered(spread, picks[0][0], *outs[0], [*returned.pop(0), *near] if places > 3 else near, cost=128 * MIB)
    (joined,) = ordered(call_sum, [kept[places - 2], along(kept[places - 1], hops)])
    returned.append([along(joined, [(q, origin(q, places - 2)) for _, q in hops])])
    total = total.astype(jnp.float32)
    for block in sum(returned, []):
        total = total + block.astype(jnp.float32)
    return total.astype(jnp.bfloat16)


def solution(mesh):
    placed = (
        P(("groups", "node", "local"), None),
        P(("groups", "node", "local"), None),
        P(("groups", "node", "local"), None),
        P("node", None, "local"),
        P("node", None, "local"),
        P("node", "local", None),
    )
    return jax.shard_map(
        on_device,
        mesh=mesh,
        in_specs=placed,
        out_specs=P(("groups", "node", "local"), None),
        check_vma=False,
    )
```

```python
import functools

import jax
import jax.numpy as jnp
from jax import lax
from jax.experimental import pallas as pl
from jax.experimental.pallas import tpu as pltpu
from jax.sharding import PartitionSpec as P

ANYWHERE = pl.BlockSpec(memory_space=pl.ANY)
IN_VMEM = pl.BlockSpec(memory_space=pltpu.VMEM)
MIB = 1024 * 1024


def arrivals(places):
    plan = []
    for place in range(places):
        left = [(-1, step) for step in range(1, places - place)]
        right = [(1, step) for step in range(1, place + 1)]
        plan.append(left + right if place < places // 2 else right + left)
    return plan


def call(kernel, outs, ins, after=(), scratch=(), specs=None, vmem=16, out_specs=None, cost=0):
    body = kernel
    if after:
        first, last = len(ins), len(ins) + len(after)

        def body(*refs):
            kernel(*refs[:first], *refs[last:])

    specs = list(specs or [IN_VMEM] * len(ins)) + [ANYWHERE] * len(after)
    return pl.pallas_call(
        body,
        out_shape=outs,
        in_specs=specs,
        out_specs=out_specs or [IN_VMEM] * len(outs),
        scratch_shapes=scratch,
        compiler_params=pltpu.CompilerParams(vmem_limit_bytes=vmem * MIB),
        cost_estimate=pl.CostEstimate(flops=0, bytes_accessed=cost, transcendentals=0),
    )(*ins, *after)


def in_vmem(array):
    return pltpu.with_memory_space_constraint(array, pltpu.VMEM)


def tied(arrays, after):
    return pl.pallas_call(
        lambda *refs: None,
        out_shape=[jax.ShapeDtypeStruct(a.shape, a.dtype) for a in arrays],
        in_specs=[ANYWHERE] * (len(arrays) + len(after)),
        out_specs=[ANYWHERE] * len(arrays),
        input_output_aliases={k: k for k in range(len(arrays))},
        cost_estimate=pl.CostEstimate(flops=0, bytes_accessed=0, transcendentals=0),
    )(*[in_vmem(a) for a in arrays], *after)


def first_kernel(experts, tokens, routes, scale, block, *refs):
    picked, (route_held, scale_held, sems) = refs[:4], refs[4:]
    count, width = tokens.shape
    ins = [
        pltpu.make_async_copy(routes, route_held, sems.at[0]),
        pltpu.make_async_copy(scale, scale_held, sems.at[1]),
        pltpu.make_async_copy(tokens, block.at[:, :width], sems.at[2]),
    ]
    for copy in ins:
        copy.start()
    for copy in ins[:2]:
        copy.wait()
    lane = lax.broadcasted_iota(jnp.int32, (count, block.shape[1] - width), 1)
    expert, part = lax.rem(lane, experts), lax.div(lane, experts)
    weight = jnp.zeros(lane.shape, jnp.float32)
    routes, scale = route_held[...].T, scale_held[...].T
    for r in range(routes.shape[1]):
        weight += jnp.where(routes[:, r : r + 1] == expert, scale[:, r : r + 1], 0.0)
    high = weight.astype(jnp.bfloat16).astype(jnp.float32)
    middle = (weight - high).astype(jnp.bfloat16).astype(jnp.float32)
    low = weight - high - middle
    marks = jnp.where(part == 0, high, jnp.where(part == 1, middle, jnp.where(part == 2, low, 0.0)))
    block[:, width:] = marks.astype(jnp.bfloat16)
    ins[2].wait()
    choose(block, *picked)


def passing_kernel(*refs):
    for source, result in zip(refs, refs[len(refs) // 2 :]):
        result[...] = source[...]


def choose(held, own_map, other_map, own_rows, other_rows):
    node = lax.axis_index("node")
    count, cap = own_map.shape
    marks = held[:, held.shape[1] - 128 :].astype(jnp.float32)
    lane = lax.broadcasted_iota(jnp.int32, marks.shape, 1)
    earlier = lax.broadcasted_iota(jnp.int32, (count, count), 0) > lax.broadcasted_iota(jnp.int32, (count, count), 1)
    named = jnp.where(marks != 0, 1.0, 0.0)
    rank = jnp.dot(
        jnp.where(earlier, 1.0, 0.0).astype(jnp.bfloat16), named.astype(jnp.bfloat16), preferred_element_type=jnp.float32
    )
    place = jnp.where(named > 0, rank, -1.0)
    slot = lax.broadcasted_iota(jnp.int32, (count, cap), 1)
    for expert, one_hot, rows in ((node, own_map, own_rows), (node ^ 1, other_map, other_rows)):
        mine = jnp.sum(jnp.where(lane == expert, place, 0.0), axis=1, keepdims=True).astype(jnp.int32)
        chosen = jnp.where(mine == slot, 1.0, 0.0).astype(jnp.bfloat16)
        one_hot[...] = chosen
        rows[...] = lax.dot_general(
            chosen, held[...], (((0,), (0,)), ((), ())), preferred_element_type=jnp.float32
        ).astype(jnp.bfloat16)


def pick_kernel(users, *refs):
    blocks, (held, sem) = refs[: len(users)], refs[len(users) + 4 :]
    node = lax.axis_index("node")
    for block, places in zip(blocks, users):
        here = functools.reduce(jnp.logical_or, [lax.div(node, 2) == place for place in places])

        @pl.when(here)
        def _():
            copy = pltpu.make_async_copy(block, held, sem)
            copy.start()
            copy.wait()

    choose(held, *refs[len(users) : len(users) + 4])


def expert_kernel(experts, own, other, *refs):
    weights, (own_out, other_out, rows, hidden, gates, ups, downs, sems) = refs[:6], refs[6:]
    cap, width = own_out.shape
    tiles, _, size = gates.shape
    each = tiles // 2
    queue = []
    for tile in range(tiles):
        part = pl.ds(tile % each * size, size)
        gate_w, up_w = weights[tile // each * 3 : tile // each * 3 + 2]
        queue.append(pltpu.make_async_copy(gate_w.at[:, part], gates.at[tile], sems.at[tile, 0]))
        queue.append(pltpu.make_async_copy(up_w.at[:, part], ups.at[tile], sems.at[tile, 1]))
    for half, down in enumerate(weights[2::3]):
        queue.append(pltpu.make_async_copy(down, downs.at[half], sems.at[half, 2]))
    ahead = iter(queue[4:])
    for copy in queue[:4]:
        copy.start()

    def arrived(copy):
        copy.wait()
        for following in ahead:
            following.start()
            break

    rows[:cap] = own[:, :width]
    rows[cap:] = other[:, :width]
    for tile in range(tiles):
        arrived(queue[2 * tile])
        gate = jnp.dot(rows[...], gates[tile], preferred_element_type=jnp.float32)
        arrived(queue[2 * tile + 1])
        up = jnp.dot(rows[...], ups[tile], preferred_element_type=jnp.float32)
        hidden[:, tile * size : (tile + 1) * size] = (gate / (1.0 + jnp.exp(-gate)) * up).astype(jnp.bfloat16)
    arrived(queue[-2])
    arrived(queue[-1])
    node = lax.axis_index("node")
    scales = []
    for marked in (own, other):
        marks = marked[:, width:].astype(jnp.float32)
        lane = lax.broadcasted_iota(jnp.int32, marks.shape, 1)
        mine = (lax.rem(lane, experts) == node) & (lane < 3 * experts)
        scales.append(jnp.sum(jnp.where(mine, marks, 0.0), axis=1, keepdims=True))
    step = 512 if width % 512 == 0 else width
    for start in range(0, width, step):
        cut = slice(start, start + step)
        out = jnp.dot(hidden[:, : each * size], downs[0, :, cut], preferred_element_type=jnp.float32)
        out += jnp.dot(hidden[:, each * size :], downs[1, :, cut], preferred_element_type=jnp.float32)
        own_out[:, cut] = (out[:cap] * scales[0]).astype(jnp.bfloat16)
        other_out[:, cut] = (out[cap:] * scales[1]).astype(jnp.bfloat16)


def spread_kernel(own_map, other_map, own_out, other_out, *refs):
    result = refs[-1]
    total = jnp.dot(own_map[...], own_out[...], preferred_element_type=jnp.float32)
    total += jnp.dot(other_map[...], other_out[...], preferred_element_type=jnp.float32)
    for extra in refs[:-1]:
        total += extra[...].astype(jnp.float32)
    result[...] = total.astype(jnp.bfloat16)


def join_kernel(index, whole, half, result):
    size = half.shape[1]
    total = whole[:, index * size : (index + 1) * size].astype(jnp.float32) + half[...].astype(jnp.float32)
    result[...] = total.astype(jnp.bfloat16)


def halves_kernel(*refs):
    spread_kernel(*refs[:-2])
    size = refs[-1].shape[1]
    refs[-2][...] = refs[-3][:, :size]
    refs[-1][...] = refs[-3][:, size:]


def finish_kernel(*refs):
    *whole, low, high, result = refs
    size = low.shape[1]
    for half, first in ((low, 0), (high, size)):
        total = half[...].astype(jnp.float32)
        for extra in whole:
            total += extra[:, first : first + size].astype(jnp.float32)
        result[:, first : first + size] = total.astype(jnp.bfloat16)


def on_device(tokens, routes, route_scale, w_gate, w_up, w_down):
    count, width = tokens.shape
    experts = lax.axis_size("node")
    places = experts // 2
    hidden = w_gate.shape[2]
    size = min(hidden, 256)
    cap = -(-(5 * count // experts) // 16) * 16
    wide = width + -(-3 * experts // 128) * 128
    hbm = functools.partial(pltpu.HBM, dtype=jnp.bfloat16)
    in_hbm = functools.partial(pltpu.with_memory_space_constraint, memory_space=pltpu.HBM)
    bf16 = functools.partial(jax.ShapeDtypeStruct, dtype=jnp.bfloat16)

    own = (w_gate[0], w_up[0], w_down[0])
    block, *picked = call(
        functools.partial(first_kernel, experts),
        [bf16((count, wide)), bf16((count, cap)), bf16((count, cap)), hbm((cap, wide)), bf16((cap, wide))],
        [*map(in_hbm, (tokens, routes.T, route_scale.T))],
        (),
        [
            pltpu.VMEM(routes.shape[::-1], routes.dtype),
            pltpu.VMEM(routes.shape[::-1], route_scale.dtype),
            pltpu.SemaphoreType.DMA((3,)),
        ],
        [ANYWHERE] * 3,
    )
    swap = functools.partial(lax.ppermute, axis_name="local", perm=[(0, 1), (1, 0)])
    weights = [in_hbm(w) for w in (*own, *map(swap, own))]

    def along(block, pairs):
        moves = [(2 * a + y, 2 * b + y) for a, b in pairs for y in range(2)]
        return lax.ppermute(block, "node", moves)

    def across(block):
        return lax.ppermute(block, "node", [(n, n ^ 1) for n in range(experts)])

    def pick(blocks, users, after=(), cost=0):
        return call(
            functools.partial(pick_kernel, users),
            [bf16((count, cap)), bf16((count, cap)), bf16((cap, wide)), bf16((cap, wide))],
            blocks,
            after,
            [pltpu.VMEM((count, wide), jnp.bfloat16), pltpu.SemaphoreType.DMA],
            [ANYWHERE] * len(blocks),
            cost=cost,
        )

    def expert(own_rows, other_rows, after=(), cost=0):
        tiles = 2 * hidden // size
        return call(
            functools.partial(expert_kernel, experts),
            [bf16((cap, width)), bf16((cap, width))],
            [own_rows, other_rows, *weights],
            after,
            [
                pltpu.VMEM((2 * cap, width), jnp.bfloat16),
                pltpu.VMEM((2 * cap, 2 * hidden), jnp.bfloat16),
                pltpu.VMEM((tiles, width, size), jnp.bfloat16),
                pltpu.VMEM((tiles, width, size), jnp.bfloat16),
                pltpu.VMEM((2, hidden, width), jnp.bfloat16),
                pltpu.SemaphoreType.DMA((tiles, 3)),
            ],
            [IN_VMEM] * 2 + [ANYWHERE] * 6,
            32,
            cost=cost,
        )

    def spread(maps, own_out, other_out, extras=(), after=(), cost=0):
        ins = [*maps, own_out, other_out, *extras]
        return call(spread_kernel, [bf16((count, width))], ins, after, cost=cost)[0]

    plan = arrivals(places)
    held = {}

    last = []

    def ordered(function, *args, after=(), **options):
        out = function(*args, after=(*last, *after), **options)
        last[:] = [out[0] if isinstance(out, (list, tuple)) else out]
        return out

    picks, outs, returned = {}, {}, []

    def relay(step):
        for way in (1, -1):
            pairs = [
                (a, a + way)
                for a in range(places)
                if 0 <= a + way < places and 0 <= a - way * (step - 1) < places
            ]
            held[way, step] = along(held.get((way, step - 1), block), pairs)

    def do_pick(slot, after=(), cost=0):
        keys = sorted({row[slot - 1] for row in plan})
        blocks = [held[key] for key in keys]
        users = [[place for place, row in enumerate(plan) if row[slot - 1] == key] for key in keys]
        *maps, own_rows, other_rows = ordered(pick, blocks, users, after=after, cost=cost)
        picks[slot] = maps, own_rows, across(other_rows)

    def do_expert(slot, after=(), cost=0):
        own_out, other_out = ordered(expert, picks[slot][1], picks[slot][2], after=after, cost=cost)
        outs[slot] = own_out, across(other_out)

    def origin(place, slot):
        way, step = plan[place][slot - 1]
        return place - way * step

    hops = []
    for place in range(places):
        target = origin(place, places - 1)
        near = place + (1 if target > place else -1)
        if near != target and origin(near, places - 2) == target:
            hops.append((place, near))
    staying = {places - 1: [a for a, _ in hops], places - 2: [b for _, b in hops]}
    kept, halves = {}, []

    def spread_halves(maps, own_out, other_out, after=()):
        outs = [bf16((count, width)), bf16((count, width // 2)), bf16((count, width // 2))]
        return call(halves_kernel, outs, [*maps, own_out, other_out], after)

    def do_spread(slot, after=()):
        done, *halves[:] = ordered(spread_halves, picks[slot][0], *outs[slot], after=after)
        kept[slot] = done
        home = [(a, origin(a, slot)) for a in range(places) if a not in staying.get(slot, ())]
        rounds = []
        while home:
            now = list({b: (a, b) for a, b in home}.values())
            home = [pair for pair in home if pair not in now]
            rounds.append(along(done, now))
        returned.append(rounds)

    def join(whole, half, index, after=()):
        return call(functools.partial(join_kernel, index), [bf16(half.shape)], [whole, half], after)[0]

    def finish(whole, parts):
        while len(whole) > 8:
            summed = sum(array.astype(jnp.float32) for array in whole[:8])
            whole = [summed.astype(jnp.bfloat16), *whole[8:]]
        return call(finish_kernel, [bf16((count, width))], [*whole, *parts])[0]

    relay(1)
    relay(2)
    do_pick(1, after=weights[3:])
    picks[0] = picked[:2], picked[2], across(picked[3])
    do_expert(1, cost=64 * MIB)
    held[1, 2], held[-1, 2] = call(
        passing_kernel, [bf16((count, wide))] * 2, [held[1, 2], held[-1, 2]], [*last, picks[1][2], picks[0][2]]
    )
    for step in range(3, places):
        relay(step)
    do_pick(2)
    do_spread(1)
    do_pick(3)
    do_expert(2)
    for slot in range(3, places):
        do_expert(slot)
        do_spread(slot - 1, after=returned[slot - 3])
        if slot + 1 < places:
            do_pick(slot + 1)
    do_expert(0)
    do_spread(places - 1)
    near = returned.pop(places - 3)
    total = ordered(spread, picks[0][0], *outs[0], [*returned.pop(0), *near] if places > 3 else near, cost=128 * MIB)
    homes = [(q, origin(q, places - 2)) for _, q in hops]
    parts = []
    for arrived in [along(half, hops) for half in halves]:
        parts.append(along(ordered(join, kept[places - 2], arrived, len(parts)), homes))
    return finish([total, *sum(returned, [])], parts)


def solution(mesh):
    placed = (
        P(("groups", "node", "local"), None),
        P(("groups", "node", "local"), None),
        P(("groups", "node", "local"), None),
        P("node", None, "local"),
        P("node", None, "local"),
        P("node", "local", None),
    )
    return jax.shard_map(
        on_device,
        mesh=mesh,
        in_specs=placed,
        out_specs=P(("groups", "node", "local"), None),
        check_vma=False,
    )
```

```python
import functools

import jax
import jax.numpy as jnp
from jax import lax
from jax.experimental import pallas as pl
from jax.experimental.pallas import tpu as pltpu
from jax.sharding import PartitionSpec as P

ANYWHERE = pl.BlockSpec(memory_space=pl.ANY)
IN_VMEM = pl.BlockSpec(memory_space=pltpu.VMEM)
MIB = 1024 * 1024


def arrivals(places):
    plan = []
    for place in range(places):
        left = [(-1, step) for step in range(1, places - place)]
        right = [(1, step) for step in range(1, place + 1)]
        plan.append(left + right if place < places // 2 else right + left)
    return plan


def call(kernel, outs, ins, after=(), scratch=(), specs=None, vmem=16, out_specs=None, cost=0):
    body = kernel
    if after:
        first, last = len(ins), len(ins) + len(after)

        def body(*refs):
            kernel(*refs[:first], *refs[last:])

    specs = list(specs or [IN_VMEM] * len(ins)) + [ANYWHERE] * len(after)
    return pl.pallas_call(
        body,
        out_shape=outs,
        in_specs=specs,
        out_specs=out_specs or [IN_VMEM] * len(outs),
        scratch_shapes=scratch,
        compiler_params=pltpu.CompilerParams(vmem_limit_bytes=vmem * MIB),
        cost_estimate=pl.CostEstimate(flops=0, bytes_accessed=cost, transcendentals=0),
    )(*ins, *after)


def in_vmem(array):
    return pltpu.with_memory_space_constraint(array, pltpu.VMEM)


def tied(arrays, after):
    return pl.pallas_call(
        lambda *refs: None,
        out_shape=[jax.ShapeDtypeStruct(a.shape, a.dtype) for a in arrays],
        in_specs=[ANYWHERE] * (len(arrays) + len(after)),
        out_specs=[ANYWHERE] * len(arrays),
        input_output_aliases={k: k for k in range(len(arrays))},
        cost_estimate=pl.CostEstimate(flops=0, bytes_accessed=0, transcendentals=0),
    )(*[in_vmem(a) for a in arrays], *after)


def first_kernel(experts, tokens, routes, scale, block, *refs):
    picked, (route_held, scale_held, sems) = refs[:4], refs[4:]
    count, width = tokens.shape
    ins = [
        pltpu.make_async_copy(routes, route_held, sems.at[0]),
        pltpu.make_async_copy(scale, scale_held, sems.at[1]),
        pltpu.make_async_copy(tokens, block.at[:, :width], sems.at[2]),
    ]
    for copy in ins:
        copy.start()
    for copy in ins[:2]:
        copy.wait()
    lane = lax.broadcasted_iota(jnp.int32, (count, block.shape[1] - width), 1)
    expert, part = lax.rem(lane, experts), lax.div(lane, experts)
    weight = jnp.zeros(lane.shape, jnp.float32)
    routes, scale = route_held[...].T, scale_held[...].T
    for r in range(routes.shape[1]):
        weight += jnp.where(routes[:, r : r + 1] == expert, scale[:, r : r + 1], 0.0)
    high = weight.astype(jnp.bfloat16).astype(jnp.float32)
    middle = (weight - high).astype(jnp.bfloat16).astype(jnp.float32)
    low = weight - high - middle
    marks = jnp.where(part == 0, high, jnp.where(part == 1, middle, jnp.where(part == 2, low, 0.0)))
    block[:, width:] = marks.astype(jnp.bfloat16)
    ins[2].wait()
    choose(block, *picked)


def passing_kernel(*refs):
    for source, result in zip(refs, refs[len(refs) // 2 :]):
        result[...] = source[...]


def choose(held, own_map, other_map, own_rows, other_rows):
    node = lax.axis_index("node")
    count, cap = own_map.shape
    marks = held[:, held.shape[1] - 128 :].astype(jnp.float32)
    lane = lax.broadcasted_iota(jnp.int32, marks.shape, 1)
    earlier = lax.broadcasted_iota(jnp.int32, (count, count), 0) > lax.broadcasted_iota(jnp.int32, (count, count), 1)
    named = jnp.where(marks != 0, 1.0, 0.0)
    rank = jnp.dot(
        jnp.where(earlier, 1.0, 0.0).astype(jnp.bfloat16), named.astype(jnp.bfloat16), preferred_element_type=jnp.float32
    )
    place = jnp.where(named > 0, rank, -1.0)
    slot = lax.broadcasted_iota(jnp.int32, (count, cap), 1)
    for expert, one_hot, rows in ((node, own_map, own_rows), (node ^ 1, other_map, other_rows)):
        mine = jnp.sum(jnp.where(lane == expert, place, 0.0), axis=1, keepdims=True).astype(jnp.int32)
        chosen = jnp.where(mine == slot, 1.0, 0.0).astype(jnp.bfloat16)
        one_hot[...] = chosen
        rows[...] = lax.dot_general(
            chosen, held[...], (((0,), (0,)), ((), ())), preferred_element_type=jnp.float32
        ).astype(jnp.bfloat16)


def pick_kernel(users, *refs):
    blocks, (held, sem) = refs[: len(users)], refs[len(users) + 4 :]
    node = lax.axis_index("node")
    for block, places in zip(blocks, users):
        here = functools.reduce(jnp.logical_or, [lax.div(node, 2) == place for place in places])

        @pl.when(here)
        def _():
            copy = pltpu.make_async_copy(block, held, sem)
            copy.start()
            copy.wait()

    choose(held, *refs[len(users) : len(users) + 4])


def expert_kernel(experts, own, other, *refs):
    weights, (own_out, other_out, rows, hidden, gates, ups, downs, sems) = refs[:6], refs[6:]
    cap, width = own_out.shape
    tiles, _, size = gates.shape
    each = tiles // 2
    queue = []
    for tile in range(tiles):
        part = pl.ds(tile % each * size, size)
        gate_w, up_w = weights[tile // each * 3 : tile // each * 3 + 2]
        queue.append(pltpu.make_async_copy(gate_w.at[:, part], gates.at[tile], sems.at[tile, 0]))
        queue.append(pltpu.make_async_copy(up_w.at[:, part], ups.at[tile], sems.at[tile, 1]))
    for half, down in enumerate(weights[2::3]):
        queue.append(pltpu.make_async_copy(down, downs.at[half], sems.at[half, 2]))
    ahead = iter(queue[4:])
    for copy in queue[:4]:
        copy.start()

    def arrived(copy):
        copy.wait()
        for following in ahead:
            following.start()
            break

    rows[:cap] = own[:, :width]
    rows[cap:] = other[:, :width]
    for tile in range(tiles):
        arrived(queue[2 * tile])
        gate = jnp.dot(rows[...], gates[tile], preferred_element_type=jnp.float32)
        arrived(queue[2 * tile + 1])
        up = jnp.dot(rows[...], ups[tile], preferred_element_type=jnp.float32)
        hidden[:, tile * size : (tile + 1) * size] = (gate / (1.0 + jnp.exp(-gate)) * up).astype(jnp.bfloat16)
    arrived(queue[-2])
    arrived(queue[-1])
    node = lax.axis_index("node")
    scales = []
    for marked in (own, other):
        marks = marked[:, width:].astype(jnp.float32)
        lane = lax.broadcasted_iota(jnp.int32, marks.shape, 1)
        mine = (lax.rem(lane, experts) == node) & (lane < 3 * experts)
        scales.append(jnp.sum(jnp.where(mine, marks, 0.0), axis=1, keepdims=True))
    step = 512 if width % 512 == 0 else width
    for start in range(0, width, step):
        cut = slice(start, start + step)
        out = jnp.dot(hidden[:, : each * size], downs[0, :, cut], preferred_element_type=jnp.float32)
        out += jnp.dot(hidden[:, each * size :], downs[1, :, cut], preferred_element_type=jnp.float32)
        own_out[:, cut] = (out[:cap] * scales[0]).astype(jnp.bfloat16)
        other_out[:, cut] = (out[cap:] * scales[1]).astype(jnp.bfloat16)


def spread_kernel(own_map, other_map, own_out, other_out, *refs):
    result = refs[-1]
    total = jnp.dot(own_map[...], own_out[...], preferred_element_type=jnp.float32)
    total += jnp.dot(other_map[...], other_out[...], preferred_element_type=jnp.float32)
    for extra in refs[:-1]:
        total += extra[...].astype(jnp.float32)
    result[...] = total.astype(jnp.bfloat16)


def sum_kernel(*refs):
    total = refs[0][...].astype(jnp.float32)
    for extra in refs[1:-1]:
        total += extra[...].astype(jnp.float32)
    refs[-1][...] = total.astype(jnp.bfloat16)


def join_kernel(index, whole, half, result):
    size = half.shape[1]
    total = whole[:, index * size : (index + 1) * size].astype(jnp.float32) + half[...].astype(jnp.float32)
    result[...] = total.astype(jnp.bfloat16)


def halves_kernel(*refs):
    spread_kernel(*refs[:-2])
    size = refs[-1].shape[1]
    refs[-2][...] = refs[-3][:, :size]
    refs[-1][...] = refs[-3][:, size:]


def low_kernel(*refs):
    *whole, low, result = refs
    size = low.shape[1]
    total = low[...].astype(jnp.float32)
    for extra in whole:
        total += extra[:, :size].astype(jnp.float32)
    result[...] = total.astype(jnp.bfloat16)


def finish_kernel(*refs):
    *whole, low, high, result = refs
    size = low.shape[1]
    total = high[...].astype(jnp.float32)
    for extra in whole:
        total += extra[:, size:].astype(jnp.float32)
    result[:, :size] = low[...]
    result[:, size:] = total.astype(jnp.bfloat16)


def on_device(tokens, routes, route_scale, w_gate, w_up, w_down):
    count, width = tokens.shape
    experts = lax.axis_size("node")
    places = experts // 2
    hidden = w_gate.shape[2]
    size = min(hidden, 256)
    cap = -(-(5 * count // experts) // 16) * 16
    wide = width + -(-3 * experts // 128) * 128
    hbm = functools.partial(pltpu.HBM, dtype=jnp.bfloat16)
    in_hbm = functools.partial(pltpu.with_memory_space_constraint, memory_space=pltpu.HBM)
    bf16 = functools.partial(jax.ShapeDtypeStruct, dtype=jnp.bfloat16)

    own = (w_gate[0], w_up[0], w_down[0])
    block, *picked = call(
        functools.partial(first_kernel, experts),
        [bf16((count, wide)), bf16((count, cap)), bf16((count, cap)), hbm((cap, wide)), hbm((cap, wide))],
        [*map(in_hbm, (tokens, routes.T, route_scale.T))],
        (),
        [
            pltpu.VMEM(routes.shape[::-1], routes.dtype),
            pltpu.VMEM(routes.shape[::-1], route_scale.dtype),
            pltpu.SemaphoreType.DMA((3,)),
        ],
        [ANYWHERE] * 3,
    )
    swap = functools.partial(lax.ppermute, axis_name="local", perm=[(0, 1), (1, 0)])
    weights = [*map(in_hbm, own), *map(swap, own)]

    def along(block, pairs):
        moves = [(2 * a + y, 2 * b + y) for a, b in pairs for y in range(2)]
        return lax.ppermute(block, "node", moves)

    def across(block):
        return lax.ppermute(block, "node", [(n, n ^ 1) for n in range(experts)])

    def pick(blocks, users, after=(), cost=0):
        return call(
            functools.partial(pick_kernel, users),
            [bf16((count, cap)), bf16((count, cap)), bf16((cap, wide)), bf16((cap, wide))],
            blocks,
            after,
            [pltpu.VMEM((count, wide), jnp.bfloat16), pltpu.SemaphoreType.DMA],
            [ANYWHERE] * len(blocks),
            cost=cost,
        )

    def expert(own_rows, other_rows, after=(), cost=0):
        tiles = 2 * hidden // size
        return call(
            functools.partial(expert_kernel, experts),
            [bf16((cap, width)), bf16((cap, width))],
            [own_rows, other_rows, *weights],
            after,
            [
                pltpu.VMEM((2 * cap, width), jnp.bfloat16),
                pltpu.VMEM((2 * cap, 2 * hidden), jnp.bfloat16),
                pltpu.VMEM((tiles, width, size), jnp.bfloat16),
                pltpu.VMEM((tiles, width, size), jnp.bfloat16),
                pltpu.VMEM((2, hidden, width), jnp.bfloat16),
                pltpu.SemaphoreType.DMA((tiles, 3)),
            ],
            [IN_VMEM] * 2 + [ANYWHERE] * 6,
            32,
            cost=cost,
        )

    def spread(maps, own_out, other_out, extras=(), after=(), cost=0):
        ins = [*maps, own_out, other_out, *extras]
        return call(spread_kernel, [bf16((count, width))], ins, after, cost=cost)[0]

    plan = arrivals(places)
    held = {}

    last = []

    def ordered(function, *args, after=(), **options):
        out = function(*args, after=(*last, *after), **options)
        last[:] = [out[0] if isinstance(out, (list, tuple)) else out]
        return out

    picks, outs, returned = {}, {}, []

    def relay(step):
        for way in (1, -1):
            pairs = [
                (a, a + way)
                for a in range(places)
                if 0 <= a + way < places and 0 <= a - way * (step - 1) < places
            ]
            held[way, step] = along(held.get((way, step - 1), block), pairs)

    def do_pick(slot, after=(), cost=0):
        keys = sorted({row[slot - 1] for row in plan})
        blocks = [held[key] for key in keys]
        users = [[place for place, row in enumerate(plan) if row[slot - 1] == key] for key in keys]
        *maps, own_rows, other_rows = ordered(pick, blocks, users, after=after, cost=cost)
        picks[slot] = maps, own_rows, across(other_rows)

    def do_expert(slot, after=(), cost=0):
        own_out, other_out = ordered(expert, picks[slot][1], picks[slot][2], after=after, cost=cost)
        outs[slot] = own_out, across(other_out)

    def origin(place, slot):
        way, step = plan[place][slot - 1]
        return place - way * step

    hops = []
    for place in range(places):
        target = origin(place, places - 1)
        near = place + (1 if target > place else -1)
        if near != target and origin(near, places - 2) == target:
            hops.append((place, near))
    staying = {places - 1: [a for a, _ in hops], places - 2: [b for _, b in hops]}
    kept, halves = {}, []

    def spread_halves(maps, own_out, other_out, after=()):
        outs = [bf16((count, width)), bf16((count, width // 2)), bf16((count, width // 2))]
        return call(halves_kernel, outs, [*maps, own_out, other_out], after)

    def do_spread(slot, after=()):
        if slot == places - 1:
            done, *halves[:] = ordered(spread_halves, picks[slot][0], *outs[slot], after=after)
        else:
            done = ordered(spread, picks[slot][0], *outs[slot], after=after)
        kept[slot] = done
        home = [(a, origin(a, slot)) for a in range(places) if a not in staying.get(slot, ())]
        rounds = []
        while home:
            now = list({b: (a, b) for a, b in home}.values())
            home = [pair for pair in home if pair not in now]
            rounds.append(along(done, now))
        returned.append(rounds)

    def call_sum(blocks, after=(), cost=0):
        return call(sum_kernel, [bf16((count, width))], blocks, after, cost=cost)

    def join(whole, half, index, after=()):
        return call(functools.partial(join_kernel, index), [bf16(half.shape)], [whole, half], after)[0]

    def finish(whole, parts):
        while len(whole) > 8:
            summed = sum(array.astype(jnp.float32) for array in whole[:8])
            whole = [summed.astype(jnp.bfloat16), *whole[8:]]
        low = call(low_kernel, [bf16(parts[0].shape)], [*whole, parts[0]], cost=128 * MIB)[0]
        return call(finish_kernel, [bf16((count, width))], [*whole, low, parts[1]])[0]

    relay(1)
    relay(2)
    do_pick(1, after=weights[3:4])
    do_expert(1, cost=64 * MIB)
    held[1, 2], held[-1, 2] = call(
        passing_kernel, [bf16((count, wide))] * 2, [held[1, 2], held[-1, 2]], [*last, picks[1][2]]
    )
    for step in range(3, places):
        relay(step)
    do_pick(2)
    do_spread(1)
    do_pick(3)
    do_expert(2)
    for slot in range(3, places):
        do_expert(slot)
        do_spread(slot - 1, after=returned[slot - 3])
        if slot + 1 < places:
            do_pick(slot + 1)
    picks[0] = picked[:2], picked[2], across(picked[3])
    do_spread(places - 1)
    do_expert(0)
    near = returned.pop(places - 3)
    (summed,) = ordered(call_sum, [*returned.pop(0), *near] if places > 3 else near, cost=128 * MIB)
    homes = [(q, origin(q, places - 2)) for _, q in hops]
    parts = []
    for arrived in [along(half, hops) for half in halves]:
        parts.append(along(ordered(join, kept[places - 2], arrived, len(parts)), homes))
    total = ordered(spread, picks[0][0], *outs[0], [summed])
    return finish([total, *sum(returned, [])], parts)


def solution(mesh):
    placed = (
        P(("groups", "node", "local"), None),
        P(("groups", "node", "local"), None),
        P(("groups", "node", "local"), None),
        P("node", None, "local"),
        P("node", None, "local"),
        P("node", "local", None),
    )
    return jax.shard_map(
        on_device,
        mesh=mesh,
        in_specs=placed,
        out_specs=P(("groups", "node", "local"), None),
        check_vma=False,
    )
```

```python
import functools

import jax
import jax.numpy as jnp
from jax import lax
from jax.experimental import pallas as pl
from jax.experimental.pallas import tpu as pltpu
from jax.sharding import PartitionSpec as P

ANYWHERE = pl.BlockSpec(memory_space=pl.ANY)
IN_VMEM = pl.BlockSpec(memory_space=pltpu.VMEM)
MIB = 1024 * 1024


def arrivals(places):
    plan = []
    for place in range(places):
        left = [(-1, step) for step in range(1, places - place)]
        right = [(1, step) for step in range(1, place + 1)]
        plan.append(left + right if place < places // 2 else right + left)
    return plan


def call(kernel, outs, ins, after=(), scratch=(), specs=None, vmem=16, out_specs=None, cost=0):
    body = kernel
    if after:
        first, last = len(ins), len(ins) + len(after)

        def body(*refs):
            kernel(*refs[:first], *refs[last:])

    specs = list(specs or [IN_VMEM] * len(ins)) + [ANYWHERE] * len(after)
    return pl.pallas_call(
        body,
        out_shape=outs,
        in_specs=specs,
        out_specs=out_specs or [IN_VMEM] * len(outs),
        scratch_shapes=scratch,
        compiler_params=pltpu.CompilerParams(vmem_limit_bytes=vmem * MIB),
        cost_estimate=pl.CostEstimate(flops=0, bytes_accessed=cost, transcendentals=0),
    )(*ins, *after)


def in_vmem(array):
    return pltpu.with_memory_space_constraint(array, pltpu.VMEM)


def tied(arrays, after):
    return pl.pallas_call(
        lambda *refs: None,
        out_shape=[jax.ShapeDtypeStruct(a.shape, a.dtype) for a in arrays],
        in_specs=[ANYWHERE] * (len(arrays) + len(after)),
        out_specs=[ANYWHERE] * len(arrays),
        input_output_aliases={k: k for k in range(len(arrays))},
        cost_estimate=pl.CostEstimate(flops=0, bytes_accessed=0, transcendentals=0),
    )(*[in_vmem(a) for a in arrays], *after)


def first_kernel(experts, tokens, routes, scale, block, *refs):
    picked, (route_held, scale_held, sems) = refs[:4], refs[4:]
    count, width = tokens.shape
    ins = [
        pltpu.make_async_copy(routes, route_held, sems.at[0]),
        pltpu.make_async_copy(scale, scale_held, sems.at[1]),
        pltpu.make_async_copy(tokens, block.at[:, :width], sems.at[2]),
    ]
    for copy in ins:
        copy.start()
    for copy in ins[:2]:
        copy.wait()
    lane = lax.broadcasted_iota(jnp.int32, (count, block.shape[1] - width), 1)
    expert, part = lax.rem(lane, experts), lax.div(lane, experts)
    weight = jnp.zeros(lane.shape, jnp.float32)
    routes, scale = route_held[...].T, scale_held[...].T
    for r in range(routes.shape[1]):
        weight += jnp.where(routes[:, r : r + 1] == expert, scale[:, r : r + 1], 0.0)
    high = weight.astype(jnp.bfloat16).astype(jnp.float32)
    middle = (weight - high).astype(jnp.bfloat16).astype(jnp.float32)
    low = weight - high - middle
    marks = jnp.where(part == 0, high, jnp.where(part == 1, middle, jnp.where(part == 2, low, 0.0)))
    block[:, width:] = marks.astype(jnp.bfloat16)
    ins[2].wait()
    choose(block, *picked)


def passing_kernel(*refs):
    for source, result in zip(refs, refs[len(refs) // 2 :]):
        result[...] = source[...]


def choose(held, own_map, other_map, own_rows, other_rows):
    node = lax.axis_index("node")
    count, cap = own_map.shape
    marks = held[:, held.shape[1] - 128 :].astype(jnp.float32)
    lane = lax.broadcasted_iota(jnp.int32, marks.shape, 1)
    earlier = lax.broadcasted_iota(jnp.int32, (count, count), 0) > lax.broadcasted_iota(jnp.int32, (count, count), 1)
    named = jnp.where(marks != 0, 1.0, 0.0)
    rank = jnp.dot(
        jnp.where(earlier, 1.0, 0.0).astype(jnp.bfloat16), named.astype(jnp.bfloat16), preferred_element_type=jnp.float32
    )
    place = jnp.where(named > 0, rank, -1.0)
    slot = lax.broadcasted_iota(jnp.int32, (count, cap), 1)
    for expert, one_hot, rows in ((node, own_map, own_rows), (node ^ 1, other_map, other_rows)):
        mine = jnp.sum(jnp.where(lane == expert, place, 0.0), axis=1, keepdims=True).astype(jnp.int32)
        chosen = jnp.where(mine == slot, 1.0, 0.0).astype(jnp.bfloat16)
        one_hot[...] = chosen
        rows[...] = lax.dot_general(
            chosen, held[...], (((0,), (0,)), ((), ())), preferred_element_type=jnp.float32
        ).astype(jnp.bfloat16)


def pick_kernel(users, *refs):
    blocks, (held, sem) = refs[: len(users)], refs[len(users) + 4 :]
    node = lax.axis_index("node")
    for block, places in zip(blocks, users):
        here = functools.reduce(jnp.logical_or, [lax.div(node, 2) == place for place in places])

        @pl.when(here)
        def _():
            copy = pltpu.make_async_copy(block, held, sem)
            copy.start()
            copy.wait()

    choose(held, *refs[len(users) : len(users) + 4])


def expert_kernel(experts, own, other, *refs):
    weights, (own_out, other_out, rows, hidden, gates, ups, downs, sems) = refs[:6], refs[6:]
    cap, width = own_out.shape
    tiles, _, size = gates.shape
    each = tiles // 2
    queue = []
    for tile in range(tiles):
        part = pl.ds(tile % each * size, size)
        gate_w, up_w = weights[tile // each * 3 : tile // each * 3 + 2]
        queue.append(pltpu.make_async_copy(gate_w.at[:, part], gates.at[tile], sems.at[tile, 0]))
        queue.append(pltpu.make_async_copy(up_w.at[:, part], ups.at[tile], sems.at[tile, 1]))
    for half, down in enumerate(weights[2::3]):
        queue.append(pltpu.make_async_copy(down, downs.at[half], sems.at[half, 2]))
    ahead = iter(queue[4:])
    for copy in queue[:4]:
        copy.start()

    def arrived(copy):
        copy.wait()
        for following in ahead:
            following.start()
            break

    rows[:cap] = own[:, :width]
    rows[cap:] = other[:, :width]
    for tile in range(tiles):
        arrived(queue[2 * tile])
        gate = jnp.dot(rows[...], gates[tile], preferred_element_type=jnp.float32)
        arrived(queue[2 * tile + 1])
        up = jnp.dot(rows[...], ups[tile], preferred_element_type=jnp.float32)
        hidden[:, tile * size : (tile + 1) * size] = (gate / (1.0 + jnp.exp(-gate)) * up).astype(jnp.bfloat16)
    arrived(queue[-2])
    arrived(queue[-1])
    node = lax.axis_index("node")
    scales = []
    for marked in (own, other):
        marks = marked[:, width:].astype(jnp.float32)
        lane = lax.broadcasted_iota(jnp.int32, marks.shape, 1)
        mine = (lax.rem(lane, experts) == node) & (lane < 3 * experts)
        scales.append(jnp.sum(jnp.where(mine, marks, 0.0), axis=1, keepdims=True))
    step = 512 if width % 512 == 0 else width
    for start in range(0, width, step):
        cut = slice(start, start + step)
        out = jnp.dot(hidden[:, : each * size], downs[0, :, cut], preferred_element_type=jnp.float32)
        out += jnp.dot(hidden[:, each * size :], downs[1, :, cut], preferred_element_type=jnp.float32)
        own_out[:, cut] = (out[:cap] * scales[0]).astype(jnp.bfloat16)
        other_out[:, cut] = (out[cap:] * scales[1]).astype(jnp.bfloat16)


def spread_kernel(own_map, other_map, own_out, other_out, *refs):
    result = refs[-1]
    total = jnp.dot(own_map[...], own_out[...], preferred_element_type=jnp.float32)
    total += jnp.dot(other_map[...], other_out[...], preferred_element_type=jnp.float32)
    for extra in refs[:-1]:
        total += extra[...].astype(jnp.float32)
    result[...] = total.astype(jnp.bfloat16)


def sum_kernel(*refs):
    total = refs[0][...].astype(jnp.float32)
    for extra in refs[1:-1]:
        total += extra[...].astype(jnp.float32)
    refs[-1][...] = total.astype(jnp.bfloat16)


def join_kernel(index, whole, half, result):
    size = half.shape[1]
    total = whole[:, index * size : (index + 1) * size].astype(jnp.float32) + half[...].astype(jnp.float32)
    result[...] = total.astype(jnp.bfloat16)


def halves_kernel(*refs):
    spread_kernel(*refs[:-2])
    size = refs[-1].shape[1]
    refs[-2][...] = refs[-3][:, :size]
    refs[-1][...] = refs[-3][:, size:]


def low_kernel(*refs):
    *whole, low, result = refs
    size = low.shape[1]
    total = low[...].astype(jnp.float32)
    for extra in whole:
        total += extra[:, :size].astype(jnp.float32)
    result[...] = total.astype(jnp.bfloat16)


def finish_kernel(*refs):
    *whole, low, high, result = refs
    size = low.shape[1]
    total = high[...].astype(jnp.float32)
    for extra in whole:
        total += extra[:, size:].astype(jnp.float32)
    result[:, :size] = low[...]
    result[:, size:] = total.astype(jnp.bfloat16)


def on_device(tokens, routes, route_scale, w_gate, w_up, w_down):
    count, width = tokens.shape
    experts = lax.axis_size("node")
    places = experts // 2
    hidden = w_gate.shape[2]
    size = min(hidden, 256)
    cap = -(-(5 * count // experts) // 16) * 16
    wide = width + -(-3 * experts // 128) * 128
    hbm = functools.partial(pltpu.HBM, dtype=jnp.bfloat16)
    in_hbm = functools.partial(pltpu.with_memory_space_constraint, memory_space=pltpu.HBM)
    bf16 = functools.partial(jax.ShapeDtypeStruct, dtype=jnp.bfloat16)

    own = (w_gate[0], w_up[0], w_down[0])
    block, *picked = call(
        functools.partial(first_kernel, experts),
        [bf16((count, wide)), bf16((count, cap)), bf16((count, cap)), hbm((cap, wide)), hbm((cap, wide))],
        [*map(in_hbm, (tokens, routes.T, route_scale.T))],
        (),
        [
            pltpu.VMEM(routes.shape[::-1], routes.dtype),
            pltpu.VMEM(routes.shape[::-1], route_scale.dtype),
            pltpu.SemaphoreType.DMA((3,)),
        ],
        [ANYWHERE] * 3,
    )
    swap = functools.partial(lax.ppermute, axis_name="local", perm=[(0, 1), (1, 0)])
    weights = [*map(in_hbm, own), *map(swap, own)]

    def along(block, pairs):
        moves = [(2 * a + y, 2 * b + y) for a, b in pairs for y in range(2)]
        return lax.ppermute(block, "node", moves)

    def across(block):
        return lax.ppermute(block, "node", [(n, n ^ 1) for n in range(experts)])

    def pick(blocks, users, after=(), cost=0):
        return call(
            functools.partial(pick_kernel, users),
            [bf16((count, cap)), bf16((count, cap)), bf16((cap, wide)), bf16((cap, wide))],
            blocks,
            after,
            [pltpu.VMEM((count, wide), jnp.bfloat16), pltpu.SemaphoreType.DMA],
            [ANYWHERE] * len(blocks),
            cost=cost,
        )

    def expert(own_rows, other_rows, after=(), cost=0):
        tiles = 2 * hidden // size
        return call(
            functools.partial(expert_kernel, experts),
            [bf16((cap, width)), bf16((cap, width))],
            [own_rows, other_rows, *weights],
            after,
            [
                pltpu.VMEM((2 * cap, width), jnp.bfloat16),
                pltpu.VMEM((2 * cap, 2 * hidden), jnp.bfloat16),
                pltpu.VMEM((tiles, width, size), jnp.bfloat16),
                pltpu.VMEM((tiles, width, size), jnp.bfloat16),
                pltpu.VMEM((2, hidden, width), jnp.bfloat16),
                pltpu.SemaphoreType.DMA((tiles, 3)),
            ],
            [IN_VMEM] * 2 + [ANYWHERE] * 6,
            32,
            cost=cost,
        )

    def spread(maps, own_out, other_out, extras=(), after=(), cost=0):
        ins = [*maps, own_out, other_out, *extras]
        return call(spread_kernel, [bf16((count, width))], ins, after, cost=cost)[0]

    plan = arrivals(places)
    held = {}

    last = []

    def ordered(function, *args, after=(), **options):
        out = function(*args, after=(*last, *after), **options)
        last[:] = [out[0] if isinstance(out, (list, tuple)) else out]
        return out

    picks, outs, returned = {}, {}, []

    def relay(step):
        for way in (1, -1):
            pairs = [
                (a, a + way)
                for a in range(places)
                if 0 <= a + way < places and 0 <= a - way * (step - 1) < places
            ]
            held[way, step] = along(held.get((way, step - 1), block), pairs)

    def do_pick(slot, after=(), cost=0):
        keys = sorted({row[slot - 1] for row in plan})
        blocks = [held[key] for key in keys]
        users = [[place for place, row in enumerate(plan) if row[slot - 1] == key] for key in keys]
        *maps, own_rows, other_rows = ordered(pick, blocks, users, after=after, cost=cost)
        picks[slot] = maps, own_rows, across(other_rows)

    def do_expert(slot, after=(), cost=0):
        own_out, other_out = ordered(expert, picks[slot][1], picks[slot][2], after=after, cost=cost)
        outs[slot] = own_out, across(other_out)

    def origin(place, slot):
        way, step = plan[place][slot - 1]
        return place - way * step

    hops = []
    for place in range(places):
        target = origin(place, places - 1)
        near = place + (1 if target > place else -1)
        if near != target and origin(near, places - 2) == target:
            hops.append((place, near))
    staying = {places - 1: [a for a, _ in hops], places - 2: [b for _, b in hops]}
    kept, halves = {}, []

    def spread_halves(maps, own_out, other_out, after=()):
        outs = [bf16((count, width)), bf16((count, width // 2)), bf16((count, width // 2))]
        return call(halves_kernel, outs, [*maps, own_out, other_out], after)

    def do_spread(slot, after=()):
        if slot == places - 1:
            done, *halves[:] = ordered(spread_halves, picks[slot][0], *outs[slot], after=after)
        else:
            done = ordered(spread, picks[slot][0], *outs[slot], after=after)
        kept[slot] = done
        home = [(a, origin(a, slot)) for a in range(places) if a not in staying.get(slot, ())]
        rounds = []
        while home:
            now = list({b: (a, b) for a, b in home}.values())
            home = [pair for pair in home if pair not in now]
            rounds.append(along(done, now))
        returned.append(rounds)

    def call_sum(blocks, after=(), cost=0):
        return call(sum_kernel, [bf16((count, width))], blocks, after, cost=cost)

    def join(whole, half, index, after=()):
        return call(functools.partial(join_kernel, index), [bf16(half.shape)], [whole, half], after)[0]

    def finish(whole, parts):
        while len(whole) > 8:
            summed = sum(array.astype(jnp.float32) for array in whole[:8])
            whole = [summed.astype(jnp.bfloat16), *whole[8:]]
        low = call(low_kernel, [bf16(parts[0].shape)], [*whole, parts[0]], cost=128 * MIB)[0]
        return call(finish_kernel, [bf16((count, width))], [*whole, low, parts[1]])[0]

    relay(1)
    do_pick(1, after=weights[3:4])
    relay(2)
    picks[0] = picked[:2], picked[2], across(picked[3])
    do_expert(1, cost=64 * MIB)
    held[1, 2], held[-1, 2] = call(
        passing_kernel, [bf16((count, wide))] * 2, [held[1, 2], held[-1, 2]], [*last, picks[1][2], picks[0][2]]
    )
    for step in range(3, places):
        relay(step)
    do_pick(2)
    do_expert(0)
    do_spread(1)
    do_pick(3)
    do_expert(2)
    for slot in range(3, places):
        do_expert(slot)
        do_spread(slot - 1, after=returned[slot - 3])
        if slot + 1 < places:
            do_pick(slot + 1)
    do_spread(places - 1)
    near = returned.pop(places - 3)
    (summed,) = ordered(call_sum, [*returned.pop(0), *near] if places > 3 else near, cost=128 * MIB)
    homes = [(q, origin(q, places - 2)) for _, q in hops]
    parts = []
    for arrived in [along(half, hops) for half in halves]:
        parts.append(along(ordered(join, kept[places - 2], arrived, len(parts)), homes))
    total = ordered(spread, picks[0][0], *outs[0], [summed])
    return finish([total, *sum(returned, [])], parts)


def solution(mesh):
    placed = (
        P(("groups", "node", "local"), None),
        P(("groups", "node", "local"), None),
        P(("groups", "node", "local"), None),
        P("node", None, "local"),
        P("node", None, "local"),
        P("node", "local", None),
    )
    return jax.shard_map(
        on_device,
        mesh=mesh,
        in_specs=placed,
        out_specs=P(("groups", "node", "local"), None),
        check_vma=False,
    )
```

```python
import functools

import jax
import jax.numpy as jnp
from jax import lax
from jax.experimental import pallas as pl
from jax.experimental.pallas import tpu as pltpu
from jax.sharding import PartitionSpec as P

ANYWHERE = pl.BlockSpec(memory_space=pl.ANY)
IN_VMEM = pl.BlockSpec(memory_space=pltpu.VMEM)
MIB = 1024 * 1024


def arrivals(places):
    plan = []
    for place in range(places):
        left = [(-1, step) for step in range(1, places - place)]
        right = [(1, step) for step in range(1, place + 1)]
        plan.append(left + right if place < places // 2 else right + left)
    return plan


def call(kernel, outs, ins, after=(), scratch=(), specs=None, vmem=16, out_specs=None, cost=0):
    body = kernel
    if after:
        first, last = len(ins), len(ins) + len(after)

        def body(*refs):
            kernel(*refs[:first], *refs[last:])

    specs = list(specs or [IN_VMEM] * len(ins)) + [ANYWHERE] * len(after)
    return pl.pallas_call(
        body,
        out_shape=outs,
        in_specs=specs,
        out_specs=out_specs or [IN_VMEM] * len(outs),
        scratch_shapes=scratch,
        compiler_params=pltpu.CompilerParams(vmem_limit_bytes=vmem * MIB),
        cost_estimate=pl.CostEstimate(flops=0, bytes_accessed=cost, transcendentals=0),
    )(*ins, *after)


def in_vmem(array):
    return pltpu.with_memory_space_constraint(array, pltpu.VMEM)


def tied(arrays, after):
    return pl.pallas_call(
        lambda *refs: None,
        out_shape=[jax.ShapeDtypeStruct(a.shape, a.dtype) for a in arrays],
        in_specs=[ANYWHERE] * (len(arrays) + len(after)),
        out_specs=[ANYWHERE] * len(arrays),
        input_output_aliases={k: k for k in range(len(arrays))},
        cost_estimate=pl.CostEstimate(flops=0, bytes_accessed=0, transcendentals=0),
    )(*[in_vmem(a) for a in arrays], *after)


def mark_kernel(experts, tokens, routes, scale, block, route_held, scale_held, sems):
    count, width = tokens.shape
    ins = [
        pltpu.make_async_copy(routes, route_held, sems.at[0]),
        pltpu.make_async_copy(scale, scale_held, sems.at[1]),
        pltpu.make_async_copy(tokens, block.at[:, :width], sems.at[2]),
    ]
    for copy in ins:
        copy.start()
    for copy in ins[:2]:
        copy.wait()
    lane = lax.broadcasted_iota(jnp.int32, (count, block.shape[1] - width), 1)
    expert, part = lax.rem(lane, experts), lax.div(lane, experts)
    weight = jnp.zeros(lane.shape, jnp.float32)
    routes, scale = route_held[...].T, scale_held[...].T
    for r in range(routes.shape[1]):
        weight += jnp.where(routes[:, r : r + 1] == expert, scale[:, r : r + 1], 0.0)
    high = weight.astype(jnp.bfloat16).astype(jnp.float32)
    middle = (weight - high).astype(jnp.bfloat16).astype(jnp.float32)
    low = weight - high - middle
    marks = jnp.where(part == 0, high, jnp.where(part == 1, middle, jnp.where(part == 2, low, 0.0)))
    block[:, width:] = marks.astype(jnp.bfloat16)
    ins[2].wait()


def passing_kernel(*refs):
    for source, result in zip(refs, refs[len(refs) // 2 :]):
        result[...] = source[...]


def choose(held, own_map, other_map, own_rows, other_rows):
    node = lax.axis_index("node")
    count, cap = own_map.shape
    marks = held[:, held.shape[1] - 128 :].astype(jnp.float32)
    lane = lax.broadcasted_iota(jnp.int32, marks.shape, 1)
    earlier = lax.broadcasted_iota(jnp.int32, (count, count), 0) > lax.broadcasted_iota(jnp.int32, (count, count), 1)
    named = jnp.where(marks != 0, 1.0, 0.0)
    rank = jnp.dot(
        jnp.where(earlier, 1.0, 0.0).astype(jnp.bfloat16), named.astype(jnp.bfloat16), preferred_element_type=jnp.float32
    )
    place = jnp.where(named > 0, rank, -1.0)
    slot = lax.broadcasted_iota(jnp.int32, (count, cap), 1)
    for expert, one_hot, rows in ((node, own_map, own_rows), (node ^ 1, other_map, other_rows)):
        mine = jnp.sum(jnp.where(lane == expert, place, 0.0), axis=1, keepdims=True).astype(jnp.int32)
        chosen = jnp.where(mine == slot, 1.0, 0.0).astype(jnp.bfloat16)
        one_hot[...] = chosen
        rows[...] = lax.dot_general(
            chosen, held[...], (((0,), (0,)), ((), ())), preferred_element_type=jnp.float32
        ).astype(jnp.bfloat16)


def pick_kernel(users, *refs):
    blocks, (held, sem) = refs[: len(users)], refs[len(users) + 4 :]
    node = lax.axis_index("node")
    for block, places in zip(blocks, users):
        here = functools.reduce(jnp.logical_or, [lax.div(node, 2) == place for place in places])

        @pl.when(here)
        def _():
            copy = pltpu.make_async_copy(block, held, sem)
            copy.start()
            copy.wait()

    choose(held, *refs[len(users) : len(users) + 4])


def expert_kernel(experts, own, other, *refs):
    weights, (own_out, other_out, rows, hidden, gates, ups, downs, sems) = refs[:6], refs[6:]
    cap, width = own_out.shape
    tiles, _, size = gates.shape
    each = tiles // 2
    queue = []
    for tile in range(tiles):
        part = pl.ds(tile % each * size, size)
        gate_w, up_w = weights[tile // each * 3 : tile // each * 3 + 2]
        queue.append(pltpu.make_async_copy(gate_w.at[:, part], gates.at[tile], sems.at[tile, 0]))
        queue.append(pltpu.make_async_copy(up_w.at[:, part], ups.at[tile], sems.at[tile, 1]))
    for half, down in enumerate(weights[2::3]):
        queue.append(pltpu.make_async_copy(down, downs.at[half], sems.at[half, 2]))
    ahead = iter(queue[4:])
    for copy in queue[:4]:
        copy.start()

    def arrived(copy):
        copy.wait()
        for following in ahead:
            following.start()
            break

    rows[:cap] = own[:, :width]
    rows[cap:] = other[:, :width]
    for tile in range(tiles):
        arrived(queue[2 * tile])
        gate = jnp.dot(rows[...], gates[tile], preferred_element_type=jnp.float32)
        arrived(queue[2 * tile + 1])
        up = jnp.dot(rows[...], ups[tile], preferred_element_type=jnp.float32)
        hidden[:, tile * size : (tile + 1) * size] = (gate / (1.0 + jnp.exp(-gate)) * up).astype(jnp.bfloat16)
    arrived(queue[-2])
    arrived(queue[-1])
    node = lax.axis_index("node")
    scales = []
    for marked in (own, other):
        marks = marked[:, width:].astype(jnp.float32)
        lane = lax.broadcasted_iota(jnp.int32, marks.shape, 1)
        mine = (lax.rem(lane, experts) == node) & (lane < 3 * experts)
        scales.append(jnp.sum(jnp.where(mine, marks, 0.0), axis=1, keepdims=True))
    step = 512 if width % 512 == 0 else width
    for start in range(0, width, step):
        cut = slice(start, start + step)
        out = jnp.dot(hidden[:, : each * size], downs[0, :, cut], preferred_element_type=jnp.float32)
        out += jnp.dot(hidden[:, each * size :], downs[1, :, cut], preferred_element_type=jnp.float32)
        own_out[:, cut] = (out[:cap] * scales[0]).astype(jnp.bfloat16)
        other_out[:, cut] = (out[cap:] * scales[1]).astype(jnp.bfloat16)


def spread_kernel(own_map, other_map, own_out, other_out, *refs):
    result = refs[-1]
    total = jnp.dot(own_map[...], own_out[...], preferred_element_type=jnp.float32)
    total += jnp.dot(other_map[...], other_out[...], preferred_element_type=jnp.float32)
    for extra in refs[:-1]:
        total += extra[...].astype(jnp.float32)
    result[...] = total.astype(jnp.bfloat16)


def sum_kernel(*refs):
    total = refs[0][...].astype(jnp.float32)
    for extra in refs[1:-1]:
        total += extra[...].astype(jnp.float32)
    refs[-1][...] = total.astype(jnp.bfloat16)


def join_kernel(index, whole, half, result):
    size = half.shape[1]
    total = whole[:, index * size : (index + 1) * size].astype(jnp.float32) + half[...].astype(jnp.float32)
    result[...] = total.astype(jnp.bfloat16)


def halves_kernel(*refs):
    spread_kernel(*refs[:-2])
    size = refs[-1].shape[1]
    refs[-2][...] = refs[-3][:, :size]
    refs[-1][...] = refs[-3][:, size:]


def low_kernel(*refs):
    *whole, low, result = refs
    size = low.shape[1]
    total = low[...].astype(jnp.float32)
    for extra in whole:
        total += extra[:, :size].astype(jnp.float32)
    result[...] = total.astype(jnp.bfloat16)


def finish_kernel(*refs):
    *whole, low, high, result = refs
    size = low.shape[1]
    total = high[...].astype(jnp.float32)
    for extra in whole:
        total += extra[:, size:].astype(jnp.float32)
    result[:, :size] = low[...]
    result[:, size:] = total.astype(jnp.bfloat16)


def on_device(tokens, routes, route_scale, w_gate, w_up, w_down):
    count, width = tokens.shape
    experts = lax.axis_size("node")
    places = experts // 2
    hidden = w_gate.shape[2]
    size = min(hidden, 256)
    cap = -(-(5 * count // experts) // 16) * 16
    wide = width + -(-3 * experts // 128) * 128
    hbm = functools.partial(pltpu.HBM, dtype=jnp.bfloat16)
    in_hbm = functools.partial(pltpu.with_memory_space_constraint, memory_space=pltpu.HBM)
    bf16 = functools.partial(jax.ShapeDtypeStruct, dtype=jnp.bfloat16)

    own = (w_gate[0], w_up[0], w_down[0])
    (block,) = call(
        functools.partial(mark_kernel, experts),
        [bf16((count, wide))],
        [*map(in_hbm, (tokens, routes.T, route_scale.T))],
        (),
        [
            pltpu.VMEM(routes.shape[::-1], routes.dtype),
            pltpu.VMEM(routes.shape[::-1], route_scale.dtype),
            pltpu.SemaphoreType.DMA((3,)),
        ],
        [ANYWHERE] * 3,
    )
    swap = functools.partial(lax.ppermute, axis_name="local", perm=[(0, 1), (1, 0)])
    weights = [*map(in_hbm, own), *map(swap, own)]

    def along(block, pairs):
        moves = [(2 * a + y, 2 * b + y) for a, b in pairs for y in range(2)]
        return lax.ppermute(block, "node", moves)

    def across(block):
        return lax.ppermute(block, "node", [(n, n ^ 1) for n in range(experts)])

    def pick(blocks, users, after=(), cost=0):
        rows = hbm if len(blocks) == 1 else bf16
        return call(
            functools.partial(pick_kernel, users),
            [bf16((count, cap)), bf16((count, cap)), rows((cap, wide)), rows((cap, wide))],
            blocks,
            after,
            [pltpu.VMEM((count, wide), jnp.bfloat16), pltpu.SemaphoreType.DMA],
            [ANYWHERE] * len(blocks),
            cost=cost,
        )

    def expert(own_rows, other_rows, after=(), cost=0):
        tiles = 2 * hidden // size
        return call(
            functools.partial(expert_kernel, experts),
            [bf16((cap, width)), bf16((cap, width))],
            [own_rows, other_rows, *weights],
            after,
            [
                pltpu.VMEM((2 * cap, width), jnp.bfloat16),
                pltpu.VMEM((2 * cap, 2 * hidden), jnp.bfloat16),
                pltpu.VMEM((tiles, width, size), jnp.bfloat16),
                pltpu.VMEM((tiles, width, size), jnp.bfloat16),
                pltpu.VMEM((2, hidden, width), jnp.bfloat16),
                pltpu.SemaphoreType.DMA((tiles, 3)),
            ],
            [IN_VMEM] * 2 + [ANYWHERE] * 6,
            32,
            cost=cost,
        )

    def spread(maps, own_out, other_out, extras=(), after=(), cost=0):
        ins = [*maps, own_out, other_out, *extras]
        return call(spread_kernel, [bf16((count, width))], ins, after, cost=cost)[0]

    plan = arrivals(places)
    held = {}

    last = []

    def ordered(function, *args, after=(), **options):
        out = function(*args, after=(*last, *after), **options)
        last[:] = [out[0] if isinstance(out, (list, tuple)) else out]
        return out

    picks, outs, returned = {}, {}, []

    def relay(step):
        for way in (1, -1):
            pairs = [
                (a, a + way)
                for a in range(places)
                if 0 <= a + way < places and 0 <= a - way * (step - 1) < places
            ]
            held[way, step] = along(held.get((way, step - 1), block), pairs)

    def do_pick(slot, after=(), cost=0):
        if slot == 0:
            *maps, own_rows, other_rows = ordered(pick, [block], [range(places)], after=after)
            picks[0] = maps, own_rows, across(other_rows)
            return
        keys = sorted({row[slot - 1] for row in plan})
        blocks = [held[key] for key in keys]
        users = [[place for place, row in enumerate(plan) if row[slot - 1] == key] for key in keys]
        *maps, own_rows, other_rows = ordered(pick, blocks, users, after=after, cost=cost)
        picks[slot] = maps, own_rows, across(other_rows)

    def do_expert(slot, after=(), cost=0):
        own_out, other_out = ordered(expert, picks[slot][1], picks[slot][2], after=after, cost=cost)
        outs[slot] = own_out, across(other_out)

    def origin(place, slot):
        way, step = plan[place][slot - 1]
        return place - way * step

    hops = []
    for place in range(places):
        target = origin(place, places - 1)
        near = place + (1 if target > place else -1)
        if near != target and origin(near, places - 2) == target:
            hops.append((place, near))
    staying = {places - 1: [a for a, _ in hops], places - 2: [b for _, b in hops]}
    kept, halves = {}, []

    def spread_halves(maps, own_out, other_out, after=()):
        outs = [bf16((count, width)), bf16((count, width // 2)), bf16((count, width // 2))]
        return call(halves_kernel, outs, [*maps, own_out, other_out], after)

    def do_spread(slot, after=(), cost=0):
        if slot == places - 1:
            done, *halves[:] = ordered(spread_halves, picks[slot][0], *outs[slot], after=after)
        else:
            done = ordered(spread, picks[slot][0], *outs[slot], after=after, cost=cost)
        kept[slot] = done
        home = [(a, origin(a, slot)) for a in range(places) if a not in staying.get(slot, ())]
        rounds = []
        while home:
            now = list({b: (a, b) for a, b in home}.values())
            home = [pair for pair in home if pair not in now]
            rounds.append(along(done, now))
        returned.append(rounds)

    def call_sum(blocks, after=(), cost=0):
        return call(sum_kernel, [bf16((count, width))], blocks, after, cost=cost)

    def join(whole, half, index, after=()):
        return call(functools.partial(join_kernel, index), [bf16(half.shape)], [whole, half], after)[0]

    def finish(whole, parts):
        while len(whole) > 8:
            summed = sum(array.astype(jnp.float32) for array in whole[:8])
            whole = [summed.astype(jnp.bfloat16), *whole[8:]]
        low = call(low_kernel, [bf16(parts[0].shape)], [*whole, parts[0]], cost=128 * MIB)[0]
        return call(finish_kernel, [bf16((count, width))], [*whole, low, parts[1]])[0]

    relay(1)
    relay(2)
    do_pick(1, after=weights[3:4])
    do_pick(0)
    do_expert(1, cost=64 * MIB)
    held[1, 2], held[-1, 2] = call(
        passing_kernel, [bf16((count, wide))] * 2, [held[1, 2], held[-1, 2]], [*last, picks[1][2]]
    )
    for step in range(3, places):
        relay(step)
    do_pick(2)
    do_spread(1, cost=64 * MIB)
    do_pick(3)
    do_expert(2)
    for slot in range(3, places):
        do_expert(slot)
        do_spread(slot - 1, after=returned[slot - 3])
        if slot + 1 < places:
            do_pick(slot + 1)
    do_spread(places - 1)
    do_expert(0)
    near = returned.pop(places - 3)
    (summed,) = ordered(call_sum, [*returned.pop(0), *near] if places > 3 else near, cost=128 * MIB)
    homes = [(q, origin(q, places - 2)) for _, q in hops]
    parts = []
    for arrived in [along(half, hops) for half in halves]:
        parts.append(along(ordered(join, kept[places - 2], arrived, len(parts)), homes))
    total = ordered(spread, picks[0][0], *outs[0], [summed])
    return finish([total, *sum(returned, [])], parts)


def solution(mesh):
    placed = (
        P(("groups", "node", "local"), None),
        P(("groups", "node", "local"), None),
        P(("groups", "node", "local"), None),
        P("node", None, "local"),
        P("node", None, "local"),
        P("node", "local", None),
    )
    return jax.shard_map(
        on_device,
        mesh=mesh,
        in_specs=placed,
        out_specs=P(("groups", "node", "local"), None),
        check_vma=False,
    )
```

```python
import functools

import jax
import jax.numpy as jnp
from jax import lax
from jax.experimental import pallas as pl
from jax.experimental.pallas import tpu as pltpu
from jax.sharding import PartitionSpec as P

ANYWHERE = pl.BlockSpec(memory_space=pl.ANY)
IN_VMEM = pl.BlockSpec(memory_space=pltpu.VMEM)
MIB = 1024 * 1024


def arrivals(places):
    plan = []
    for place in range(places):
        left = [(-1, step) for step in range(1, places - place)]
        right = [(1, step) for step in range(1, place + 1)]
        plan.append(left + right if place < places // 2 else right + left)
    return plan


def call(kernel, outs, ins, after=(), scratch=(), specs=None, vmem=16, out_specs=None, cost=0):
    body = kernel
    if after:
        first, last = len(ins), len(ins) + len(after)

        def body(*refs):
            kernel(*refs[:first], *refs[last:])

    specs = list(specs or [IN_VMEM] * len(ins)) + [ANYWHERE] * len(after)
    return pl.pallas_call(
        body,
        out_shape=outs,
        in_specs=specs,
        out_specs=out_specs or [IN_VMEM] * len(outs),
        scratch_shapes=scratch,
        compiler_params=pltpu.CompilerParams(vmem_limit_bytes=vmem * MIB),
        cost_estimate=pl.CostEstimate(flops=0, bytes_accessed=cost, transcendentals=0),
    )(*ins, *after)


def in_vmem(array):
    return pltpu.with_memory_space_constraint(array, pltpu.VMEM)


def tied(arrays, after):
    return pl.pallas_call(
        lambda *refs: None,
        out_shape=[jax.ShapeDtypeStruct(a.shape, a.dtype) for a in arrays],
        in_specs=[ANYWHERE] * (len(arrays) + len(after)),
        out_specs=[ANYWHERE] * len(arrays),
        input_output_aliases={k: k for k in range(len(arrays))},
        cost_estimate=pl.CostEstimate(flops=0, bytes_accessed=0, transcendentals=0),
    )(*[in_vmem(a) for a in arrays], *after)


def mark_kernel(experts, tokens, routes, scale, block, route_held, scale_held, sems):
    count, width = tokens.shape
    ins = [
        pltpu.make_async_copy(routes, route_held, sems.at[0]),
        pltpu.make_async_copy(scale, scale_held, sems.at[1]),
        pltpu.make_async_copy(tokens, block.at[:, :width], sems.at[2]),
    ]
    for copy in ins:
        copy.start()
    for copy in ins[:2]:
        copy.wait()
    lane = lax.broadcasted_iota(jnp.int32, (count, block.shape[1] - width), 1)
    expert, part = lax.rem(lane, experts), lax.div(lane, experts)
    weight = jnp.zeros(lane.shape, jnp.float32)
    routes, scale = route_held[...].T, scale_held[...].T
    for r in range(routes.shape[1]):
        weight += jnp.where(routes[:, r : r + 1] == expert, scale[:, r : r + 1], 0.0)
    high = weight.astype(jnp.bfloat16).astype(jnp.float32)
    middle = (weight - high).astype(jnp.bfloat16).astype(jnp.float32)
    low = weight - high - middle
    marks = jnp.where(part == 0, high, jnp.where(part == 1, middle, jnp.where(part == 2, low, 0.0)))
    block[:, width:] = marks.astype(jnp.bfloat16)
    ins[2].wait()


def passing_kernel(*refs):
    for source, result in zip(refs, refs[len(refs) // 2 :]):
        result[...] = source[...]


def choose(held, own_map, other_map, own_rows, other_rows):
    node = lax.axis_index("node")
    count, cap = own_map.shape
    marks = held[:, held.shape[1] - 128 :].astype(jnp.float32)
    lane = lax.broadcasted_iota(jnp.int32, marks.shape, 1)
    earlier = lax.broadcasted_iota(jnp.int32, (count, count), 0) > lax.broadcasted_iota(jnp.int32, (count, count), 1)
    named = jnp.where(marks != 0, 1.0, 0.0)
    rank = jnp.dot(
        jnp.where(earlier, 1.0, 0.0).astype(jnp.bfloat16), named.astype(jnp.bfloat16), preferred_element_type=jnp.float32
    )
    place = jnp.where(named > 0, rank, -1.0)
    slot = lax.broadcasted_iota(jnp.int32, (count, cap), 1)
    for expert, one_hot, rows in ((node, own_map, own_rows), (node ^ 1, other_map, other_rows)):
        mine = jnp.sum(jnp.where(lane == expert, place, 0.0), axis=1, keepdims=True).astype(jnp.int32)
        chosen = jnp.where(mine == slot, 1.0, 0.0).astype(jnp.bfloat16)
        one_hot[...] = chosen
        rows[...] = lax.dot_general(
            chosen, held[...], (((0,), (0,)), ((), ())), preferred_element_type=jnp.float32
        ).astype(jnp.bfloat16)


def pick_kernel(users, *refs):
    blocks, (held, sem) = refs[: len(users)], refs[len(users) + 4 :]
    node = lax.axis_index("node")
    for block, places in zip(blocks, users):
        here = functools.reduce(jnp.logical_or, [lax.div(node, 2) == place for place in places])

        @pl.when(here)
        def _():
            copy = pltpu.make_async_copy(block, held, sem)
            copy.start()
            copy.wait()

    choose(held, *refs[len(users) : len(users) + 4])


def expert_kernel(experts, count, *refs):
    marked, weights, outs = refs[:count], refs[count : count + 6], refs[count + 6 : 2 * count + 6]
    rows, hidden, gates, ups, downs, sems = refs[2 * count + 6 :]
    cap, width = outs[0].shape
    tiles, _, size = gates.shape
    each = tiles // 2
    queue = []
    for tile in range(tiles):
        part = pl.ds(tile % each * size, size)
        gate_w, up_w = weights[tile // each * 3 : tile // each * 3 + 2]
        queue.append(pltpu.make_async_copy(gate_w.at[:, part], gates.at[tile], sems.at[tile, 0]))
        queue.append(pltpu.make_async_copy(up_w.at[:, part], ups.at[tile], sems.at[tile, 1]))
    for half, down in enumerate(weights[2::3]):
        queue.append(pltpu.make_async_copy(down, downs.at[half], sems.at[half, 2]))
    ahead = iter(queue[4:])
    for copy in queue[:4]:
        copy.start()

    def arrived(copy):
        copy.wait()
        for following in ahead:
            following.start()
            break

    for k, source in enumerate(marked):
        rows[k * cap : (k + 1) * cap] = source[:, :width]
    for tile in range(tiles):
        arrived(queue[2 * tile])
        gate = jnp.dot(rows[...], gates[tile], preferred_element_type=jnp.float32)
        arrived(queue[2 * tile + 1])
        up = jnp.dot(rows[...], ups[tile], preferred_element_type=jnp.float32)
        hidden[:, tile * size : (tile + 1) * size] = (gate / (1.0 + jnp.exp(-gate)) * up).astype(jnp.bfloat16)
    arrived(queue[-2])
    arrived(queue[-1])
    node = lax.axis_index("node")
    scales = []
    for source in marked:
        marks = source[:, width:].astype(jnp.float32)
        lane = lax.broadcasted_iota(jnp.int32, marks.shape, 1)
        mine = (lax.rem(lane, experts) == node) & (lane < 3 * experts)
        scales.append(jnp.sum(jnp.where(mine, marks, 0.0), axis=1, keepdims=True))
    step = 512 if width % 512 == 0 else width
    for start in range(0, width, step):
        cut = slice(start, start + step)
        out = jnp.dot(hidden[:, : each * size], downs[0, :, cut], preferred_element_type=jnp.float32)
        out += jnp.dot(hidden[:, each * size :], downs[1, :, cut], preferred_element_type=jnp.float32)
        for k, result in enumerate(outs):
            result[:, cut] = (out[k * cap : (k + 1) * cap] * scales[k]).astype(jnp.bfloat16)


def spread_kernel(own_map, other_map, own_out, other_out, *refs):
    result = refs[-1]
    total = jnp.dot(own_map[...], own_out[...], preferred_element_type=jnp.float32)
    total += jnp.dot(other_map[...], other_out[...], preferred_element_type=jnp.float32)
    for extra in refs[:-1]:
        total += extra[...].astype(jnp.float32)
    result[...] = total.astype(jnp.bfloat16)


def sum_kernel(*refs):
    total = refs[0][...].astype(jnp.float32)
    for extra in refs[1:-1]:
        total += extra[...].astype(jnp.float32)
    refs[-1][...] = total.astype(jnp.bfloat16)


def join_kernel(index, whole, half, result):
    size = half.shape[1]
    total = whole[:, index * size : (index + 1) * size].astype(jnp.float32) + half[...].astype(jnp.float32)
    result[...] = total.astype(jnp.bfloat16)


def halves_kernel(*refs):
    spread_kernel(*refs[:-2])
    size = refs[-1].shape[1]
    refs[-2][...] = refs[-3][:, :size]
    refs[-1][...] = refs[-3][:, size:]


def low_kernel(*refs):
    *whole, low, result = refs
    size = low.shape[1]
    total = low[...].astype(jnp.float32)
    for extra in whole:
        total += extra[:, :size].astype(jnp.float32)
    result[...] = total.astype(jnp.bfloat16)


def finish_kernel(total, *refs):
    *whole, low, high, result = refs
    size = low.shape[1]
    result[:, :size] = (low[...].astype(jnp.float32) + total[:, :size].astype(jnp.float32)).astype(jnp.bfloat16)
    rest = high[...].astype(jnp.float32) + total[:, size:].astype(jnp.float32)
    for extra in whole:
        rest += extra[:, size:].astype(jnp.float32)
    result[:, size:] = rest.astype(jnp.bfloat16)


def on_device(tokens, routes, route_scale, w_gate, w_up, w_down):
    count, width = tokens.shape
    experts = lax.axis_size("node")
    places = experts // 2
    hidden = w_gate.shape[2]
    size = min(hidden, 256)
    cap = -(-(5 * count // experts) // 16) * 16
    wide = width + -(-3 * experts // 128) * 128
    hbm = functools.partial(pltpu.HBM, dtype=jnp.bfloat16)
    in_hbm = functools.partial(pltpu.with_memory_space_constraint, memory_space=pltpu.HBM)
    bf16 = functools.partial(jax.ShapeDtypeStruct, dtype=jnp.bfloat16)

    own = (w_gate[0], w_up[0], w_down[0])
    (block,) = call(
        functools.partial(mark_kernel, experts),
        [bf16((count, wide))],
        [*map(in_hbm, (tokens, routes.T, route_scale.T))],
        (),
        [
            pltpu.VMEM(routes.shape[::-1], routes.dtype),
            pltpu.VMEM(routes.shape[::-1], route_scale.dtype),
            pltpu.SemaphoreType.DMA((3,)),
        ],
        [ANYWHERE] * 3,
    )
    swap = functools.partial(lax.ppermute, axis_name="local", perm=[(0, 1), (1, 0)])
    weights = [*map(in_hbm, own), *map(swap, own)]

    def along(block, pairs):
        moves = [(2 * a + y, 2 * b + y) for a, b in pairs for y in range(2)]
        return lax.ppermute(block, "node", moves)

    def across(block):
        return lax.ppermute(block, "node", [(n, n ^ 1) for n in range(experts)])

    def pick(blocks, users, after=(), cost=0):
        rows = hbm if len(blocks) == 1 else bf16
        return call(
            functools.partial(pick_kernel, users),
            [bf16((count, cap)), bf16((count, cap)), rows((cap, wide)), rows((cap, wide))],
            blocks,
            after,
            [pltpu.VMEM((count, wide), jnp.bfloat16), pltpu.SemaphoreType.DMA],
            [ANYWHERE] * len(blocks),
            cost=cost,
        )

    def expert(rows, after=(), cost=0):
        tiles = 2 * hidden // size
        return call(
            functools.partial(expert_kernel, experts, len(rows)),
            [bf16((cap, width))] * len(rows),
            [*rows, *weights],
            after,
            [
                pltpu.VMEM((len(rows) * cap, width), jnp.bfloat16),
                pltpu.VMEM((len(rows) * cap, 2 * hidden), jnp.bfloat16),
                pltpu.VMEM((tiles, width, size), jnp.bfloat16),
                pltpu.VMEM((tiles, width, size), jnp.bfloat16),
                pltpu.VMEM((2, hidden, width), jnp.bfloat16),
                pltpu.SemaphoreType.DMA((tiles, 3)),
            ],
            [IN_VMEM] * len(rows) + [ANYWHERE] * 6,
            32,
            cost=cost,
        )

    def spread(maps, own_out, other_out, extras=(), after=(), cost=0):
        ins = [*maps, own_out, other_out, *extras]
        return call(spread_kernel, [bf16((count, width))], ins, after, cost=cost)[0]

    plan = arrivals(places)
    held = {}

    last = []

    def ordered(function, *args, after=(), **options):
        out = function(*args, after=(*last, *after), **options)
        last[:] = [out[0] if isinstance(out, (list, tuple)) else out]
        return out

    picks, outs, returned = {}, {}, []

    def relay(step):
        for way in (1, -1):
            pairs = [
                (a, a + way)
                for a in range(places)
                if 0 <= a + way < places and 0 <= a - way * (step - 1) < places
            ]
            held[way, step] = along(held.get((way, step - 1), block), pairs)

    def do_pick(slot, after=(), cost=0):
        if slot == 0:
            *maps, own_rows, other_rows = ordered(pick, [block], [range(places)], after=after)
            picks[0] = maps, own_rows, across(other_rows)
            return
        keys = sorted({row[slot - 1] for row in plan})
        blocks = [held[key] for key in keys]
        users = [[place for place, row in enumerate(plan) if row[slot - 1] == key] for key in keys]
        *maps, own_rows, other_rows = ordered(pick, blocks, users, after=after, cost=cost)
        picks[slot] = maps, own_rows, across(other_rows)

    def do_expert(slot, after=(), cost=0):
        own_out, other_out = ordered(expert, picks[slot][1:], after=after, cost=cost)
        outs[slot] = own_out, across(other_out)

    def origin(place, slot):
        way, step = plan[place][slot - 1]
        return place - way * step

    hops = []
    for place in range(places):
        target = origin(place, places - 1)
        near = place + (1 if target > place else -1)
        if near != target and origin(near, places - 2) == target:
            hops.append((place, near))
    staying = {places - 1: [a for a, _ in hops], places - 2: [b for _, b in hops]}
    kept, halves = {}, []

    def spread_halves(maps, own_out, other_out, after=()):
        outs = [bf16((count, width)), bf16((count, width // 2)), bf16((count, width // 2))]
        return call(halves_kernel, outs, [*maps, own_out, other_out], after)

    def do_spread(slot, after=(), cost=0):
        if slot == places - 1:
            done, *halves[:] = ordered(spread_halves, picks[slot][0], *outs[slot], after=after)
        else:
            done = ordered(spread, picks[slot][0], *outs[slot], after=after, cost=cost)
        kept[slot] = done
        home = [(a, origin(a, slot)) for a in range(places) if a not in staying.get(slot, ())]
        rounds = []
        while home:
            now = list({b: (a, b) for a, b in home}.values())
            home = [pair for pair in home if pair not in now]
            rounds.append(along(done, now))
        returned.append(rounds)

    def call_sum(blocks, after=(), cost=0):
        return call(sum_kernel, [bf16((count, width))], blocks, after, cost=cost)

    def join(whole, half, index, after=()):
        return call(functools.partial(join_kernel, index), [bf16(half.shape)], [whole, half], after)[0]

    def finish(whole, parts, summed):
        while len(whole) > 8:
            merged = sum(array.astype(jnp.float32) for array in whole[:8])
            whole = [merged.astype(jnp.bfloat16), *whole[8:]]
        low = ordered(finish_low, whole, parts[0])
        total = ordered(spread, picks[0][0], *outs[0], [summed])
        return call(finish_kernel, [bf16((count, width))], [total, *whole, low, parts[1]])[0]

    def finish_low(whole, half, after=()):
        return call(low_kernel, [bf16(half.shape)], [*whole, half], after, cost=128 * MIB)[0]

    relay(1)
    relay(2)
    do_pick(1, after=weights[3:4])
    do_pick(0)
    do_expert(1, cost=64 * MIB)
    held[1, 2], held[-1, 2] = call(
        passing_kernel, [bf16((count, wide))] * 2, [held[1, 2], held[-1, 2]], [*last, picks[1][2]]
    )
    for step in range(3, places):
        relay(step)
    do_pick(2)
    do_spread(1, cost=64 * MIB)
    do_pick(3)
    do_expert(2)
    for slot in range(3, places):
        do_expert(slot)
        do_spread(slot - 1, after=returned[slot - 3])
        if slot + 1 < places:
            do_pick(slot + 1)
    (own_out,) = ordered(expert, picks[0][1:2])
    do_spread(places - 1)
    (other_out,) = ordered(expert, picks[0][2:])
    outs[0] = own_out, across(other_out)
    near = returned.pop(places - 3)
    (summed,) = ordered(call_sum, [*returned.pop(0), *near] if places > 3 else near, cost=128 * MIB)
    homes = [(q, origin(q, places - 2)) for _, q in hops]
    parts = []
    for arrived in [along(half, hops) for half in halves]:
        parts.append(along(ordered(join, kept[places - 2], arrived, len(parts)), homes))
    return finish(sum(returned, []), parts, summed)


def solution(mesh):
    placed = (
        P(("groups", "node", "local"), None),
        P(("groups", "node", "local"), None),
        P(("groups", "node", "local"), None),
        P("node", None, "local"),
        P("node", None, "local"),
        P("node", "local", None),
    )
    return jax.shard_map(
        on_device,
        mesh=mesh,
        in_specs=placed,
        out_specs=P(("groups", "node", "local"), None),
        check_vma=False,
    )
```

```python
import functools

import jax
import jax.numpy as jnp
from jax import lax
from jax.experimental import pallas as pl
from jax.experimental.pallas import tpu as pltpu
from jax.sharding import PartitionSpec as P

ANYWHERE = pl.BlockSpec(memory_space=pl.ANY)
IN_VMEM = pl.BlockSpec(memory_space=pltpu.VMEM)
MIB = 1024 * 1024


def arrivals(places):
    plan = []
    for place in range(places):
        ways = (-1, 1) if place < places // 2 else (1, -1)
        steps = [(way, step) for step in range(1, places) for way in ways]
        plan.append([(way, step) for way, step in steps if 0 <= place - way * step < places])
    return plan


def call(kernel, outs, ins, after=(), scratch=(), specs=None, vmem=16, out_specs=None, cost=0):
    body = kernel
    if after:
        first, last = len(ins), len(ins) + len(after)

        def body(*refs):
            kernel(*refs[:first], *refs[last:])

    specs = list(specs or [IN_VMEM] * len(ins)) + [ANYWHERE] * len(after)
    return pl.pallas_call(
        body,
        out_shape=outs,
        in_specs=specs,
        out_specs=out_specs or [IN_VMEM] * len(outs),
        scratch_shapes=scratch,
        compiler_params=pltpu.CompilerParams(vmem_limit_bytes=vmem * MIB),
        cost_estimate=pl.CostEstimate(flops=0, bytes_accessed=cost, transcendentals=0),
    )(*ins, *after)


def in_vmem(array):
    return pltpu.with_memory_space_constraint(array, pltpu.VMEM)


def tied(arrays, after):
    return pl.pallas_call(
        lambda *refs: None,
        out_shape=[jax.ShapeDtypeStruct(a.shape, a.dtype) for a in arrays],
        in_specs=[ANYWHERE] * (len(arrays) + len(after)),
        out_specs=[ANYWHERE] * len(arrays),
        input_output_aliases={k: k for k in range(len(arrays))},
        cost_estimate=pl.CostEstimate(flops=0, bytes_accessed=0, transcendentals=0),
    )(*[in_vmem(a) for a in arrays], *after)


def mark_kernel(experts, tokens, routes, scale, block, route_held, scale_held, sems):
    count, width = tokens.shape
    ins = [
        pltpu.make_async_copy(routes, route_held, sems.at[0]),
        pltpu.make_async_copy(scale, scale_held, sems.at[1]),
        pltpu.make_async_copy(tokens, block.at[:, :width], sems.at[2]),
    ]
    for copy in ins:
        copy.start()
    for copy in ins[:2]:
        copy.wait()
    lane = lax.broadcasted_iota(jnp.int32, (count, block.shape[1] - width), 1)
    expert, part = lax.rem(lane, experts), lax.div(lane, experts)
    weight = jnp.zeros(lane.shape, jnp.float32)
    routes, scale = route_held[...].T, scale_held[...].T
    for r in range(routes.shape[1]):
        weight += jnp.where(routes[:, r : r + 1] == expert, scale[:, r : r + 1], 0.0)
    high = weight.astype(jnp.bfloat16).astype(jnp.float32)
    middle = (weight - high).astype(jnp.bfloat16).astype(jnp.float32)
    low = weight - high - middle
    marks = jnp.where(part == 0, high, jnp.where(part == 1, middle, jnp.where(part == 2, low, 0.0)))
    block[:, width:] = marks.astype(jnp.bfloat16)
    ins[2].wait()


def passing_kernel(*refs):
    for source, result in zip(refs, refs[len(refs) // 2 :]):
        result[...] = source[...]


def choose(held, own_map, other_map, own_rows, other_rows):
    node = lax.axis_index("node")
    count, cap = own_map.shape
    marks = held[:, held.shape[1] - 128 :].astype(jnp.float32)
    lane = lax.broadcasted_iota(jnp.int32, marks.shape, 1)
    earlier = lax.broadcasted_iota(jnp.int32, (count, count), 0) > lax.broadcasted_iota(jnp.int32, (count, count), 1)
    named = jnp.where(marks != 0, 1.0, 0.0)
    rank = jnp.dot(
        jnp.where(earlier, 1.0, 0.0).astype(jnp.bfloat16), named.astype(jnp.bfloat16), preferred_element_type=jnp.float32
    )
    place = jnp.where(named > 0, rank, -1.0)
    slot = lax.broadcasted_iota(jnp.int32, (count, cap), 1)
    for expert, one_hot, rows in ((node, own_map, own_rows), (node ^ 1, other_map, other_rows)):
        mine = jnp.sum(jnp.where(lane == expert, place, 0.0), axis=1, keepdims=True).astype(jnp.int32)
        chosen = jnp.where(mine == slot, 1.0, 0.0).astype(jnp.bfloat16)
        one_hot[...] = chosen
        rows[...] = lax.dot_general(
            chosen, held[...], (((0,), (0,)), ((), ())), preferred_element_type=jnp.float32
        ).astype(jnp.bfloat16)


def pick_kernel(users, *refs):
    blocks, (held, sem) = refs[: len(users)], refs[len(users) + 4 :]
    node = lax.axis_index("node")
    for block, places in zip(blocks, users):
        here = functools.reduce(jnp.logical_or, [lax.div(node, 2) == place for place in places])

        @pl.when(here)
        def _():
            copy = pltpu.make_async_copy(block, held, sem)
            copy.start()
            copy.wait()

    choose(held, *refs[len(users) : len(users) + 4])


def expert_kernel(experts, count, *refs):
    marked, weights, outs = refs[:count], refs[count : count + 6], refs[count + 6 : 2 * count + 6]
    rows, hidden, gates, ups, downs, sems = refs[2 * count + 6 :]
    cap, width = outs[0].shape
    tiles, _, size = gates.shape
    each = tiles // 2
    queue = []
    for tile in range(tiles):
        part = pl.ds(tile % each * size, size)
        gate_w, up_w = weights[tile // each * 3 : tile // each * 3 + 2]
        queue.append(pltpu.make_async_copy(gate_w.at[:, part], gates.at[tile], sems.at[tile, 0]))
        queue.append(pltpu.make_async_copy(up_w.at[:, part], ups.at[tile], sems.at[tile, 1]))
    for half, down in enumerate(weights[2::3]):
        queue.append(pltpu.make_async_copy(down, downs.at[half], sems.at[half, 2]))
    ahead = iter(queue[4:])
    for copy in queue[:4]:
        copy.start()

    def arrived(copy):
        copy.wait()
        for following in ahead:
            following.start()
            break

    for k, source in enumerate(marked):
        rows[k * cap : (k + 1) * cap] = source[:, :width]
    for tile in range(tiles):
        arrived(queue[2 * tile])
        gate = jnp.dot(rows[...], gates[tile], preferred_element_type=jnp.float32)
        arrived(queue[2 * tile + 1])
        up = jnp.dot(rows[...], ups[tile], preferred_element_type=jnp.float32)
        hidden[:, tile * size : (tile + 1) * size] = (gate / (1.0 + jnp.exp(-gate)) * up).astype(jnp.bfloat16)
    arrived(queue[-2])
    arrived(queue[-1])
    node = lax.axis_index("node")
    scales = []
    for source in marked:
        marks = source[:, width:].astype(jnp.float32)
        lane = lax.broadcasted_iota(jnp.int32, marks.shape, 1)
        mine = (lax.rem(lane, experts) == node) & (lane < 3 * experts)
        scales.append(jnp.sum(jnp.where(mine, marks, 0.0), axis=1, keepdims=True))
    step = 512 if width % 512 == 0 else width
    for start in range(0, width, step):
        cut = slice(start, start + step)
        out = jnp.dot(hidden[:, : each * size], downs[0, :, cut], preferred_element_type=jnp.float32)
        out += jnp.dot(hidden[:, each * size :], downs[1, :, cut], preferred_element_type=jnp.float32)
        for k, result in enumerate(outs):
            result[:, cut] = (out[k * cap : (k + 1) * cap] * scales[k]).astype(jnp.bfloat16)


def spread_kernel(own_map, other_map, own_out, other_out, *refs):
    result = refs[-1]
    total = jnp.dot(own_map[...], own_out[...], preferred_element_type=jnp.float32)
    total += jnp.dot(other_map[...], other_out[...], preferred_element_type=jnp.float32)
    for extra in refs[:-1]:
        total += extra[...].astype(jnp.float32)
    result[...] = total.astype(jnp.bfloat16)


def sum_kernel(*refs):
    total = refs[0][...].astype(jnp.float32)
    for extra in refs[1:-1]:
        total += extra[...].astype(jnp.float32)
    refs[-1][...] = total.astype(jnp.bfloat16)


def join_kernel(index, whole, half, result):
    size = half.shape[1]
    total = whole[:, index * size : (index + 1) * size].astype(jnp.float32) + half[...].astype(jnp.float32)
    result[...] = total.astype(jnp.bfloat16)


def halves_kernel(*refs):
    spread_kernel(*refs[:-2])
    size = refs[-1].shape[1]
    refs[-2][...] = refs[-3][:, :size]
    refs[-1][...] = refs[-3][:, size:]


def low_kernel(*refs):
    *whole, low, result = refs
    size = low.shape[1]
    total = low[...].astype(jnp.float32)
    for extra in whole:
        total += extra[:, :size].astype(jnp.float32)
    result[...] = total.astype(jnp.bfloat16)


def finish_kernel(total, *refs):
    *whole, low, high, result = refs
    size = low.shape[1]
    result[:, :size] = (low[...].astype(jnp.float32) + total[:, :size].astype(jnp.float32)).astype(jnp.bfloat16)
    rest = high[...].astype(jnp.float32) + total[:, size:].astype(jnp.float32)
    for extra in whole:
        rest += extra[:, size:].astype(jnp.float32)
    result[:, size:] = rest.astype(jnp.bfloat16)


def on_device(tokens, routes, route_scale, w_gate, w_up, w_down):
    count, width = tokens.shape
    experts = lax.axis_size("node")
    places = experts // 2
    hidden = w_gate.shape[2]
    size = min(hidden, 256)
    cap = -(-(5 * count // experts) // 16) * 16
    wide = width + -(-3 * experts // 128) * 128
    hbm = functools.partial(pltpu.HBM, dtype=jnp.bfloat16)
    in_hbm = functools.partial(pltpu.with_memory_space_constraint, memory_space=pltpu.HBM)
    bf16 = functools.partial(jax.ShapeDtypeStruct, dtype=jnp.bfloat16)

    own = (w_gate[0], w_up[0], w_down[0])
    (block,) = call(
        functools.partial(mark_kernel, experts),
        [bf16((count, wide))],
        [*map(in_hbm, (tokens, routes.T, route_scale.T))],
        (),
        [
            pltpu.VMEM(routes.shape[::-1], routes.dtype),
            pltpu.VMEM(routes.shape[::-1], route_scale.dtype),
            pltpu.SemaphoreType.DMA((3,)),
        ],
        [ANYWHERE] * 3,
    )
    swap = functools.partial(lax.ppermute, axis_name="local", perm=[(0, 1), (1, 0)])
    weights = [*map(in_hbm, own), *map(swap, own)]

    def along(block, pairs):
        moves = [(2 * a + y, 2 * b + y) for a, b in pairs for y in range(2)]
        return lax.ppermute(block, "node", moves)

    def across(block):
        return lax.ppermute(block, "node", [(n, n ^ 1) for n in range(experts)])

    def pick(blocks, users, after=(), cost=0):
        rows = hbm if len(blocks) == 1 else bf16
        return call(
            functools.partial(pick_kernel, users),
            [bf16((count, cap)), bf16((count, cap)), rows((cap, wide)), rows((cap, wide))],
            blocks,
            after,
            [pltpu.VMEM((count, wide), jnp.bfloat16), pltpu.SemaphoreType.DMA],
            [ANYWHERE] * len(blocks),
            cost=cost,
        )

    def expert(rows, after=(), cost=0):
        tiles = 2 * hidden // size
        return call(
            functools.partial(expert_kernel, experts, len(rows)),
            [bf16((cap, width))] * len(rows),
            [*rows, *weights],
            after,
            [
                pltpu.VMEM((len(rows) * cap, width), jnp.bfloat16),
                pltpu.VMEM((len(rows) * cap, 2 * hidden), jnp.bfloat16),
                pltpu.VMEM((tiles, width, size), jnp.bfloat16),
                pltpu.VMEM((tiles, width, size), jnp.bfloat16),
                pltpu.VMEM((2, hidden, width), jnp.bfloat16),
                pltpu.SemaphoreType.DMA((tiles, 3)),
            ],
            [IN_VMEM] * len(rows) + [ANYWHERE] * 6,
            32,
            cost=cost,
        )

    def spread(maps, own_out, other_out, extras=(), after=(), cost=0):
        ins = [*maps, own_out, other_out, *extras]
        return call(spread_kernel, [bf16((count, width))], ins, after, cost=cost)[0]

    plan = arrivals(places)
    held = {}

    last = []

    def ordered(function, *args, after=(), **options):
        out = function(*args, after=(*last, *after), **options)
        last[:] = [out[0] if isinstance(out, (list, tuple)) else out]
        return out

    picks, outs, returned = {}, {}, []

    def relay(step):
        for way in (1, -1):
            pairs = [
                (a, a + way)
                for a in range(places)
                if 0 <= a + way < places and 0 <= a - way * (step - 1) < places
            ]
            held[way, step] = along(held.get((way, step - 1), block), pairs)

    def do_pick(slot, after=(), cost=0):
        if slot == 0:
            *maps, own_rows, other_rows = ordered(pick, [block], [range(places)], after=after)
            picks[0] = maps, own_rows, across(other_rows)
            return
        keys = sorted({row[slot - 1] for row in plan})
        blocks = [held[key] for key in keys]
        users = [[place for place, row in enumerate(plan) if row[slot - 1] == key] for key in keys]
        *maps, own_rows, other_rows = ordered(pick, blocks, users, after=after, cost=cost)
        picks[slot] = maps, own_rows, across(other_rows)

    def do_expert(slot, after=(), cost=0):
        own_out, other_out = ordered(expert, picks[slot][1:], after=after, cost=cost)
        outs[slot] = own_out, across(other_out)

    def origin(place, slot):
        way, step = plan[place][slot - 1]
        return place - way * step

    final = places - 1
    hops = [
        (a, b)
        for a, b in ((0, 1), (places - 1, places - 2))
        if origin(a, final) == origin(b, final) and origin(b, final) not in (a, b)
    ]
    staying = {place for hop in hops for place in hop}
    kept, halves = {}, []

    def spread_halves(maps, own_out, other_out, after=()):
        outs = [bf16((count, width)), bf16((count, width // 2)), bf16((count, width // 2))]
        return call(halves_kernel, outs, [*maps, own_out, other_out], after)

    def do_spread(slot, after=(), cost=0):
        if slot == places - 1:
            done, *halves[:] = ordered(spread_halves, picks[slot][0], *outs[slot], after=after)
        else:
            done = ordered(spread, picks[slot][0], *outs[slot], after=after, cost=cost)
        kept[slot] = done
        home = [(a, origin(a, slot)) for a in range(places) if slot < final or a not in staying]
        rounds = []
        while home:
            now = list({b: (a, b) for a, b in home}.values())
            home = [pair for pair in home if pair not in now]
            rounds.append(along(done, now))
        returned.append(rounds)

    def call_sum(blocks, after=(), cost=0):
        return call(sum_kernel, [bf16((count, width))], blocks, after, cost=cost)

    def join(whole, half, index, after=()):
        return call(functools.partial(join_kernel, index), [bf16(half.shape)], [whole, half], after)[0]

    def finish(whole, parts, summed):
        while len(whole) > 8:
            merged = sum(array.astype(jnp.float32) for array in whole[:8])
            whole = [merged.astype(jnp.bfloat16), *whole[8:]]
        low = ordered(finish_low, whole, parts[0])
        total = ordered(spread, picks[0][0], *outs[0], [summed])
        return call(finish_kernel, [bf16((count, width))], [total, *whole, low, parts[1]])[0]

    def finish_low(whole, half, after=()):
        return call(low_kernel, [bf16(half.shape)], [*whole, half], after, cost=128 * MIB)[0]

    relay(1)
    relay(2)
    do_pick(1, after=weights[3:4])
    do_pick(0)
    do_expert(1, cost=64 * MIB)
    held[1, 2], held[-1, 2] = call(
        passing_kernel, [bf16((count, wide))] * 2, [held[1, 2], held[-1, 2]], [*last, picks[1][2]]
    )
    for step in range(3, places):
        relay(step)
    do_pick(2)
    do_spread(1, cost=64 * MIB)
    do_pick(3)
    do_expert(2)
    for slot in range(3, places):
        do_expert(slot)
        do_spread(slot - 1, after=returned[slot - 3])
        if slot + 1 < places:
            do_pick(slot + 1)
    (own_out,) = ordered(expert, picks[0][1:2])
    do_spread(places - 1)
    (other_out,) = ordered(expert, picks[0][2:])
    outs[0] = own_out, across(other_out)
    near = returned.pop(places - 3)
    (summed,) = ordered(call_sum, [*returned.pop(0), *near] if places > 3 else near, cost=128 * MIB)
    homes = [(q, origin(q, final)) for _, q in hops]
    parts = []
    for arrived in [along(half, hops) for half in halves]:
        parts.append(along(ordered(join, kept[final], arrived, len(parts)), homes))
    return finish(sum(returned, []), parts, summed)


def solution(mesh):
    placed = (
        P(("groups", "node", "local"), None),
        P(("groups", "node", "local"), None),
        P(("groups", "node", "local"), None),
        P("node", None, "local"),
        P("node", None, "local"),
        P("node", "local", None),
    )
    return jax.shard_map(
        on_device,
        mesh=mesh,
        in_specs=placed,
        out_specs=P(("groups", "node", "local"), None),
        check_vma=False,
    )
```

```python
import functools

import jax
import jax.numpy as jnp
from jax import lax
from jax.experimental import pallas as pl
from jax.experimental.pallas import tpu as pltpu
from jax.sharding import PartitionSpec as P

ANYWHERE = pl.BlockSpec(memory_space=pl.ANY)
IN_VMEM = pl.BlockSpec(memory_space=pltpu.VMEM)
MIB = 1024 * 1024


def arrivals(places):
    plan = []
    for place in range(places):
        ways = (-1, 1) if place < places // 2 else (1, -1)
        steps = [(way, step) for step in range(1, places) for way in ways]
        plan.append([(way, step) for way, step in steps if 0 <= place - way * step < places])
    return plan


def call(kernel, outs, ins, after=(), scratch=(), specs=None, vmem=16, out_specs=None, cost=0):
    body = kernel
    if after:
        first, last = len(ins), len(ins) + len(after)

        def body(*refs):
            kernel(*refs[:first], *refs[last:])

    specs = list(specs or [IN_VMEM] * len(ins)) + [ANYWHERE] * len(after)
    return pl.pallas_call(
        body,
        out_shape=outs,
        in_specs=specs,
        out_specs=out_specs or [IN_VMEM] * len(outs),
        scratch_shapes=scratch,
        compiler_params=pltpu.CompilerParams(vmem_limit_bytes=vmem * MIB),
        cost_estimate=pl.CostEstimate(flops=0, bytes_accessed=cost, transcendentals=0),
    )(*ins, *after)


def in_vmem(array):
    return pltpu.with_memory_space_constraint(array, pltpu.VMEM)


def tied(arrays, after):
    return pl.pallas_call(
        lambda *refs: None,
        out_shape=[jax.ShapeDtypeStruct(a.shape, a.dtype) for a in arrays],
        in_specs=[ANYWHERE] * (len(arrays) + len(after)),
        out_specs=[ANYWHERE] * len(arrays),
        input_output_aliases={k: k for k in range(len(arrays))},
        cost_estimate=pl.CostEstimate(flops=0, bytes_accessed=0, transcendentals=0),
    )(*[in_vmem(a) for a in arrays], *after)


def mark_kernel(experts, tokens, routes, scale, block, route_held, scale_held, sems):
    count, width = tokens.shape
    ins = [
        pltpu.make_async_copy(routes, route_held, sems.at[0]),
        pltpu.make_async_copy(scale, scale_held, sems.at[1]),
        pltpu.make_async_copy(tokens, block.at[:, :width], sems.at[2]),
    ]
    for copy in ins:
        copy.start()
    for copy in ins[:2]:
        copy.wait()
    lane = lax.broadcasted_iota(jnp.int32, (count, block.shape[1] - width), 1)
    expert, part = lax.rem(lane, experts), lax.div(lane, experts)
    weight = jnp.zeros(lane.shape, jnp.float32)
    routes, scale = route_held[...].T, scale_held[...].T
    for r in range(routes.shape[1]):
        weight += jnp.where(routes[:, r : r + 1] == expert, scale[:, r : r + 1], 0.0)
    high = weight.astype(jnp.bfloat16).astype(jnp.float32)
    middle = (weight - high).astype(jnp.bfloat16).astype(jnp.float32)
    low = weight - high - middle
    marks = jnp.where(part == 0, high, jnp.where(part == 1, middle, jnp.where(part == 2, low, 0.0)))
    block[:, width:] = marks.astype(jnp.bfloat16)
    ins[2].wait()


def passing_kernel(*refs):
    for source, result in zip(refs, refs[len(refs) // 2 :]):
        result[...] = source[...]


def choose(held, own_map, other_map, own_rows, other_rows):
    node = lax.axis_index("node")
    count, cap = own_map.shape
    marks = held[:, held.shape[1] - 128 :].astype(jnp.float32)
    lane = lax.broadcasted_iota(jnp.int32, marks.shape, 1)
    earlier = lax.broadcasted_iota(jnp.int32, (count, count), 0) > lax.broadcasted_iota(jnp.int32, (count, count), 1)
    named = jnp.where(marks != 0, 1.0, 0.0)
    rank = jnp.dot(
        jnp.where(earlier, 1.0, 0.0).astype(jnp.bfloat16), named.astype(jnp.bfloat16), preferred_element_type=jnp.float32
    )
    place = jnp.where(named > 0, rank, -1.0)
    slot = lax.broadcasted_iota(jnp.int32, (count, cap), 1)
    for expert, one_hot, rows in ((node, own_map, own_rows), (node ^ 1, other_map, other_rows)):
        mine = jnp.sum(jnp.where(lane == expert, place, 0.0), axis=1, keepdims=True).astype(jnp.int32)
        chosen = jnp.where(mine == slot, 1.0, 0.0).astype(jnp.bfloat16)
        one_hot[...] = chosen
        rows[...] = lax.dot_general(
            chosen, held[...], (((0,), (0,)), ((), ())), preferred_element_type=jnp.float32
        ).astype(jnp.bfloat16)


def pick_kernel(users, *refs):
    blocks, (held, sem) = refs[: len(users)], refs[len(users) + 4 :]
    node = lax.axis_index("node")
    for block, places in zip(blocks, users):
        here = functools.reduce(jnp.logical_or, [lax.div(node, 2) == place for place in places])

        @pl.when(here)
        def _():
            copy = pltpu.make_async_copy(block, held, sem)
            copy.start()
            copy.wait()

    choose(held, *refs[len(users) : len(users) + 4])


def expert_kernel(experts, count, *refs):
    marked, weights, outs = refs[:count], refs[count : count + 6], refs[count + 6 : 2 * count + 6]
    rows, hidden, gates, ups, downs, sems = refs[2 * count + 6 :]
    cap, width = outs[0].shape
    tiles, _, size = gates.shape
    each = tiles // 2
    queue = []
    for tile in range(tiles):
        part = pl.ds(tile % each * size, size)
        gate_w, up_w = weights[tile // each * 3 : tile // each * 3 + 2]
        queue.append(pltpu.make_async_copy(gate_w.at[:, part], gates.at[tile], sems.at[tile, 0]))
        queue.append(pltpu.make_async_copy(up_w.at[:, part], ups.at[tile], sems.at[tile, 1]))
    for half, down in enumerate(weights[2::3]):
        queue.append(pltpu.make_async_copy(down, downs.at[half], sems.at[half, 2]))
    ahead = iter(queue[4:])
    for copy in queue[:4]:
        copy.start()

    def arrived(copy):
        copy.wait()
        for following in ahead:
            following.start()
            break

    for k, source in enumerate(marked):
        rows[k * cap : (k + 1) * cap] = source[:, :width]
    for tile in range(tiles):
        arrived(queue[2 * tile])
        gate = jnp.dot(rows[...], gates[tile], preferred_element_type=jnp.float32)
        arrived(queue[2 * tile + 1])
        up = jnp.dot(rows[...], ups[tile], preferred_element_type=jnp.float32)
        hidden[:, tile * size : (tile + 1) * size] = (gate / (1.0 + jnp.exp(-gate)) * up).astype(jnp.bfloat16)
    arrived(queue[-2])
    arrived(queue[-1])
    node = lax.axis_index("node")
    scales = []
    for source in marked:
        marks = source[:, width:].astype(jnp.float32)
        lane = lax.broadcasted_iota(jnp.int32, marks.shape, 1)
        mine = (lax.rem(lane, experts) == node) & (lane < 3 * experts)
        scales.append(jnp.sum(jnp.where(mine, marks, 0.0), axis=1, keepdims=True))
    step = 512 if width % 512 == 0 else width
    for start in range(0, width, step):
        cut = slice(start, start + step)
        out = jnp.dot(hidden[:, : each * size], downs[0, :, cut], preferred_element_type=jnp.float32)
        out += jnp.dot(hidden[:, each * size :], downs[1, :, cut], preferred_element_type=jnp.float32)
        for k, result in enumerate(outs):
            result[:, cut] = (out[k * cap : (k + 1) * cap] * scales[k]).astype(jnp.bfloat16)


def spread_kernel(own_map, other_map, own_out, other_out, *refs):
    result = refs[-1]
    total = jnp.dot(own_map[...], own_out[...], preferred_element_type=jnp.float32)
    total += jnp.dot(other_map[...], other_out[...], preferred_element_type=jnp.float32)
    for extra in refs[:-1]:
        total += extra[...].astype(jnp.float32)
    result[...] = total.astype(jnp.bfloat16)


def sum_kernel(*refs):
    total = refs[0][...].astype(jnp.float32)
    for extra in refs[1:-1]:
        total += extra[...].astype(jnp.float32)
    refs[-1][...] = total.astype(jnp.bfloat16)


def join_kernel(index, whole, half, result):
    size = half.shape[1]
    total = whole[:, index * size : (index + 1) * size].astype(jnp.float32) + half[...].astype(jnp.float32)
    result[...] = total.astype(jnp.bfloat16)


def halves_kernel(*refs):
    spread_kernel(*refs[:-2])
    size = refs[-1].shape[1]
    refs[-2][...] = refs[-3][:, :size]
    refs[-1][...] = refs[-3][:, size:]


def low_kernel(*refs):
    *whole, low, result = refs
    size = low.shape[1]
    total = low[...].astype(jnp.float32)
    for extra in whole:
        total += extra[:, :size].astype(jnp.float32)
    result[...] = total.astype(jnp.bfloat16)


def finish_kernel(total, *refs):
    *whole, low, high, result = refs
    size = low.shape[1]
    result[:, :size] = (low[...].astype(jnp.float32) + total[:, :size].astype(jnp.float32)).astype(jnp.bfloat16)
    rest = high[...].astype(jnp.float32) + total[:, size:].astype(jnp.float32)
    for extra in whole:
        rest += extra[:, size:].astype(jnp.float32)
    result[:, size:] = rest.astype(jnp.bfloat16)


def on_device(tokens, routes, route_scale, w_gate, w_up, w_down):
    count, width = tokens.shape
    experts = lax.axis_size("node")
    places = experts // 2
    hidden = w_gate.shape[2]
    size = min(hidden, 256)
    cap = -(-(5 * count // experts) // 16) * 16
    wide = width + -(-3 * experts // 128) * 128
    hbm = functools.partial(pltpu.HBM, dtype=jnp.bfloat16)
    in_hbm = functools.partial(pltpu.with_memory_space_constraint, memory_space=pltpu.HBM)
    bf16 = functools.partial(jax.ShapeDtypeStruct, dtype=jnp.bfloat16)

    own = (w_gate[0], w_up[0], w_down[0])
    (block,) = call(
        functools.partial(mark_kernel, experts),
        [bf16((count, wide))],
        [*map(in_hbm, (tokens, routes.T, route_scale.T))],
        (),
        [
            pltpu.VMEM(routes.shape[::-1], routes.dtype),
            pltpu.VMEM(routes.shape[::-1], route_scale.dtype),
            pltpu.SemaphoreType.DMA((3,)),
        ],
        [ANYWHERE] * 3,
    )
    swap = functools.partial(lax.ppermute, axis_name="local", perm=[(0, 1), (1, 0)])
    weights = [*map(in_hbm, own), *map(swap, own)]

    def along(block, pairs):
        moves = [(2 * a + y, 2 * b + y) for a, b in pairs for y in range(2)]
        return lax.ppermute(block, "node", moves)

    def across(block):
        return lax.ppermute(block, "node", [(n, n ^ 1) for n in range(experts)])

    def pick(blocks, users, after=(), cost=0):
        rows = hbm if len(blocks) == 1 else bf16
        return call(
            functools.partial(pick_kernel, users),
            [bf16((count, cap)), bf16((count, cap)), rows((cap, wide)), rows((cap, wide))],
            blocks,
            after,
            [pltpu.VMEM((count, wide), jnp.bfloat16), pltpu.SemaphoreType.DMA],
            [ANYWHERE] * len(blocks),
            cost=cost,
        )

    def expert(rows, after=(), cost=0):
        tiles = 2 * hidden // size
        return call(
            functools.partial(expert_kernel, experts, len(rows)),
            [bf16((cap, width))] * len(rows),
            [*rows, *weights],
            after,
            [
                pltpu.VMEM((len(rows) * cap, width), jnp.bfloat16),
                pltpu.VMEM((len(rows) * cap, 2 * hidden), jnp.bfloat16),
                pltpu.VMEM((tiles, width, size), jnp.bfloat16),
                pltpu.VMEM((tiles, width, size), jnp.bfloat16),
                pltpu.VMEM((2, hidden, width), jnp.bfloat16),
                pltpu.SemaphoreType.DMA((tiles, 3)),
            ],
            [IN_VMEM] * len(rows) + [ANYWHERE] * 6,
            32,
            cost=cost,
        )

    def spread(maps, own_out, other_out, extras=(), after=(), cost=0):
        ins = [*maps, own_out, other_out, *extras]
        return call(spread_kernel, [bf16((count, width))], ins, after, cost=cost)[0]

    plan = arrivals(places)
    held = {}

    last = []

    def ordered(function, *args, after=(), **options):
        out = function(*args, after=(*last, *after), **options)
        last[:] = [out[0] if isinstance(out, (list, tuple)) else out]
        return out

    picks, outs, returned = {}, {}, []

    def relay(step):
        for way in (1, -1):
            pairs = [
                (a, a + way)
                for a in range(places)
                if 0 <= a + way < places and 0 <= a - way * (step - 1) < places
            ]
            held[way, step] = along(held.get((way, step - 1), block), pairs)

    def do_pick(slot, after=(), cost=0):
        if slot == 0:
            *maps, own_rows, other_rows = ordered(pick, [block], [range(places)], after=after)
            picks[0] = maps, own_rows, across(other_rows)
            return
        keys = sorted({row[slot - 1] for row in plan})
        blocks = [held[key] for key in keys]
        users = [[place for place, row in enumerate(plan) if row[slot - 1] == key] for key in keys]
        *maps, own_rows, other_rows = ordered(pick, blocks, users, after=after, cost=cost)
        picks[slot] = maps, own_rows, across(other_rows)

    def do_expert(slot, after=(), cost=0):
        own_out, other_out = ordered(expert, picks[slot][1:], after=after, cost=cost)
        outs[slot] = own_out, across(other_out)

    def origin(place, slot):
        way, step = plan[place][slot - 1]
        return place - way * step

    final = places - 1
    hops = [
        (a, b)
        for a, b in ((0, 1), (places - 1, places - 2))
        if origin(a, final) == origin(b, final) and origin(b, final) not in (a, b)
    ]
    staying = {place for hop in hops for place in hop}
    kept, halves = {}, []

    def spread_halves(maps, own_out, other_out, after=()):
        outs = [bf16((count, width)), bf16((count, width // 2)), bf16((count, width // 2))]
        return call(halves_kernel, outs, [*maps, own_out, other_out], after)

    def do_spread(slot, after=(), cost=0):
        if slot == places - 1:
            done, *halves[:] = ordered(spread_halves, picks[slot][0], *outs[slot], after=after)
        else:
            done = ordered(spread, picks[slot][0], *outs[slot], after=after, cost=cost)
        kept[slot] = done
        home = [(a, origin(a, slot)) for a in range(places) if slot < final or a not in staying]
        rounds = []
        while home:
            now = list({b: (a, b) for a, b in home}.values())
            home = [pair for pair in home if pair not in now]
            rounds.append(along(done, now))
        returned.append(rounds)

    def call_sum(blocks, after=(), cost=0):
        return call(sum_kernel, [bf16((count, width))], blocks, after, cost=cost)

    def join(whole, half, index, after=()):
        return call(functools.partial(join_kernel, index), [bf16(half.shape)], [whole, half], after)[0]

    def finish(whole, parts, summed):
        while len(whole) > 8:
            merged = sum(array.astype(jnp.float32) for array in whole[:8])
            whole = [merged.astype(jnp.bfloat16), *whole[8:]]
        low = ordered(finish_low, whole, parts[0])
        total = ordered(spread, picks[0][0], *outs[0], [summed])
        return call(finish_kernel, [bf16((count, width))], [total, *whole, low, parts[1]])[0]

    def finish_low(whole, half, after=()):
        return call(low_kernel, [bf16(half.shape)], [*whole, half], after, cost=128 * MIB)[0]

    relay(1)
    relay(2)
    do_pick(1, after=weights[3:4])
    do_pick(0)
    do_expert(1, cost=64 * MIB)
    held[1, 2], held[-1, 2] = call(
        passing_kernel, [bf16((count, wide))] * 2, [held[1, 2], held[-1, 2]], [*last, picks[1][2]]
    )
    for step in range(3, places):
        relay(step)
    do_pick(2, after=[picks[0][2]])
    do_expert(0)
    do_spread(1, cost=64 * MIB)
    do_pick(3)
    do_expert(2)
    for slot in range(3, places):
        do_expert(slot)
        do_spread(slot - 1, after=returned[slot - 3])
        if slot + 1 < places:
            do_pick(slot + 1)
    do_spread(places - 1)
    near = returned.pop(places - 3)
    (summed,) = ordered(call_sum, [*returned.pop(0), *near] if places > 3 else near, cost=128 * MIB)
    homes = [(q, origin(q, final)) for _, q in hops]
    parts = []
    for arrived in [along(half, hops) for half in halves]:
        parts.append(along(ordered(join, kept[final], arrived, len(parts)), homes))
    return finish(sum(returned, []), parts, summed)


def solution(mesh):
    placed = (
        P(("groups", "node", "local"), None),
        P(("groups", "node", "local"), None),
        P(("groups", "node", "local"), None),
        P("node", None, "local"),
        P("node", None, "local"),
        P("node", "local", None),
    )
    return jax.shard_map(
        on_device,
        mesh=mesh,
        in_specs=placed,
        out_specs=P(("groups", "node", "local"), None),
        check_vma=False,
    )
```

```python
import functools

import jax
import jax.numpy as jnp
from jax import lax
from jax.experimental import pallas as pl
from jax.experimental.pallas import tpu as pltpu
from jax.sharding import PartitionSpec as P

ANYWHERE = pl.BlockSpec(memory_space=pl.ANY)
IN_VMEM = pl.BlockSpec(memory_space=pltpu.VMEM)
MIB = 1024 * 1024


def arrivals(places):
    plan = []
    for place in range(places):
        ways = (-1, 1) if place < places // 2 else (1, -1)
        steps = [(way, step) for step in range(1, places) for way in ways]
        plan.append([(way, step) for way, step in steps if 0 <= place - way * step < places])
    return plan


def call(kernel, outs, ins, after=(), scratch=(), specs=None, vmem=16, out_specs=None, cost=0):
    body = kernel
    if after:
        first, last = len(ins), len(ins) + len(after)

        def body(*refs):
            kernel(*refs[:first], *refs[last:])

    specs = list(specs or [IN_VMEM] * len(ins)) + [ANYWHERE] * len(after)
    return pl.pallas_call(
        body,
        out_shape=outs,
        in_specs=specs,
        out_specs=out_specs or [IN_VMEM] * len(outs),
        scratch_shapes=scratch,
        compiler_params=pltpu.CompilerParams(vmem_limit_bytes=vmem * MIB),
        cost_estimate=pl.CostEstimate(flops=0, bytes_accessed=cost, transcendentals=0),
    )(*ins, *after)


def in_vmem(array):
    return pltpu.with_memory_space_constraint(array, pltpu.VMEM)


def tied(arrays, after):
    return pl.pallas_call(
        lambda *refs: None,
        out_shape=[jax.ShapeDtypeStruct(a.shape, a.dtype) for a in arrays],
        in_specs=[ANYWHERE] * (len(arrays) + len(after)),
        out_specs=[ANYWHERE] * len(arrays),
        input_output_aliases={k: k for k in range(len(arrays))},
        cost_estimate=pl.CostEstimate(flops=0, bytes_accessed=0, transcendentals=0),
    )(*[in_vmem(a) for a in arrays], *after)


def mark_kernel(experts, tokens, routes, scale, block, route_held, scale_held, sems):
    count, width = tokens.shape
    ins = [
        pltpu.make_async_copy(routes, route_held, sems.at[0]),
        pltpu.make_async_copy(scale, scale_held, sems.at[1]),
        pltpu.make_async_copy(tokens, block.at[:, :width], sems.at[2]),
    ]
    for copy in ins:
        copy.start()
    for copy in ins[:2]:
        copy.wait()
    lane = lax.broadcasted_iota(jnp.int32, (count, block.shape[1] - width), 1)
    expert, part = lax.rem(lane, experts), lax.div(lane, experts)
    weight = jnp.zeros(lane.shape, jnp.float32)
    routes, scale = route_held[...].T, scale_held[...].T
    for r in range(routes.shape[1]):
        weight += jnp.where(routes[:, r : r + 1] == expert, scale[:, r : r + 1], 0.0)
    high = weight.astype(jnp.bfloat16).astype(jnp.float32)
    middle = (weight - high).astype(jnp.bfloat16).astype(jnp.float32)
    low = weight - high - middle
    marks = jnp.where(part == 0, high, jnp.where(part == 1, middle, jnp.where(part == 2, low, 0.0)))
    block[:, width:] = marks.astype(jnp.bfloat16)
    ins[2].wait()


def passing_kernel(*refs):
    for source, result in zip(refs, refs[len(refs) // 2 :]):
        result[...] = source[...]


def choose(held, own_map, other_map, scales, own_rows, other_rows):
    node = lax.axis_index("node")
    count, cap = own_map.shape
    marks = held[:, held.shape[1] - 128 :].astype(jnp.float32)
    lane = lax.broadcasted_iota(jnp.int32, marks.shape, 1)
    earlier = lax.broadcasted_iota(jnp.int32, (count, count), 0) > lax.broadcasted_iota(jnp.int32, (count, count), 1)
    named = jnp.where(marks != 0, 1.0, 0.0)
    rank = jnp.dot(
        jnp.where(earlier, 1.0, 0.0).astype(jnp.bfloat16), named.astype(jnp.bfloat16), preferred_element_type=jnp.float32
    )
    place = jnp.where(named > 0, rank, -1.0)
    slot = lax.broadcasted_iota(jnp.int32, (count, cap), 1)
    scales[...] = jnp.zeros(scales.shape, jnp.float32)
    width, experts = own_rows.shape[1], lax.axis_size("node")
    for k, (expert, one_hot, rows) in enumerate(((node, own_map, own_rows), (node ^ 1, other_map, other_rows))):
        parts = (lax.rem(lane, experts) == expert) & (lane < 3 * experts)
        scales[:, k : k + 1] = jnp.sum(jnp.where(parts, marks, 0.0), axis=1, keepdims=True)
        mine = jnp.sum(jnp.where(lane == expert, place, 0.0), axis=1, keepdims=True).astype(jnp.int32)
        chosen = jnp.where(mine == slot, 1.0, 0.0).astype(jnp.bfloat16)
        one_hot[...] = chosen
        rows[...] = lax.dot_general(
            chosen, held[:, :width], (((0,), (0,)), ((), ())), preferred_element_type=jnp.float32
        ).astype(jnp.bfloat16)


def pick_kernel(users, *refs):
    blocks, (held, sem) = refs[: len(users)], refs[len(users) + 5 :]
    node = lax.axis_index("node")
    for block, places in zip(blocks, users):
        here = functools.reduce(jnp.logical_or, [lax.div(node, 2) == place for place in places])

        @pl.when(here)
        def _():
            copy = pltpu.make_async_copy(block, held, sem)
            copy.start()
            copy.wait()

    choose(held, *refs[len(users) : len(users) + 5])


def expert_kernel(count, *refs):
    marked, weights, outs = refs[:count], refs[count : count + 6], refs[count + 6 : 2 * count + 6]
    rows, hidden, gates, ups, downs, sems = refs[2 * count + 6 :]
    cap, width = outs[0].shape
    tiles, _, size = gates.shape
    each = tiles // 2
    queue = []
    for tile in range(tiles):
        part = pl.ds(tile % each * size, size)
        gate_w, up_w = weights[tile // each * 3 : tile // each * 3 + 2]
        queue.append(pltpu.make_async_copy(gate_w.at[:, part], gates.at[tile], sems.at[tile, 0]))
        queue.append(pltpu.make_async_copy(up_w.at[:, part], ups.at[tile], sems.at[tile, 1]))
    for half, down in enumerate(weights[2::3]):
        queue.append(pltpu.make_async_copy(down, downs.at[half], sems.at[half, 2]))
    ahead = iter(queue[4:])
    for copy in queue[:4]:
        copy.start()

    def arrived(copy):
        copy.wait()
        for following in ahead:
            following.start()
            break

    for k, source in enumerate(marked):
        rows[k * cap : (k + 1) * cap] = source[...]
    for tile in range(tiles):
        arrived(queue[2 * tile])
        gate = jnp.dot(rows[...], gates[tile], preferred_element_type=jnp.float32)
        arrived(queue[2 * tile + 1])
        up = jnp.dot(rows[...], ups[tile], preferred_element_type=jnp.float32)
        hidden[:, tile * size : (tile + 1) * size] = (gate / (1.0 + jnp.exp(-gate)) * up).astype(jnp.bfloat16)
    arrived(queue[-2])
    arrived(queue[-1])
    step = 512 if width % 512 == 0 else width
    for start in range(0, width, step):
        cut = slice(start, start + step)
        out = jnp.dot(hidden[:, : each * size], downs[0, :, cut], preferred_element_type=jnp.float32)
        out += jnp.dot(hidden[:, each * size :], downs[1, :, cut], preferred_element_type=jnp.float32)
        for k, result in enumerate(outs):
            result[:, cut] = out[k * cap : (k + 1) * cap].astype(jnp.bfloat16)


def spread_kernel(own_map, other_map, scales, own_out, other_out, *refs):
    result = refs[-1]
    total = jnp.dot(own_map[...], own_out[...], preferred_element_type=jnp.float32) * scales[:, :1]
    total += jnp.dot(other_map[...], other_out[...], preferred_element_type=jnp.float32) * scales[:, 1:2]
    for extra in refs[:-1]:
        total += extra[...].astype(jnp.float32)
    result[...] = total.astype(jnp.bfloat16)


def sum_kernel(*refs):
    total = refs[0][...].astype(jnp.float32)
    for extra in refs[1:-1]:
        total += extra[...].astype(jnp.float32)
    refs[-1][...] = total.astype(jnp.bfloat16)


def join_kernel(index, whole, half, result):
    size = half.shape[1]
    total = whole[:, index * size : (index + 1) * size].astype(jnp.float32) + half[...].astype(jnp.float32)
    result[...] = total.astype(jnp.bfloat16)


def halves_kernel(*refs):
    spread_kernel(*refs[:-2])
    size = refs[-1].shape[1]
    refs[-2][...] = refs[-3][:, :size]
    refs[-1][...] = refs[-3][:, size:]


def low_kernel(*refs):
    *whole, low, result = refs
    size = low.shape[1]
    total = low[...].astype(jnp.float32)
    for extra in whole:
        total += extra[:, :size].astype(jnp.float32)
    result[...] = total.astype(jnp.bfloat16)


def finish_kernel(total, *refs):
    *whole, low, high, result = refs
    size = low.shape[1]
    result[:, :size] = (low[...].astype(jnp.float32) + total[:, :size].astype(jnp.float32)).astype(jnp.bfloat16)
    rest = high[...].astype(jnp.float32) + total[:, size:].astype(jnp.float32)
    for extra in whole:
        rest += extra[:, size:].astype(jnp.float32)
    result[:, size:] = rest.astype(jnp.bfloat16)


def on_device(tokens, routes, route_scale, w_gate, w_up, w_down):
    count, width = tokens.shape
    experts = lax.axis_size("node")
    places = experts // 2
    hidden = w_gate.shape[2]
    size = min(hidden, 256)
    cap = -(-(5 * count // experts) // 16) * 16
    wide = width + -(-3 * experts // 128) * 128
    hbm = functools.partial(pltpu.HBM, dtype=jnp.bfloat16)
    in_hbm = functools.partial(pltpu.with_memory_space_constraint, memory_space=pltpu.HBM)
    bf16 = functools.partial(jax.ShapeDtypeStruct, dtype=jnp.bfloat16)

    own = (w_gate[0], w_up[0], w_down[0])
    (block,) = call(
        functools.partial(mark_kernel, experts),
        [bf16((count, wide))],
        [*map(in_hbm, (tokens, routes.T, route_scale.T))],
        (),
        [
            pltpu.VMEM(routes.shape[::-1], routes.dtype),
            pltpu.VMEM(routes.shape[::-1], route_scale.dtype),
            pltpu.SemaphoreType.DMA((3,)),
        ],
        [ANYWHERE] * 3,
    )
    swap = functools.partial(lax.ppermute, axis_name="local", perm=[(0, 1), (1, 0)])
    weights = [*map(in_hbm, own), *map(swap, own)]

    def along(block, pairs):
        moves = [(2 * a + y, 2 * b + y) for a, b in pairs for y in range(2)]
        return lax.ppermute(block, "node", moves)

    def across(block):
        return lax.ppermute(block, "node", [(n, n ^ 1) for n in range(experts)])

    def pick(blocks, users, after=(), cost=0):
        rows = hbm if len(blocks) == 1 else bf16
        factors = jax.ShapeDtypeStruct((count, 128), jnp.float32)
        return call(
            functools.partial(pick_kernel, users),
            [bf16((count, cap)), bf16((count, cap)), factors, rows((cap, width)), rows((cap, width))],
            blocks,
            after,
            [pltpu.VMEM((count, wide), jnp.bfloat16), pltpu.SemaphoreType.DMA],
            [ANYWHERE] * len(blocks),
            cost=cost,
        )

    def expert(rows, after=(), cost=0):
        tiles = 2 * hidden // size
        return call(
            functools.partial(expert_kernel, len(rows)),
            [bf16((cap, width))] * len(rows),
            [*rows, *weights],
            after,
            [
                pltpu.VMEM((len(rows) * cap, width), jnp.bfloat16),
                pltpu.VMEM((len(rows) * cap, 2 * hidden), jnp.bfloat16),
                pltpu.VMEM((tiles, width, size), jnp.bfloat16),
                pltpu.VMEM((tiles, width, size), jnp.bfloat16),
                pltpu.VMEM((2, hidden, width), jnp.bfloat16),
                pltpu.SemaphoreType.DMA((tiles, 3)),
            ],
            [IN_VMEM] * len(rows) + [ANYWHERE] * 6,
            32,
            cost=cost,
        )

    def spread(maps, own_out, other_out, extras=(), after=(), cost=0):
        ins = [*maps, own_out, other_out, *extras]
        return call(spread_kernel, [bf16((count, width))], ins, after, cost=cost)[0]

    plan = arrivals(places)
    held = {}

    last = []

    def ordered(function, *args, after=(), **options):
        out = function(*args, after=(*last, *after), **options)
        last[:] = [out[0] if isinstance(out, (list, tuple)) else out]
        return out

    picks, outs, returned = {}, {}, []

    def relay(step):
        for way in (1, -1):
            pairs = [
                (a, a + way)
                for a in range(places)
                if 0 <= a + way < places and 0 <= a - way * (step - 1) < places
            ]
            held[way, step] = along(held.get((way, step - 1), block), pairs)

    def do_pick(slot, after=(), cost=0):
        if slot == 0:
            *maps, own_rows, other_rows = ordered(pick, [block], [range(places)], after=after)
            picks[0] = maps, own_rows, across(other_rows)
            return
        keys = sorted({row[slot - 1] for row in plan})
        blocks = [held[key] for key in keys]
        users = [[place for place, row in enumerate(plan) if row[slot - 1] == key] for key in keys]
        *maps, own_rows, other_rows = ordered(pick, blocks, users, after=after, cost=cost)
        picks[slot] = maps, own_rows, across(other_rows)

    def do_expert(slot, after=(), cost=0):
        own_out, other_out = ordered(expert, picks[slot][1:], after=after, cost=cost)
        outs[slot] = own_out, across(other_out)

    def origin(place, slot):
        way, step = plan[place][slot - 1]
        return place - way * step

    final = places - 1
    hops = [
        (a, b)
        for a, b in ((0, 1), (places - 1, places - 2))
        if origin(a, final) == origin(b, final) and origin(b, final) not in (a, b)
    ]
    staying = {place for hop in hops for place in hop}
    kept, halves = {}, []

    def spread_halves(maps, own_out, other_out, after=()):
        outs = [bf16((count, width)), bf16((count, width // 2)), bf16((count, width // 2))]
        return call(halves_kernel, outs, [*maps, own_out, other_out], after)

    def do_spread(slot, after=(), cost=0):
        if slot == places - 1:
            done, *halves[:] = ordered(spread_halves, picks[slot][0], *outs[slot], after=after)
        else:
            done = ordered(spread, picks[slot][0], *outs[slot], after=after, cost=cost)
        kept[slot] = done
        home = [(a, origin(a, slot)) for a in range(places) if slot < final or a not in staying]
        rounds = []
        while home:
            now = list({b: (a, b) for a, b in home}.values())
            home = [pair for pair in home if pair not in now]
            rounds.append(along(done, now))
        returned.append(rounds)

    def call_sum(blocks, after=(), cost=0):
        return call(sum_kernel, [bf16((count, width))], blocks, after, cost=cost)

    def join(whole, half, index, after=()):
        return call(functools.partial(join_kernel, index), [bf16(half.shape)], [whole, half], after)[0]

    def finish(whole, parts, summed):
        while len(whole) > 8:
            merged = sum(array.astype(jnp.float32) for array in whole[:8])
            whole = [merged.astype(jnp.bfloat16), *whole[8:]]
        low = ordered(finish_low, whole, parts[0])
        total = ordered(spread, picks[0][0], *outs[0], [summed])
        return call(finish_kernel, [bf16((count, width))], [total, *whole, low, parts[1]])[0]

    def finish_low(whole, half, after=()):
        return call(low_kernel, [bf16(half.shape)], [*whole, half], after, cost=128 * MIB)[0]

    relay(1)
    relay(2)
    do_pick(1, after=weights[3:4])
    do_pick(0)
    do_expert(1, cost=64 * MIB)
    held[1, 2], held[-1, 2] = call(
        passing_kernel, [bf16((count, wide))] * 2, [held[1, 2], held[-1, 2]], [*last, picks[1][2]]
    )
    for step in range(3, places):
        relay(step)
    do_pick(2, after=[picks[0][2]])
    do_expert(0)
    do_spread(1, cost=64 * MIB)
    do_pick(3)
    do_expert(2)
    for slot in range(3, places):
        do_expert(slot)
        do_spread(slot - 1, after=returned[slot - 3])
        if slot + 1 < places:
            do_pick(slot + 1)
    do_spread(places - 1)
    near = returned.pop(places - 3)
    (summed,) = ordered(call_sum, [*returned.pop(0), *near] if places > 3 else near, cost=128 * MIB)
    homes = [(q, origin(q, final)) for _, q in hops]
    parts = []
    for arrived in [along(half, hops) for half in halves]:
        parts.append(along(ordered(join, kept[final], arrived, len(parts)), homes))
    return finish(sum(returned, []), parts, summed)


def solution(mesh):
    placed = (
        P(("groups", "node", "local"), None),
        P(("groups", "node", "local"), None),
        P(("groups", "node", "local"), None),
        P("node", None, "local"),
        P("node", None, "local"),
        P("node", "local", None),
    )
    return jax.shard_map(
        on_device,
        mesh=mesh,
        in_specs=placed,
        out_specs=P(("groups", "node", "local"), None),
        check_vma=False,
    )
```

```python
import functools

import jax
import jax.numpy as jnp
from jax import lax
from jax.experimental import pallas as pl
from jax.experimental.pallas import tpu as pltpu
from jax.sharding import PartitionSpec as P

ANYWHERE = pl.BlockSpec(memory_space=pl.ANY)
IN_VMEM = pl.BlockSpec(memory_space=pltpu.VMEM)
MIB = 1024 * 1024


def arrivals(places):
    plan = []
    for place in range(places):
        ways = (-1, 1) if place < places // 2 else (1, -1)
        steps = [(way, step) for step in range(1, places) for way in ways]
        plan.append([(way, step) for way, step in steps if 0 <= place - way * step < places])
    return plan


def call(kernel, outs, ins, after=(), scratch=(), specs=None, vmem=16, out_specs=None, cost=0):
    body = kernel
    if after:
        first, last = len(ins), len(ins) + len(after)

        def body(*refs):
            kernel(*refs[:first], *refs[last:])

    specs = list(specs or [IN_VMEM] * len(ins)) + [ANYWHERE] * len(after)
    return pl.pallas_call(
        body,
        out_shape=outs,
        in_specs=specs,
        out_specs=out_specs or [IN_VMEM] * len(outs),
        scratch_shapes=scratch,
        compiler_params=pltpu.CompilerParams(vmem_limit_bytes=vmem * MIB),
        cost_estimate=pl.CostEstimate(flops=0, bytes_accessed=cost, transcendentals=0),
    )(*ins, *after)


def in_vmem(array):
    return pltpu.with_memory_space_constraint(array, pltpu.VMEM)


def tied(arrays, after):
    return pl.pallas_call(
        lambda *refs: None,
        out_shape=[jax.ShapeDtypeStruct(a.shape, a.dtype) for a in arrays],
        in_specs=[ANYWHERE] * (len(arrays) + len(after)),
        out_specs=[ANYWHERE] * len(arrays),
        input_output_aliases={k: k for k in range(len(arrays))},
        cost_estimate=pl.CostEstimate(flops=0, bytes_accessed=0, transcendentals=0),
    )(*[in_vmem(a) for a in arrays], *after)


def mark_kernel(experts, tokens, routes, scale, block, route_held, scale_held, sems):
    count, width = tokens.shape
    ins = [
        pltpu.make_async_copy(routes, route_held, sems.at[0]),
        pltpu.make_async_copy(scale, scale_held, sems.at[1]),
        pltpu.make_async_copy(tokens, block.at[:, :width], sems.at[2]),
    ]
    for copy in ins:
        copy.start()
    for copy in ins[:2]:
        copy.wait()
    lane = lax.broadcasted_iota(jnp.int32, (count, block.shape[1] - width), 1)
    expert, part = lax.rem(lane, experts), lax.div(lane, experts)
    weight = jnp.zeros(lane.shape, jnp.float32)
    routes, scale = route_held[...].T, scale_held[...].T
    for r in range(routes.shape[1]):
        weight += jnp.where(routes[:, r : r + 1] == expert, scale[:, r : r + 1], 0.0)
    high = weight.astype(jnp.bfloat16).astype(jnp.float32)
    middle = (weight - high).astype(jnp.bfloat16).astype(jnp.float32)
    low = weight - high - middle
    marks = jnp.where(part == 0, high, jnp.where(part == 1, middle, jnp.where(part == 2, low, 0.0)))
    block[:, width:] = marks.astype(jnp.bfloat16)
    ins[2].wait()


def passing_kernel(*refs):
    for source, result in zip(refs, refs[len(refs) // 2 :]):
        result[...] = source[...]


def choose(held, own_map, other_map, scales, own_rows, other_rows):
    node = lax.axis_index("node")
    count, cap = own_map.shape
    marks = held[:, held.shape[1] - 128 :].astype(jnp.float32)
    lane = lax.broadcasted_iota(jnp.int32, marks.shape, 1)
    earlier = lax.broadcasted_iota(jnp.int32, (count, count), 0) > lax.broadcasted_iota(jnp.int32, (count, count), 1)
    named = jnp.where(marks != 0, 1.0, 0.0)
    rank = jnp.dot(
        jnp.where(earlier, 1.0, 0.0).astype(jnp.bfloat16), named.astype(jnp.bfloat16), preferred_element_type=jnp.float32
    )
    place = jnp.where(named > 0, rank, -1.0)
    slot = lax.broadcasted_iota(jnp.int32, (count, cap), 1)
    scales[...] = jnp.zeros(scales.shape, jnp.float32)
    width, experts = own_rows.shape[1], lax.axis_size("node")
    for k, (expert, one_hot, rows) in enumerate(((node, own_map, own_rows), (node ^ 1, other_map, other_rows))):
        parts = (lax.rem(lane, experts) == expert) & (lane < 3 * experts)
        scales[:, k : k + 1] = jnp.sum(jnp.where(parts, marks, 0.0), axis=1, keepdims=True)
        mine = jnp.sum(jnp.where(lane == expert, place, 0.0), axis=1, keepdims=True).astype(jnp.int32)
        chosen = jnp.where(mine == slot, 1.0, 0.0).astype(jnp.bfloat16)
        one_hot[...] = chosen
        rows[...] = lax.dot_general(
            chosen, held[:, :width], (((0,), (0,)), ((), ())), preferred_element_type=jnp.float32
        ).astype(jnp.bfloat16)


def pick_kernel(users, *refs):
    blocks, (held, sem) = refs[: len(users)], refs[len(users) + 5 :]
    node = lax.axis_index("node")
    for block, places in zip(blocks, users):
        here = functools.reduce(jnp.logical_or, [lax.div(node, 2) == place for place in places])

        @pl.when(here)
        def _():
            copy = pltpu.make_async_copy(block, held, sem)
            copy.start()
            copy.wait()

    choose(held, *refs[len(users) : len(users) + 5])


def expert_kernel(count, *refs):
    marked, weights, outs = refs[:count], refs[count : count + 6], refs[count + 6 : 2 * count + 6]
    rows, hidden, gates, ups, downs, sems = refs[2 * count + 6 :]
    cap, width = outs[0].shape
    tiles, _, size = gates.shape
    each = tiles // 2
    queue = []
    for tile in range(tiles):
        part = pl.ds(tile % each * size, size)
        gate_w, up_w = weights[tile // each * 3 : tile // each * 3 + 2]
        queue.append(pltpu.make_async_copy(gate_w.at[:, part], gates.at[tile], sems.at[tile, 0]))
        queue.append(pltpu.make_async_copy(up_w.at[:, part], ups.at[tile], sems.at[tile, 1]))
    for half, down in enumerate(weights[2::3]):
        queue.append(pltpu.make_async_copy(down, downs.at[half], sems.at[half, 2]))
    ahead = iter(queue[4:])
    for copy in queue[:4]:
        copy.start()

    def arrived(copy):
        copy.wait()
        for following in ahead:
            following.start()
            break

    for k, source in enumerate(marked):
        rows[k * cap : (k + 1) * cap] = source[...]
    for tile in range(tiles):
        arrived(queue[2 * tile])
        gate = jnp.dot(rows[...], gates[tile], preferred_element_type=jnp.float32)
        arrived(queue[2 * tile + 1])
        up = jnp.dot(rows[...], ups[tile], preferred_element_type=jnp.float32)
        hidden[:, tile * size : (tile + 1) * size] = (gate / (1.0 + jnp.exp(-gate)) * up).astype(jnp.bfloat16)
    arrived(queue[-2])
    arrived(queue[-1])
    step = 512 if width % 512 == 0 else width
    for start in range(0, width, step):
        cut = slice(start, start + step)
        out = jnp.dot(hidden[:, : each * size], downs[0, :, cut], preferred_element_type=jnp.float32)
        out += jnp.dot(hidden[:, each * size :], downs[1, :, cut], preferred_element_type=jnp.float32)
        for k, result in enumerate(outs):
            result[:, cut] = out[k * cap : (k + 1) * cap].astype(jnp.bfloat16)


def spread_kernel(own_map, other_map, scales, own_out, other_out, *refs):
    result = refs[-1]
    total = jnp.dot(own_map[...], own_out[...], preferred_element_type=jnp.float32) * scales[:, :1]
    total += jnp.dot(other_map[...], other_out[...], preferred_element_type=jnp.float32) * scales[:, 1:2]
    for extra in refs[:-1]:
        total += extra[...].astype(jnp.float32)
    result[...] = total.astype(jnp.bfloat16)


def sum_kernel(*refs):
    total = refs[0][...].astype(jnp.float32)
    for extra in refs[1:-1]:
        total += extra[...].astype(jnp.float32)
    refs[-1][...] = total.astype(jnp.bfloat16)


def join_kernel(first, whole, part, result):
    cut = slice(first, first + part.shape[1])
    result[...] = (whole[:, cut].astype(jnp.float32) + part[...].astype(jnp.float32)).astype(jnp.bfloat16)


def parts_kernel(count, *refs):
    spread_kernel(*refs[:-count])
    first = 0
    for part in refs[-count:]:
        part[...] = refs[-count - 1][:, first : first + part.shape[1]]
        first += part.shape[1]


def columns_kernel(first, *refs):
    *whole, part, result = refs
    total = part[...].astype(jnp.float32)
    for extra in whole:
        total += extra[:, first : first + part.shape[1]].astype(jnp.float32)
    result[...] = total.astype(jnp.bfloat16)


def finish_kernel(total, *refs):
    result, first = refs[-1], 0
    for part in refs[:-1]:
        cut = slice(first, first + part.shape[1])
        result[:, cut] = (total[:, cut].astype(jnp.float32) + part[...].astype(jnp.float32)).astype(jnp.bfloat16)
        first += part.shape[1]


def on_device(tokens, routes, route_scale, w_gate, w_up, w_down):
    count, width = tokens.shape
    experts = lax.axis_size("node")
    places = experts // 2
    hidden = w_gate.shape[2]
    size = min(hidden, 256)
    cap = -(-(5 * count // experts) // 16) * 16
    wide = width + -(-3 * experts // 128) * 128
    hbm = functools.partial(pltpu.HBM, dtype=jnp.bfloat16)
    in_hbm = functools.partial(pltpu.with_memory_space_constraint, memory_space=pltpu.HBM)
    bf16 = functools.partial(jax.ShapeDtypeStruct, dtype=jnp.bfloat16)

    own = (w_gate[0], w_up[0], w_down[0])
    (block,) = call(
        functools.partial(mark_kernel, experts),
        [bf16((count, wide))],
        [*map(in_hbm, (tokens, routes.T, route_scale.T))],
        (),
        [
            pltpu.VMEM(routes.shape[::-1], routes.dtype),
            pltpu.VMEM(routes.shape[::-1], route_scale.dtype),
            pltpu.SemaphoreType.DMA((3,)),
        ],
        [ANYWHERE] * 3,
    )
    swap = functools.partial(lax.ppermute, axis_name="local", perm=[(0, 1), (1, 0)])
    weights = [*map(in_hbm, own), *map(swap, own)]

    def along(block, pairs):
        moves = [(2 * a + y, 2 * b + y) for a, b in pairs for y in range(2)]
        return lax.ppermute(block, "node", moves)

    def across(block):
        return lax.ppermute(block, "node", [(n, n ^ 1) for n in range(experts)])

    def pick(blocks, users, after=(), cost=0):
        rows = hbm if len(blocks) == 1 else bf16
        factors = jax.ShapeDtypeStruct((count, 128), jnp.float32)
        return call(
            functools.partial(pick_kernel, users),
            [bf16((count, cap)), bf16((count, cap)), factors, rows((cap, width)), rows((cap, width))],
            blocks,
            after,
            [pltpu.VMEM((count, wide), jnp.bfloat16), pltpu.SemaphoreType.DMA],
            [ANYWHERE] * len(blocks),
            cost=cost,
        )

    def expert(rows, after=(), cost=0):
        tiles = 2 * hidden // size
        return call(
            functools.partial(expert_kernel, len(rows)),
            [bf16((cap, width))] * len(rows),
            [*rows, *weights],
            after,
            [
                pltpu.VMEM((len(rows) * cap, width), jnp.bfloat16),
                pltpu.VMEM((len(rows) * cap, 2 * hidden), jnp.bfloat16),
                pltpu.VMEM((tiles, width, size), jnp.bfloat16),
                pltpu.VMEM((tiles, width, size), jnp.bfloat16),
                pltpu.VMEM((2, hidden, width), jnp.bfloat16),
                pltpu.SemaphoreType.DMA((tiles, 3)),
            ],
            [IN_VMEM] * len(rows) + [ANYWHERE] * 6,
            32,
            cost=cost,
        )

    def spread(maps, own_out, other_out, extras=(), after=(), cost=0):
        ins = [*maps, own_out, other_out, *extras]
        return call(spread_kernel, [bf16((count, width))], ins, after, cost=cost)[0]

    plan = arrivals(places)
    held = {}

    last = []

    def ordered(function, *args, after=(), **options):
        out = function(*args, after=(*last, *after), **options)
        last[:] = [out[0] if isinstance(out, (list, tuple)) else out]
        return out

    picks, outs, returned = {}, {}, []

    def relay(step):
        for way in (1, -1):
            pairs = [
                (a, a + way)
                for a in range(places)
                if 0 <= a + way < places and 0 <= a - way * (step - 1) < places
            ]
            held[way, step] = along(held.get((way, step - 1), block), pairs)

    def do_pick(slot, after=(), cost=0):
        if slot == 0:
            *maps, own_rows, other_rows = ordered(pick, [block], [range(places)], after=after)
            picks[0] = maps, own_rows, across(other_rows)
            return
        keys = sorted({row[slot - 1] for row in plan})
        blocks = [held[key] for key in keys]
        users = [[place for place, row in enumerate(plan) if row[slot - 1] == key] for key in keys]
        *maps, own_rows, other_rows = ordered(pick, blocks, users, after=after, cost=cost)
        picks[slot] = maps, own_rows, across(other_rows)

    def do_expert(slot, after=(), cost=0):
        own_out, other_out = ordered(expert, picks[slot][1:], after=after, cost=cost)
        outs[slot] = own_out, across(other_out)

    def origin(place, slot):
        way, step = plan[place][slot - 1]
        return place - way * step

    final = places - 1
    hops = [
        (a, b)
        for a, b in ((0, 1), (places - 1, places - 2))
        if origin(a, final) == origin(b, final) and origin(b, final) not in (a, b)
    ]
    staying = {place for hop in hops for place in hop}
    kept, pieces_of_last = {}, []
    edges = [-(-(width // 128) * k // 3) * 128 for k in range(4)]
    sizes = [b - a for a, b in zip(edges, edges[1:])]

    def spread_parts(maps, own_out, other_out, after=()):
        outs = [bf16((count, width)), *(bf16((count, size)) for size in sizes)]
        return call(functools.partial(parts_kernel, len(sizes)), outs, [*maps, own_out, other_out], after)

    def do_spread(slot, after=(), cost=0):
        if slot == places - 1:
            done, *pieces_of_last[:] = ordered(spread_parts, picks[slot][0], *outs[slot], after=after)
        else:
            done = ordered(spread, picks[slot][0], *outs[slot], after=after, cost=cost)
        kept[slot] = done
        home = [(a, origin(a, slot)) for a in range(places) if slot < final or a not in staying]
        rounds = []
        while home:
            now = list({b: (a, b) for a, b in home}.values())
            home = [pair for pair in home if pair not in now]
            rounds.append(along(done, now))
        returned.append(rounds)

    def call_sum(blocks, after=(), cost=0):
        return call(sum_kernel, [bf16((count, width))], blocks, after, cost=cost)

    def join(whole, part, first, after=()):
        return call(functools.partial(join_kernel, first), [bf16(part.shape)], [whole, part], after)[0]

    def columns(whole, part, first, after=(), cost=0):
        kernel = functools.partial(columns_kernel, first)
        return call(kernel, [bf16(part.shape)], [*whole, part], after, cost=cost)[0]

    def finish(whole, parts, total):
        while len(whole) > 8:
            merged = sum(array.astype(jnp.float32) for array in whole[:8])
            whole = [merged.astype(jnp.bfloat16), *whole[8:]]
        done = [ordered(columns, whole, part, first, cost=128 * MIB) for part, first in zip(parts[:-1], edges)]
        if whole:
            parts[-1] = ordered(columns, whole, parts[-1], edges[len(parts) - 1])
        return call(finish_kernel, [bf16((count, width))], [total, *done, parts[-1]])[0]

    relay(1)
    relay(2)
    do_pick(1, after=weights[3:4])
    do_pick(0)
    do_expert(1, cost=64 * MIB)
    held[1, 2], held[-1, 2] = call(
        passing_kernel, [bf16((count, wide))] * 2, [held[1, 2], held[-1, 2]], [*last, picks[1][2]]
    )
    for step in range(3, places):
        relay(step)
    do_pick(2, after=[picks[0][2]])
    do_expert(0)
    do_spread(1, cost=64 * MIB)
    do_pick(3)
    do_expert(2)
    for slot in range(3, places):
        do_expert(slot)
        do_spread(slot - 1, after=returned[slot - 3])
        if slot + 1 < places:
            do_pick(slot + 1)
    do_spread(places - 1)
    near = returned.pop(places - 3)
    (summed,) = ordered(call_sum, [*returned.pop(0), *near] if places > 3 else near, cost=128 * MIB)
    homes = [(q, origin(q, final)) for _, q in hops]
    parts = []
    for arrived, first in zip([along(part, hops) for part in pieces_of_last], edges):
        parts.append(along(ordered(join, kept[final], arrived, first), homes))
        if first == 0:
            total = ordered(spread, picks[0][0], *outs[0], [summed])
    return finish(sum(returned, []), parts, total)


def solution(mesh):
    placed = (
        P(("groups", "node", "local"), None),
        P(("groups", "node", "local"), None),
        P(("groups", "node", "local"), None),
        P("node", None, "local"),
        P("node", None, "local"),
        P("node", "local", None),
    )
    return jax.shard_map(
        on_device,
        mesh=mesh,
        in_specs=placed,
        out_specs=P(("groups", "node", "local"), None),
        check_vma=False,
    )
```

```python
import functools

import jax
import jax.numpy as jnp
from jax import lax
from jax.experimental import pallas as pl
from jax.experimental.pallas import tpu as pltpu
from jax.sharding import PartitionSpec as P

ANYWHERE = pl.BlockSpec(memory_space=pl.ANY)
IN_VMEM = pl.BlockSpec(memory_space=pltpu.VMEM)
MIB = 1024 * 1024


def arrivals(places):
    plan = []
    for place in range(places):
        ways = (-1, 1) if place < places // 2 else (1, -1)
        steps = [(way, step) for step in range(1, places) for way in ways]
        plan.append([(way, step) for way, step in steps if 0 <= place - way * step < places])
    return plan


def call(kernel, outs, ins, after=(), scratch=(), specs=None, vmem=16, out_specs=None, cost=0):
    body = kernel
    if after:
        first, last = len(ins), len(ins) + len(after)

        def body(*refs):
            kernel(*refs[:first], *refs[last:])

    specs = list(specs or [IN_VMEM] * len(ins)) + [ANYWHERE] * len(after)
    return pl.pallas_call(
        body,
        out_shape=outs,
        in_specs=specs,
        out_specs=out_specs or [IN_VMEM] * len(outs),
        scratch_shapes=scratch,
        compiler_params=pltpu.CompilerParams(vmem_limit_bytes=vmem * MIB),
        cost_estimate=pl.CostEstimate(flops=0, bytes_accessed=cost, transcendentals=0),
    )(*ins, *after)


def in_vmem(array):
    return pltpu.with_memory_space_constraint(array, pltpu.VMEM)


def tied(arrays, after):
    return pl.pallas_call(
        lambda *refs: None,
        out_shape=[jax.ShapeDtypeStruct(a.shape, a.dtype) for a in arrays],
        in_specs=[ANYWHERE] * (len(arrays) + len(after)),
        out_specs=[ANYWHERE] * len(arrays),
        input_output_aliases={k: k for k in range(len(arrays))},
        cost_estimate=pl.CostEstimate(flops=0, bytes_accessed=0, transcendentals=0),
    )(*[in_vmem(a) for a in arrays], *after)


def mark_kernel(experts, tokens, routes, scale, block, route_held, scale_held, sems):
    count, width = tokens.shape
    ins = [
        pltpu.make_async_copy(routes, route_held, sems.at[0]),
        pltpu.make_async_copy(scale, scale_held, sems.at[1]),
        pltpu.make_async_copy(tokens, block.at[:, :width], sems.at[2]),
    ]
    for copy in ins:
        copy.start()
    for copy in ins[:2]:
        copy.wait()
    lane = lax.broadcasted_iota(jnp.int32, (count, block.shape[1] - width), 1)
    expert, part = lax.rem(lane, experts), lax.div(lane, experts)
    weight = jnp.zeros(lane.shape, jnp.float32)
    routes, scale = route_held[...].T, scale_held[...].T
    for r in range(routes.shape[1]):
        weight += jnp.where(routes[:, r : r + 1] == expert, scale[:, r : r + 1], 0.0)
    high = weight.astype(jnp.bfloat16).astype(jnp.float32)
    middle = (weight - high).astype(jnp.bfloat16).astype(jnp.float32)
    low = weight - high - middle
    marks = jnp.where(part == 0, high, jnp.where(part == 1, middle, jnp.where(part == 2, low, 0.0)))
    block[:, width:] = marks.astype(jnp.bfloat16)
    ins[2].wait()


def passing_kernel(*refs):
    for source, result in zip(refs, refs[len(refs) // 2 :]):
        result[...] = source[...]


def choose(held, own_map, other_map, scales, own_rows, other_rows):
    node = lax.axis_index("node")
    count, cap = own_map.shape
    marks = held[:, held.shape[1] - 128 :].astype(jnp.float32)
    lane = lax.broadcasted_iota(jnp.int32, marks.shape, 1)
    earlier = lax.broadcasted_iota(jnp.int32, (count, count), 0) > lax.broadcasted_iota(jnp.int32, (count, count), 1)
    named = jnp.where(marks != 0, 1.0, 0.0)
    rank = jnp.dot(
        jnp.where(earlier, 1.0, 0.0).astype(jnp.bfloat16), named.astype(jnp.bfloat16), preferred_element_type=jnp.float32
    )
    place = jnp.where(named > 0, rank, -1.0)
    slot = lax.broadcasted_iota(jnp.int32, (count, cap), 1)
    scales[...] = jnp.zeros(scales.shape, jnp.float32)
    width, experts = own_rows.shape[1], lax.axis_size("node")
    for k, (expert, one_hot, rows) in enumerate(((node, own_map, own_rows), (node ^ 1, other_map, other_rows))):
        parts = (lax.rem(lane, experts) == expert) & (lane < 3 * experts)
        scales[:, k : k + 1] = jnp.sum(jnp.where(parts, marks, 0.0), axis=1, keepdims=True)
        mine = jnp.sum(jnp.where(lane == expert, place, 0.0), axis=1, keepdims=True).astype(jnp.int32)
        chosen = jnp.where(mine == slot, 1.0, 0.0).astype(jnp.bfloat16)
        one_hot[...] = chosen
        rows[...] = lax.dot_general(
            chosen, held[:, :width], (((0,), (0,)), ((), ())), preferred_element_type=jnp.float32
        ).astype(jnp.bfloat16)


def pick_kernel(users, *refs):
    blocks, (held, sem) = refs[: len(users)], refs[len(users) + 5 :]
    node = lax.axis_index("node")
    for block, places in zip(blocks, users):
        here = functools.reduce(jnp.logical_or, [lax.div(node, 2) == place for place in places])

        @pl.when(here)
        def _():
            copy = pltpu.make_async_copy(block, held, sem)
            copy.start()
            copy.wait()

    choose(held, *refs[len(users) : len(users) + 5])


def expert_kernel(count, *refs):
    marked, weights, outs = refs[:count], refs[count : count + 6], refs[count + 6 : 2 * count + 6]
    rows, hidden, gates, ups, downs, sems = refs[2 * count + 6 :]
    cap, width = outs[0].shape
    tiles, _, size = gates.shape
    each = tiles // 2
    queue = []
    for tile in range(tiles):
        part = pl.ds(tile % each * size, size)
        gate_w, up_w = weights[tile // each * 3 : tile // each * 3 + 2]
        queue.append(pltpu.make_async_copy(gate_w.at[:, part], gates.at[tile], sems.at[tile, 0]))
        queue.append(pltpu.make_async_copy(up_w.at[:, part], ups.at[tile], sems.at[tile, 1]))
    for half, down in enumerate(weights[2::3]):
        queue.append(pltpu.make_async_copy(down, downs.at[half], sems.at[half, 2]))
    ahead = iter(queue[4:])
    for copy in queue[:4]:
        copy.start()

    def arrived(copy):
        copy.wait()
        for following in ahead:
            following.start()
            break

    for k, source in enumerate(marked):
        rows[k * cap : (k + 1) * cap] = source[...]
    for tile in range(tiles):
        arrived(queue[2 * tile])
        gate = jnp.dot(rows[...], gates[tile], preferred_element_type=jnp.float32)
        arrived(queue[2 * tile + 1])
        up = jnp.dot(rows[...], ups[tile], preferred_element_type=jnp.float32)
        hidden[:, tile * size : (tile + 1) * size] = (gate / (1.0 + jnp.exp(-gate)) * up).astype(jnp.bfloat16)
    arrived(queue[-2])
    arrived(queue[-1])
    step = 512 if width % 512 == 0 else width
    for start in range(0, width, step):
        cut = slice(start, start + step)
        out = jnp.dot(hidden[:, : each * size], downs[0, :, cut], preferred_element_type=jnp.float32)
        out += jnp.dot(hidden[:, each * size :], downs[1, :, cut], preferred_element_type=jnp.float32)
        for k, result in enumerate(outs):
            result[:, cut] = out[k * cap : (k + 1) * cap].astype(jnp.bfloat16)


def spread_kernel(own_map, other_map, scales, own_out, other_out, *refs):
    result = refs[-1]
    total = jnp.dot(own_map[...], own_out[...], preferred_element_type=jnp.float32) * scales[:, :1]
    total += jnp.dot(other_map[...], other_out[...], preferred_element_type=jnp.float32) * scales[:, 1:2]
    for extra in refs[:-1]:
        total += extra[...].astype(jnp.float32)
    result[...] = total.astype(jnp.bfloat16)


def sum_kernel(*refs):
    total = refs[0][...].astype(jnp.float32)
    for extra in refs[1:-1]:
        total += extra[...].astype(jnp.float32)
    refs[-1][...] = total.astype(jnp.bfloat16)


def join_kernel(first, whole, part, result):
    cut = slice(first, first + part.shape[1])
    result[...] = (whole[:, cut].astype(jnp.float32) + part[...].astype(jnp.float32)).astype(jnp.bfloat16)


def parts_kernel(count, *refs):
    spread_kernel(*refs[:-count])
    first = 0
    for part in refs[-count:]:
        part[...] = refs[-count - 1][:, first : first + part.shape[1]]
        first += part.shape[1]


def columns_kernel(first, *refs):
    *whole, part, result = refs
    total = part[...].astype(jnp.float32)
    for extra in whole:
        total += extra[:, first : first + part.shape[1]].astype(jnp.float32)
    result[...] = total.astype(jnp.bfloat16)


def finish_kernel(total, *refs):
    result, first = refs[-1], 0
    for part in refs[:-1]:
        cut = slice(first, first + part.shape[1])
        result[:, cut] = (total[:, cut].astype(jnp.float32) + part[...].astype(jnp.float32)).astype(jnp.bfloat16)
        first += part.shape[1]


def on_device(tokens, routes, route_scale, w_gate, w_up, w_down):
    count, width = tokens.shape
    experts = lax.axis_size("node")
    places = experts // 2
    hidden = w_gate.shape[2]
    size = min(hidden, 256)
    cap = -(-(5 * count // experts) // 16) * 16
    wide = width + -(-3 * experts // 128) * 128
    hbm = functools.partial(pltpu.HBM, dtype=jnp.bfloat16)
    in_hbm = functools.partial(pltpu.with_memory_space_constraint, memory_space=pltpu.HBM)
    bf16 = functools.partial(jax.ShapeDtypeStruct, dtype=jnp.bfloat16)

    own = (w_gate[0], w_up[0], w_down[0])
    (block,) = call(
        functools.partial(mark_kernel, experts),
        [bf16((count, wide))],
        [*map(in_hbm, (tokens, routes.T, route_scale.T))],
        (),
        [
            pltpu.VMEM(routes.shape[::-1], routes.dtype),
            pltpu.VMEM(routes.shape[::-1], route_scale.dtype),
            pltpu.SemaphoreType.DMA((3,)),
        ],
        [ANYWHERE] * 3,
    )
    swap = functools.partial(lax.ppermute, axis_name="local", perm=[(0, 1), (1, 0)])
    weights = [*map(in_hbm, own), *map(swap, own)]

    def along(block, pairs):
        moves = [(2 * a + y, 2 * b + y) for a, b in pairs for y in range(2)]
        return lax.ppermute(block, "node", moves)

    def across(block):
        return lax.ppermute(block, "node", [(n, n ^ 1) for n in range(experts)])

    def pick(blocks, users, after=(), cost=0):
        rows = hbm if len(blocks) == 1 else bf16
        factors = jax.ShapeDtypeStruct((count, 128), jnp.float32)
        return call(
            functools.partial(pick_kernel, users),
            [bf16((count, cap)), bf16((count, cap)), factors, rows((cap, width)), rows((cap, width))],
            blocks,
            after,
            [pltpu.VMEM((count, wide), jnp.bfloat16), pltpu.SemaphoreType.DMA],
            [ANYWHERE] * len(blocks),
            cost=cost,
        )

    def expert(rows, after=(), cost=0):
        tiles = 2 * hidden // size
        return call(
            functools.partial(expert_kernel, len(rows)),
            [bf16((cap, width))] * len(rows),
            [*rows, *weights],
            after,
            [
                pltpu.VMEM((len(rows) * cap, width), jnp.bfloat16),
                pltpu.VMEM((len(rows) * cap, 2 * hidden), jnp.bfloat16),
                pltpu.VMEM((tiles, width, size), jnp.bfloat16),
                pltpu.VMEM((tiles, width, size), jnp.bfloat16),
                pltpu.VMEM((2, hidden, width), jnp.bfloat16),
                pltpu.SemaphoreType.DMA((tiles, 3)),
            ],
            [IN_VMEM] * len(rows) + [ANYWHERE] * 6,
            32,
            cost=cost,
        )

    def spread(maps, own_out, other_out, extras=(), after=(), cost=0):
        ins = [*maps, own_out, other_out, *extras]
        return call(spread_kernel, [bf16((count, width))], ins, after, cost=cost)[0]

    plan = arrivals(places)
    held = {}

    last = []

    def ordered(function, *args, after=(), **options):
        out = function(*args, after=(*last, *after), **options)
        last[:] = [out[0] if isinstance(out, (list, tuple)) else out]
        return out

    picks, outs, returned = {}, {}, []

    def relay(step):
        for way in (1, -1):
            pairs = [
                (a, a + way)
                for a in range(places)
                if 0 <= a + way < places and 0 <= a - way * (step - 1) < places
            ]
            held[way, step] = along(held.get((way, step - 1), block), pairs)

    def do_pick(slot, after=(), cost=0):
        if slot == 0:
            *maps, own_rows, other_rows = ordered(pick, [block], [range(places)], after=after)
            picks[0] = maps, own_rows, across(other_rows)
            return
        keys = sorted({row[slot - 1] for row in plan})
        blocks = [held[key] for key in keys]
        users = [[place for place, row in enumerate(plan) if row[slot - 1] == key] for key in keys]
        *maps, own_rows, other_rows = ordered(pick, blocks, users, after=after, cost=cost)
        picks[slot] = maps, own_rows, across(other_rows)

    def do_expert(slot, after=(), cost=0):
        own_out, other_out = ordered(expert, picks[slot][1:], after=after, cost=cost)
        outs[slot] = own_out, across(other_out)

    def origin(place, slot):
        way, step = plan[place][slot - 1]
        return place - way * step

    final = places - 1
    hops = [
        (a, b)
        for a, b in ((0, 1), (places - 1, places - 2))
        if origin(a, final) == origin(b, final) and origin(b, final) not in (a, b)
    ]
    staying = {place for hop in hops for place in hop}
    kept, pieces_of_last = {}, []
    edges = [-(-(width // 128) * k // 4) * 128 for k in range(5)]
    sizes = [b - a for a, b in zip(edges, edges[1:])]

    def spread_parts(maps, own_out, other_out, after=()):
        outs = [bf16((count, width)), *(bf16((count, size)) for size in sizes)]
        return call(functools.partial(parts_kernel, len(sizes)), outs, [*maps, own_out, other_out], after)

    def do_spread(slot, after=(), cost=0):
        if slot == places - 1:
            done, *pieces_of_last[:] = ordered(spread_parts, picks[slot][0], *outs[slot], after=after)
        else:
            done = ordered(spread, picks[slot][0], *outs[slot], after=after, cost=cost)
        kept[slot] = done
        home = [(a, origin(a, slot)) for a in range(places) if slot < final or a not in staying]
        rounds = []
        while home:
            now = list({b: (a, b) for a, b in home}.values())
            home = [pair for pair in home if pair not in now]
            rounds.append(along(done, now))
        returned.append(rounds)

    def call_sum(blocks, after=(), cost=0):
        return call(sum_kernel, [bf16((count, width))], blocks, after, cost=cost)

    def join(whole, part, first, after=()):
        return call(functools.partial(join_kernel, first), [bf16(part.shape)], [whole, part], after)[0]

    def columns(whole, part, first, after=(), cost=0):
        kernel = functools.partial(columns_kernel, first)
        return call(kernel, [bf16(part.shape)], [*whole, part], after, cost=cost)[0]

    def finish(whole, parts, total):
        while len(whole) > 8:
            merged = sum(array.astype(jnp.float32) for array in whole[:8])
            whole = [merged.astype(jnp.bfloat16), *whole[8:]]
        done = [ordered(columns, whole, part, first, cost=128 * MIB) for part, first in zip(parts[:-1], edges)]
        if whole:
            parts[-1] = ordered(columns, whole, parts[-1], edges[len(parts) - 1])
        return call(finish_kernel, [bf16((count, width))], [total, *done, parts[-1]])[0]

    relay(1)
    relay(2)
    do_pick(1, after=weights[3:4])
    do_pick(0)
    do_expert(1, cost=64 * MIB)
    held[1, 2], held[-1, 2] = call(
        passing_kernel, [bf16((count, wide))] * 2, [held[1, 2], held[-1, 2]], [*last, picks[1][2]]
    )
    for step in range(3, places):
        relay(step)
    do_pick(2, after=[picks[0][2]])
    do_expert(0)
    do_spread(1, cost=64 * MIB)
    do_pick(3)
    do_expert(2)
    for slot in range(3, places):
        do_expert(slot)
        do_spread(slot - 1, after=returned[slot - 3])
        if slot + 1 < places:
            do_pick(slot + 1)
    do_spread(places - 1)
    near = returned.pop(places - 3)
    (summed,) = ordered(call_sum, [*returned.pop(0), *near] if places > 3 else near, cost=128 * MIB)
    homes = [(q, origin(q, final)) for _, q in hops]
    parts = []
    for arrived, first in zip([along(part, hops) for part in pieces_of_last], edges):
        parts.append(along(ordered(join, kept[final], arrived, first), homes))
        if first == 0:
            total = ordered(spread, picks[0][0], *outs[0], [summed])
    return finish(sum(returned, []), parts, total)


def solution(mesh):
    placed = (
        P(("groups", "node", "local"), None),
        P(("groups", "node", "local"), None),
        P(("groups", "node", "local"), None),
        P("node", None, "local"),
        P("node", None, "local"),
        P("node", "local", None),
    )
    return jax.shard_map(
        on_device,
        mesh=mesh,
        in_specs=placed,
        out_specs=P(("groups", "node", "local"), None),
        check_vma=False,
    )
```

```python
import functools

import jax
import jax.numpy as jnp
from jax import lax
from jax.experimental import pallas as pl
from jax.experimental.pallas import tpu as pltpu
from jax.sharding import PartitionSpec as P

ANYWHERE = pl.BlockSpec(memory_space=pl.ANY)
IN_VMEM = pl.BlockSpec(memory_space=pltpu.VMEM)
MIB = 1024 * 1024


def arrivals(places):
    plan = []
    for place in range(places):
        ways = (-1, 1) if place < places // 2 else (1, -1)
        steps = [(way, step) for step in range(1, places) for way in ways]
        plan.append([(way, step) for way, step in steps if 0 <= place - way * step < places])
    return plan


def call(kernel, outs, ins, after=(), scratch=(), specs=None, vmem=16, out_specs=None, cost=0):
    body = kernel
    if after:
        first, last = len(ins), len(ins) + len(after)

        def body(*refs):
            kernel(*refs[:first], *refs[last:])

    specs = list(specs or [IN_VMEM] * len(ins)) + [ANYWHERE] * len(after)
    return pl.pallas_call(
        body,
        out_shape=outs,
        in_specs=specs,
        out_specs=out_specs or [IN_VMEM] * len(outs),
        scratch_shapes=scratch,
        compiler_params=pltpu.CompilerParams(vmem_limit_bytes=vmem * MIB),
        cost_estimate=pl.CostEstimate(flops=0, bytes_accessed=cost, transcendentals=0),
    )(*ins, *after)


def in_vmem(array):
    return pltpu.with_memory_space_constraint(array, pltpu.VMEM)


def tied(arrays, after):
    return pl.pallas_call(
        lambda *refs: None,
        out_shape=[jax.ShapeDtypeStruct(a.shape, a.dtype) for a in arrays],
        in_specs=[ANYWHERE] * (len(arrays) + len(after)),
        out_specs=[ANYWHERE] * len(arrays),
        input_output_aliases={k: k for k in range(len(arrays))},
        cost_estimate=pl.CostEstimate(flops=0, bytes_accessed=0, transcendentals=0),
    )(*[in_vmem(a) for a in arrays], *after)


def mark_kernel(experts, tokens, routes, scale, block, route_held, scale_held, sems):
    count, width = tokens.shape
    ins = [
        pltpu.make_async_copy(routes, route_held, sems.at[0]),
        pltpu.make_async_copy(scale, scale_held, sems.at[1]),
        pltpu.make_async_copy(tokens, block.at[:, :width], sems.at[2]),
    ]
    for copy in ins:
        copy.start()
    for copy in ins[:2]:
        copy.wait()
    lane = lax.broadcasted_iota(jnp.int32, (count, block.shape[1] - width), 1)
    expert, part = lax.rem(lane, experts), lax.div(lane, experts)
    weight = jnp.zeros(lane.shape, jnp.float32)
    routes, scale = route_held[...].T, scale_held[...].T
    for r in range(routes.shape[1]):
        weight += jnp.where(routes[:, r : r + 1] == expert, scale[:, r : r + 1], 0.0)
    high = weight.astype(jnp.bfloat16).astype(jnp.float32)
    middle = (weight - high).astype(jnp.bfloat16).astype(jnp.float32)
    low = weight - high - middle
    marks = jnp.where(part == 0, high, jnp.where(part == 1, middle, jnp.where(part == 2, low, 0.0)))
    block[:, width:] = marks.astype(jnp.bfloat16)
    ins[2].wait()


def passing_kernel(*refs):
    for source, result in zip(refs, refs[len(refs) // 2 :]):
        result[...] = source[...]


def choose(held, own_map, other_map, scales, own_rows, other_rows):
    node = lax.axis_index("node")
    count, cap = own_map.shape
    marks = held[:, held.shape[1] - 128 :].astype(jnp.float32)
    lane = lax.broadcasted_iota(jnp.int32, marks.shape, 1)
    earlier = lax.broadcasted_iota(jnp.int32, (count, count), 0) > lax.broadcasted_iota(jnp.int32, (count, count), 1)
    named = jnp.where(marks != 0, 1.0, 0.0)
    rank = jnp.dot(
        jnp.where(earlier, 1.0, 0.0).astype(jnp.bfloat16), named.astype(jnp.bfloat16), preferred_element_type=jnp.float32
    )
    place = jnp.where(named > 0, rank, -1.0)
    slot = lax.broadcasted_iota(jnp.int32, (count, cap), 1)
    scales[...] = jnp.zeros(scales.shape, jnp.float32)
    width, experts = own_rows.shape[1], lax.axis_size("node")
    for k, (expert, one_hot, rows) in enumerate(((node, own_map, own_rows), (node ^ 1, other_map, other_rows))):
        parts = (lax.rem(lane, experts) == expert) & (lane < 3 * experts)
        scales[:, k : k + 1] = jnp.sum(jnp.where(parts, marks, 0.0), axis=1, keepdims=True)
        mine = jnp.sum(jnp.where(lane == expert, place, 0.0), axis=1, keepdims=True).astype(jnp.int32)
        chosen = jnp.where(mine == slot, 1.0, 0.0).astype(jnp.bfloat16)
        one_hot[...] = chosen
        rows[...] = lax.dot_general(
            chosen, held[:, :width], (((0,), (0,)), ((), ())), preferred_element_type=jnp.float32
        ).astype(jnp.bfloat16)


def pick_kernel(users, *refs):
    blocks, (held, sem) = refs[: len(users)], refs[len(users) + 5 :]
    node = lax.axis_index("node")
    for block, places in zip(blocks, users):
        here = functools.reduce(jnp.logical_or, [lax.div(node, 2) == place for place in places])

        @pl.when(here)
        def _():
            copy = pltpu.make_async_copy(block, held, sem)
            copy.start()
            copy.wait()

    choose(held, *refs[len(users) : len(users) + 5])


def expert_kernel(count, *refs):
    marked, weights, outs = refs[:count], refs[count : count + 6], refs[count + 6 : 2 * count + 6]
    rows, hidden, gates, ups, downs, sems = refs[2 * count + 6 :]
    cap, width = outs[0].shape
    tiles, _, size = gates.shape
    each = tiles // 2
    queue = []
    for tile in range(tiles):
        part = pl.ds(tile % each * size, size)
        gate_w, up_w = weights[tile // each * 3 : tile // each * 3 + 2]
        queue.append(pltpu.make_async_copy(gate_w.at[:, part], gates.at[tile], sems.at[tile, 0]))
        queue.append(pltpu.make_async_copy(up_w.at[:, part], ups.at[tile], sems.at[tile, 1]))
    for half, down in enumerate(weights[2::3]):
        queue.append(pltpu.make_async_copy(down, downs.at[half], sems.at[half, 2]))
    ahead = iter(queue[4:])
    for copy in queue[:4]:
        copy.start()

    def arrived(copy):
        copy.wait()
        for following in ahead:
            following.start()
            break

    for k, source in enumerate(marked):
        rows[k * cap : (k + 1) * cap] = source[...]
    for tile in range(tiles):
        arrived(queue[2 * tile])
        gate = jnp.dot(rows[...], gates[tile], preferred_element_type=jnp.float32)
        arrived(queue[2 * tile + 1])
        up = jnp.dot(rows[...], ups[tile], preferred_element_type=jnp.float32)
        hidden[:, tile * size : (tile + 1) * size] = (gate / (1.0 + jnp.exp(-gate)) * up).astype(jnp.bfloat16)
    arrived(queue[-2])
    arrived(queue[-1])
    step = 512 if width % 512 == 0 else width
    for start in range(0, width, step):
        cut = slice(start, start + step)
        out = jnp.dot(hidden[:, : each * size], downs[0, :, cut], preferred_element_type=jnp.float32)
        out += jnp.dot(hidden[:, each * size :], downs[1, :, cut], preferred_element_type=jnp.float32)
        for k, result in enumerate(outs):
            result[:, cut] = out[k * cap : (k + 1) * cap].astype(jnp.bfloat16)


def spread_kernel(own_map, other_map, scales, own_out, other_out, *refs):
    result = refs[-1]
    total = jnp.dot(own_map[...], own_out[...], preferred_element_type=jnp.float32) * scales[:, :1]
    total += jnp.dot(other_map[...], other_out[...], preferred_element_type=jnp.float32) * scales[:, 1:2]
    for extra in refs[:-1]:
        total += extra[...].astype(jnp.float32)
    result[...] = total.astype(jnp.bfloat16)


def sum_kernel(*refs):
    total = refs[0][...].astype(jnp.float32)
    for extra in refs[1:-1]:
        total += extra[...].astype(jnp.float32)
    refs[-1][...] = total.astype(jnp.bfloat16)


def join_kernel(first, whole, part, result):
    cut = slice(first, first + part.shape[1])
    result[...] = (whole[:, cut].astype(jnp.float32) + part[...].astype(jnp.float32)).astype(jnp.bfloat16)


def parts_kernel(count, *refs):
    spread_kernel(*refs[:-count])
    first = 0
    for part in refs[-count:]:
        part[...] = refs[-count - 1][:, first : first + part.shape[1]]
        first += part.shape[1]


def columns_kernel(first, *refs):
    *whole, part, result = refs
    total = part[...].astype(jnp.float32)
    for extra in whole:
        total += extra[:, first : first + part.shape[1]].astype(jnp.float32)
    result[...] = total.astype(jnp.bfloat16)


def finish_kernel(total, *refs):
    result, first = refs[-1], 0
    for part in refs[:-1]:
        cut = slice(first, first + part.shape[1])
        result[:, cut] = (total[:, cut].astype(jnp.float32) + part[...].astype(jnp.float32)).astype(jnp.bfloat16)
        first += part.shape[1]


def on_device(tokens, routes, route_scale, w_gate, w_up, w_down):
    count, width = tokens.shape
    experts = lax.axis_size("node")
    places = experts // 2
    hidden = w_gate.shape[2]
    size = min(hidden, 256)
    cap = -(-(5 * count // experts) // 16) * 16
    wide = width + -(-3 * experts // 128) * 128
    hbm = functools.partial(pltpu.HBM, dtype=jnp.bfloat16)
    in_hbm = functools.partial(pltpu.with_memory_space_constraint, memory_space=pltpu.HBM)
    bf16 = functools.partial(jax.ShapeDtypeStruct, dtype=jnp.bfloat16)

    own = (w_gate[0], w_up[0], w_down[0])
    (block,) = call(
        functools.partial(mark_kernel, experts),
        [bf16((count, wide))],
        [*map(in_hbm, (tokens, routes.T, route_scale.T))],
        (),
        [
            pltpu.VMEM(routes.shape[::-1], routes.dtype),
            pltpu.VMEM(routes.shape[::-1], route_scale.dtype),
            pltpu.SemaphoreType.DMA((3,)),
        ],
        [ANYWHERE] * 3,
    )
    swap = functools.partial(lax.ppermute, axis_name="local", perm=[(0, 1), (1, 0)])
    weights = [*map(in_hbm, own), *map(swap, own)]

    def along(block, pairs):
        moves = [(2 * a + y, 2 * b + y) for a, b in pairs for y in range(2)]
        return lax.ppermute(block, "node", moves)

    def across(block):
        return lax.ppermute(block, "node", [(n, n ^ 1) for n in range(experts)])

    def pick(blocks, users, after=(), cost=0):
        rows = hbm if len(blocks) == 1 else bf16
        factors = jax.ShapeDtypeStruct((count, 128), jnp.float32)
        return call(
            functools.partial(pick_kernel, users),
            [bf16((count, cap)), bf16((count, cap)), factors, rows((cap, width)), rows((cap, width))],
            blocks,
            after,
            [pltpu.VMEM((count, wide), jnp.bfloat16), pltpu.SemaphoreType.DMA],
            [ANYWHERE] * len(blocks),
            cost=cost,
        )

    def expert(rows, after=(), cost=0):
        tiles = 2 * hidden // size
        return call(
            functools.partial(expert_kernel, len(rows)),
            [bf16((cap, width))] * len(rows),
            [*rows, *weights],
            after,
            [
                pltpu.VMEM((len(rows) * cap, width), jnp.bfloat16),
                pltpu.VMEM((len(rows) * cap, 2 * hidden), jnp.bfloat16),
                pltpu.VMEM((tiles, width, size), jnp.bfloat16),
                pltpu.VMEM((tiles, width, size), jnp.bfloat16),
                pltpu.VMEM((2, hidden, width), jnp.bfloat16),
                pltpu.SemaphoreType.DMA((tiles, 3)),
            ],
            [IN_VMEM] * len(rows) + [ANYWHERE] * 6,
            32,
            cost=cost,
        )

    def spread(maps, own_out, other_out, extras=(), after=(), cost=0):
        ins = [*maps, own_out, other_out, *extras]
        return call(spread_kernel, [bf16((count, width))], ins, after, cost=cost)[0]

    plan = arrivals(places)
    held = {}

    last = []

    def ordered(function, *args, after=(), **options):
        out = function(*args, after=(*last, *after), **options)
        last[:] = [out[0] if isinstance(out, (list, tuple)) else out]
        return out

    picks, outs, returned = {}, {}, []

    def relay(step):
        for way in (1, -1):
            pairs = [
                (a, a + way)
                for a in range(places)
                if 0 <= a + way < places and 0 <= a - way * (step - 1) < places
            ]
            held[way, step] = along(held.get((way, step - 1), block), pairs)

    def do_pick(slot, after=(), cost=0):
        if slot == 0:
            *maps, own_rows, other_rows = ordered(pick, [block], [range(places)], after=after)
            picks[0] = maps, own_rows, across(other_rows)
            return
        keys = sorted({row[slot - 1] for row in plan})
        blocks = [held[key] for key in keys]
        users = [[place for place, row in enumerate(plan) if row[slot - 1] == key] for key in keys]
        *maps, own_rows, other_rows = ordered(pick, blocks, users, after=after, cost=cost)
        picks[slot] = maps, own_rows, across(other_rows)

    def do_expert(slot, after=(), cost=0):
        own_out, other_out = ordered(expert, picks[slot][1:], after=after, cost=cost)
        outs[slot] = own_out, across(other_out)

    def origin(place, slot):
        way, step = plan[place][slot - 1]
        return place - way * step

    final = places - 1
    hops = [
        (a, b)
        for a, b in ((0, 1), (places - 1, places - 2))
        if origin(a, final) == origin(b, final) and origin(b, final) not in (a, b)
    ]
    staying = {place for hop in hops for place in hop}
    kept, pieces_of_last = {}, []
    edges = [-(-(width // 128) * k // 5) * 128 for k in range(6)]
    sizes = [b - a for a, b in zip(edges, edges[1:])]

    def spread_parts(maps, own_out, other_out, after=()):
        outs = [bf16((count, width)), *(bf16((count, size)) for size in sizes)]
        return call(functools.partial(parts_kernel, len(sizes)), outs, [*maps, own_out, other_out], after)

    def do_spread(slot, after=(), cost=0):
        if slot == places - 1:
            done, *pieces_of_last[:] = ordered(spread_parts, picks[slot][0], *outs[slot], after=after)
        else:
            done = ordered(spread, picks[slot][0], *outs[slot], after=after, cost=cost)
        kept[slot] = done
        home = [(a, origin(a, slot)) for a in range(places) if slot < final or a not in staying]
        rounds = []
        while home:
            now = list({b: (a, b) for a, b in home}.values())
            home = [pair for pair in home if pair not in now]
            rounds.append(along(done, now))
        returned.append(rounds)

    def call_sum(blocks, after=(), cost=0):
        return call(sum_kernel, [bf16((count, width))], blocks, after, cost=cost)

    def join(whole, part, first, after=()):
        return call(functools.partial(join_kernel, first), [bf16(part.shape)], [whole, part], after)[0]

    def columns(whole, part, first, after=(), cost=0):
        kernel = functools.partial(columns_kernel, first)
        return call(kernel, [bf16(part.shape)], [*whole, part], after, cost=cost)[0]

    def finish(whole, parts, total):
        while len(whole) > 8:
            merged = sum(array.astype(jnp.float32) for array in whole[:8])
            whole = [merged.astype(jnp.bfloat16), *whole[8:]]
        done = [ordered(columns, whole, part, first, cost=128 * MIB) for part, first in zip(parts[:-1], edges)]
        if whole:
            parts[-1] = ordered(columns, whole, parts[-1], edges[len(parts) - 1])
        return call(finish_kernel, [bf16((count, width))], [total, *done, parts[-1]])[0]

    relay(1)
    relay(2)
    do_pick(1, after=weights[3:4])
    do_pick(0)
    do_expert(1, cost=64 * MIB)
    held[1, 2], held[-1, 2] = call(
        passing_kernel, [bf16((count, wide))] * 2, [held[1, 2], held[-1, 2]], [*last, picks[1][2]]
    )
    for step in range(3, places):
        relay(step)
    do_pick(2, after=[picks[0][2]])
    do_expert(0)
    do_spread(1, cost=64 * MIB)
    do_pick(3)
    do_expert(2)
    for slot in range(3, places):
        do_expert(slot)
        do_spread(slot - 1, after=returned[slot - 3])
        if slot + 1 < places:
            do_pick(slot + 1)
    do_spread(places - 1)
    near = returned.pop(places - 3)
    (summed,) = ordered(call_sum, [*returned.pop(0), *near] if places > 3 else near, cost=128 * MIB)
    homes = [(q, origin(q, final)) for _, q in hops]
    parts = []
    for arrived, first in zip([along(part, hops) for part in pieces_of_last], edges):
        parts.append(along(ordered(join, kept[final], arrived, first), homes))
        if first == 0:
            total = ordered(spread, picks[0][0], *outs[0], [summed])
    return finish(sum(returned, []), parts, total)


def solution(mesh):
    placed = (
        P(("groups", "node", "local"), None),
        P(("groups", "node", "local"), None),
        P(("groups", "node", "local"), None),
        P("node", None, "local"),
        P("node", None, "local"),
        P("node", "local", None),
    )
    return jax.shard_map(
        on_device,
        mesh=mesh,
        in_specs=placed,
        out_specs=P(("groups", "node", "local"), None),
        check_vma=False,
    )
```
